32 devices in a mesh: dp: 16 (over z, y, core), tensor: 2 (over x).
Axes of the slice: x: 2, y: 2, z: 4, core: 2. Of those that a mesh axis runs over, the one named last changes fastest.
Arguments:
- tokens: bfloat16 [8192, 2048], P('dp'), may hold values from -6 to 6
- cotangent: bfloat16 [8192, 2048], P('dp'), may hold values from -6 to 6
- segment_ids: int32 [8192], P('dp'), may hold values from 0 to 47, as said below
- counts: int32 [16], P('dp'), may hold values from 256 to 512, as said below
- mixer_gain: bfloat16 [2048], P(('dp', 'tensor')), may hold values from 0.5 to 1.5
- query_proj: bfloat16 [2048, 1024], P('dp', 'tensor'), may hold values from -0.125 to 0.125
- key_value_matrix: bfloat16 [2048, 2, 256], P('dp', None, 'tensor'), may hold values from -0.125 to 0.125
- attend_proj: bfloat16 [1024, 2048], P('tensor', 'dp'), may hold values from -1 to 1
- inner_proj: bfloat16 [2048, 2, 3072], P('dp', None, 'tensor'), may hold values from -0.125 to 0.125
- state_proj: bfloat16 [2048, 512], P(('dp', 'tensor')), may hold values from -0.125 to 0.125
- step_proj: bfloat16 [2048, 48], P('dp', 'tensor'), may hold values from -0.125 to 0.125
- conv_inner: bfloat16 [5, 3072], P(None, 'tensor'), may hold values from -3 to 3
- conv_state: bfloat16 [5, 512], P(None, ('dp', 'tensor')), may hold values from -3 to 3
- step_bias: bfloat16 [48], P('tensor'), may hold values from -5 to -1
- decay_log: bfloat16 [48], P('tensor'), may hold values from 0 to 2.5
- skip_gain: bfloat16 [48], P('tensor'), may hold values from 0.5 to 1.5
- gated_gain: bfloat16 [3072], P('tensor'), may hold values from 0.5 to 1.5
- mamba_proj: bfloat16 [3072, 2048], P('tensor', 'dp'), may hold values from -0.109375 to 0.109375
- dense_gain: bfloat16 [2048], P(('dp', 'tensor')), may hold values from 0.5 to 1.5
- gateup_proj: bfloat16 [2048, 2, 4096], P('dp', None, 'tensor'), may hold values from -0.125 to 0.125
- down_proj: bfloat16 [4096, 2048], P('tensor', 'dp'), may hold values from -0.1875 to 0.1875
Outputs:
- output: bfloat16 [8192, 2048], P('dp')
- grad_tokens: float32 [8192, 2048], P('dp')
- grad_mixer_gain: float32 [2048], P(('dp', 'tensor'))
- grad_query_proj: float32 [2048, 1024], P('dp', 'tensor')
- grad_keyval_proj: float32 [2048, 2, 256], P('dp', None, 'tensor')
- grad_attend_proj: float32 [1024, 2048], P('tensor', 'dp')
- grad_inner_proj: float32 [2048, 2, 3072], P('dp', None, 'tensor')
- grad_state_proj: float32 [2048, 512], P(('dp', 'tensor'))
- grad_step_proj: float32 [2048, 48], P('dp', 'tensor')
- grad_conv_inner: float32 [5, 3072], P(None, 'tensor')
- grad_conv_state: float32 [5, 512], P(None, ('dp', 'tensor'))
- grad_step_bias: float32 [48], P('tensor')
- grad_decay_log: float32 [48], P('tensor')
- grad_skip_gain: float32 [48], P('tensor')
- grad_gated_gain: float32 [3072], P('tensor')
- grad_mamba_proj: float32 [3072, 2048], P('tensor', 'dp')
- grad_dense_gain: float32 [2048], P(('dp', 'tensor'))
- grad_gateup_proj: float32 [2048, 2, 4096], P('dp', None, 'tensor')
- grad_down_proj: float32 [4096, 2048], P('tensor', 'dp')
The draws below stay inside these ranges and needn't reach their ends.
Inputs may be any that keep to these rules, and one draw needn't show every extreme that they name: `counts`: row slots at or past a device's count are padding. One index of dp holds exactly 512 live rows and another exactly 256. `segment_ids`: never falling along the rows. A device's rows hold at most three documents of its own, numbered from 3 times its dp index; no document crosses devices; padding rows carry the number of the device's last document.
All inputs are finite; a program needn't handle non-finite values.
Results may differ from the reference program's by a relative error of at most 0.022.
Values may be sent and summed in bfloat16 or wider, within the bound.
A program may use at most 256 MiB of HBM per device.

```python
import math
from functools import partial
import jax
import jax.numpy as jnp
from jax import lax

MODEL_DIMENSION = 2048
NH = 48
HP = 64
NS = 256
CONVK = 4
HQ = 8
KEY_VALUE_HEADS = 2
HEAD_DIMENSION = 128
FF = 4096
TOKEN_ROW_SLOTS = 512
DSSM = 3072
TOKENS = 8192
N_DP = 16


def layout(key):
    order = jax.random.permutation(jax.random.fold_in(key, 11), N_DP)
    live_rows = jax.random.randint(jax.random.fold_in(key, 12), (N_DP,), TOKEN_ROW_SLOTS // 2, TOKEN_ROW_SLOTS + 1)
    live_rows = jnp.where(order == 0, TOKEN_ROW_SLOTS, jnp.where(order == 1, TOKEN_ROW_SLOTS // 2, live_rows)).astype(jnp.int32)
    cut_rows = jax.random.randint(jax.random.fold_in(key, 13), (N_DP, 2), 1, live_rows[:, None])
    return (live_rows, cut_rows)


def draw_counts(key, part):
    live_rows, cut_rows = layout(key)
    return live_rows


def draw_segment_ids(key, part):
    live_rows, cut_rows = layout(key)
    row_index = jnp.arange(TOKEN_ROW_SLOTS, dtype=jnp.int32)[None, :]
    device_base = 3 * jnp.arange(N_DP, dtype=jnp.int32)[:, None]
    later = (row_index >= cut_rows[:, 0:1]).astype(jnp.int32) + (row_index >= cut_rows[:, 1:2]).astype(jnp.int32)
    return (device_base + later).reshape(TOKENS).astype(jnp.int32)


def steps_of(rng, shape, shards, low, largest):
    level, own = 1.0, jax.random.fold_in(rng, 6)
    for dim, blocks in shards:
        steps = jnp.exp(jax.random.uniform(jax.random.fold_in(own, dim), (blocks,), jnp.float32, low / len(shards), largest / len(shards)))
        level = level * jnp.repeat(steps, shape[dim] // blocks).reshape([-1 if axis == dim else 1 for axis in range(len(shape))])
    return level


def normal_values(rng, dims, width, reach, shards=(), held_as=jnp.bfloat16):
    factor_of = steps_of(rng, dims, shards, -0.22, 0.18) if shards else 1.0
    drawn = jax.random.normal(rng, dims, jnp.float32) * width * factor_of
    return jnp.minimum(jnp.maximum(drawn, -reach), reach).astype(held_as)


def setup_inputs(seed: int = 0) -> dict:
    key_list = jax.random.split(jax.random.key(seed), 22)
    return {
        "tokens": normal_values(key_list[0], (TOKENS, MODEL_DIMENSION), 1.0, 6.0, ((0, 16),)),
        "cotangent": normal_values(key_list[1], (TOKENS, MODEL_DIMENSION), 1.0, 6.0, ((0, 16),)),
        "segment_ids": draw_segment_ids(jax.random.fold_in(key_list[21], 71), 0),
        "counts": draw_counts(jax.random.fold_in(key_list[21], 71), 0),
        "mixer_gain": jnp.clip(1.0 + 0.1 * jax.random.normal(key_list[4], (MODEL_DIMENSION,), jnp.float32), 0.5, 1.5).astype(jnp.bfloat16),
        "query_proj": normal_values(key_list[5], (MODEL_DIMENSION, HQ * HEAD_DIMENSION), MODEL_DIMENSION ** -0.5, 0.125, ((0, 16), (1, 2))),
        "key_value_matrix": normal_values(key_list[6], (MODEL_DIMENSION, 2, KEY_VALUE_HEADS * HEAD_DIMENSION), MODEL_DIMENSION ** -0.5, 0.125, ((0, 16), (2, 2))),
        "attend_proj": normal_values(key_list[7], (HQ * HEAD_DIMENSION, MODEL_DIMENSION), (HQ * HEAD_DIMENSION // 32) ** -0.5, 1.0, ((0, 2), (1, 16))),
        "inner_proj": normal_values(key_list[8], (MODEL_DIMENSION, 2, DSSM), MODEL_DIMENSION ** -0.5, 0.125, ((0, 16), (2, 2))),
        "state_proj": normal_values(key_list[9], (MODEL_DIMENSION, 2 * NS), MODEL_DIMENSION ** -0.5, 0.125, ((0, 32),)),
        "step_proj": normal_values(key_list[10], (MODEL_DIMENSION, NH), MODEL_DIMENSION ** -0.5, 0.125, ((0, 16), (1, 2))),
        "conv_inner": normal_values(key_list[11], (CONVK + 1, DSSM), 0.5, 3.0, ((1, 2),)),
        "conv_state": normal_values(key_list[12], (CONVK + 1, 2 * NS), 0.5, 3.0, ((1, 32),)),
        "step_bias": jnp.clip(-5.0 + 4.0 * jax.random.uniform(key_list[13], (NH,), jnp.float32) ** steps_of(key_list[13], (NH,), ((0, 2),), -0.2, 0.2), -5.0, -1.0).astype(jnp.bfloat16),
        "decay_log": jnp.clip(2.5 * jax.random.uniform(key_list[14], (NH,), jnp.float32) ** steps_of(key_list[14], (NH,), ((0, 2),), -0.2, 0.2), 0.0, 2.5).astype(jnp.bfloat16),
        "skip_gain": jnp.clip(0.5 + 1.0 * jax.random.uniform(key_list[15], (NH,), jnp.float32) ** steps_of(key_list[15], (NH,), ((0, 2),), -0.2, 0.2), 0.5, 1.5).astype(jnp.bfloat16),
        "gated_gain": jnp.clip(1.0 + 0.1 * jax.random.normal(key_list[16], (DSSM,), jnp.float32), 0.5, 1.5).astype(jnp.bfloat16),
        "mamba_proj": normal_values(key_list[17], (DSSM, MODEL_DIMENSION), DSSM ** -0.5, 0.109375, ((0, 2), (1, 16))),
        "dense_gain": jnp.clip(1.0 + 0.1 * jax.random.normal(key_list[18], (MODEL_DIMENSION,), jnp.float32), 0.5, 1.5).astype(jnp.bfloat16),
        "gateup_proj": normal_values(key_list[19], (MODEL_DIMENSION, 2, FF), MODEL_DIMENSION ** -0.5, 0.125, ((0, 16), (2, 2))),
        "down_proj": normal_values(key_list[20], (FF, MODEL_DIMENSION), (FF // 4) ** -0.5, 0.1875, ((0, 2), (1, 16))),
    }


EPS = 1e-05
THETA = 100000000000.0
HIGH = lax.Precision.HIGHEST

@jax.custom_vjp
def low(v):
    return lax.optimization_barrier(v.astype(jnp.bfloat16)).astype(jnp.float32)

@jax.custom_vjp
def low_back(v):
    return v

def low_keep(v):
    return (low(v), None)

def low_pass(kept, grad):
    return (grad,)

def back_keep(v):
    return (v, None)

def back_low(kept, grad):
    return (low(grad),)
low.defvjp(low_keep, low_pass)
low_back.defvjp(back_keep, back_low)

def matrix_product(left, right):
    return jnp.dot(left, right, precision=HIGH, preferred_element_type=jnp.float32)

def rms_scale(values, gain):
    return values * lax.rsqrt(lax.optimization_barrier(jnp.mean(values * values, axis=-1, keepdims=True)) + EPS) * gain

def positions_of(segment):
    row_index = jnp.arange(segment.shape[0], dtype=jnp.int32)
    starts = jnp.concatenate([jnp.ones((1,), jnp.bool_), segment[1:] != segment[:-1]])
    first_row = lax.cummax(jnp.where(starts, row_index, 0), axis=0)
    return row_index - first_row

def rotate(values, position):
    half_width = values.shape[-1] // 2
    frequency = jnp.exp(jnp.arange(half_width, dtype=jnp.float32) * (-2.0 * math.log(THETA) / values.shape[-1]))
    angles = position.astype(jnp.float32)[:, None] * frequency[None, :]
    cos_table = jnp.cos(angles)[:, None, :]
    sin_table = jnp.sin(angles)[:, None, :]
    first_half = values[..., :half_width]
    second_half = values[..., half_width:]
    return jnp.concatenate([first_half * cos_table - second_half * sin_table, second_half * cos_table + first_half * sin_table], axis=-1)

def causal_conv(values, kernel, segment):
    tap_count = kernel.shape[0] - 1
    summed = kernel[tap_count] + kernel[tap_count - 1] * values
    for lag_step in range(1, tap_count):
        shifted = jnp.concatenate([jnp.zeros((lag_step, values.shape[1]), values.dtype), values[:-lag_step]], axis=0)
        same_doc = jnp.concatenate([jnp.zeros((lag_step,), jnp.bool_), segment[lag_step:] == segment[:-lag_step]])
        summed = summed + kernel[tap_count - 1 - lag_step] * jnp.where(same_doc[:, None], shifted, 0.0)
    return summed

def decay_matrix(log_decay, causal):
    running = jnp.cumsum(log_decay, axis=0).T
    gaps_ij = running[:, :, None] - running[:, None, :]
    return jnp.where(causal[None], jnp.exp(jnp.where(causal[None], gaps_ij, -60.0)), 0.0)

def attend(query_r, key_r, value_r, mask_qk):
    group_size = query_r.shape[1] // key_r.shape[1]
    keys_all = jnp.repeat(key_r, group_size, axis=1)
    values_all = jnp.repeat(value_r, group_size, axis=1)
    scores = low_back(jnp.einsum('ihd,jhd->hij', query_r, keys_all, precision=HIGH) * query_r.shape[-1] ** (-0.5))
    scores = jnp.where(mask_qk[None], scores, -1e+30)
    top_score = lax.optimization_barrier(jnp.max(scores, axis=-1, keepdims=True))
    weights = jnp.exp(scores - top_score)
    probs = weights / lax.optimization_barrier(jnp.sum(weights, axis=-1, keepdims=True))
    return jnp.einsum('hij,jhd->ihd', low(probs), values_all, precision=HIGH)

def mixer_block(params, pieces):
    conv_inner, conv_state, step_bias, decay_log, skip_gain, gated_gain = params
    query_p, key_p, value_p, gate_z, inner_x, state_in, step_raw, segment, live_rows = pieces
    row_count = segment.shape[0]
    row_index = jnp.arange(row_count, dtype=jnp.int32)
    valid_rows = (row_index < live_rows).astype(jnp.float32)[:, None]
    position = positions_of(segment)
    causal = (row_index[None, :] <= row_index[:, None]) & (segment[None, :] == segment[:, None])
    mask_qk = causal & (row_index[None, :] < live_rows)
    query_r = low(rotate(query_p, position))
    key_r = low(rotate(key_p, position))
    value_r = low(value_p)
    attended = low_back(low(attend(query_r, key_r, value_r, mask_qk))).reshape(row_count, HQ * HEAD_DIMENSION)
    conv_x = jax.nn.silu(causal_conv(inner_x * valid_rows, conv_inner, segment))
    conv_bc = jax.nn.silu(causal_conv(state_in * valid_rows, conv_state, segment))
    step_size = jax.nn.softplus(step_raw + step_bias) * valid_rows
    log_decay = step_size * -jnp.exp(decay_log)
    state_b = low(conv_bc[:, :NS])
    state_c = low(conv_bc[:, NS:])
    gram_mat = low_back(jnp.dot(state_c, state_b.T, precision=HIGH, preferred_element_type=jnp.float32))
    mixing = low(gram_mat[None] * decay_matrix(log_decay, causal))
    x_heads = conv_x.reshape(row_count, NH, HP)
    inflow = low(step_size[:, :, None] * x_heads)
    ssm_out = low_back(jnp.einsum('hij,jhp->ihp', mixing, inflow, precision=HIGH))
    mixed_y = (ssm_out + skip_gain[None, :, None] * x_heads).reshape(row_count, DSSM)
    gated_y = mixed_y * jax.nn.silu(gate_z)
    normed = gated_y * lax.rsqrt(lax.optimization_barrier(jnp.mean(gated_y * gated_y, axis=-1, keepdims=True)) + EPS) * gated_gain
    return (attended, low(normed))

def layer(segment_ids, counts, tokens, mixer_gain, query_proj, key_value_matrix, attend_proj, inner_proj, state_proj, step_proj, conv_inner, conv_state, step_bias, decay_log, skip_gain, gated_gain, mamba_proj, dense_gain, gateup_proj, down_proj):
    valid_rows = (jnp.arange(TOKEN_ROW_SLOTS, dtype=jnp.int32)[None, :] < counts[:, None]).reshape(TOKENS, 1).astype(jnp.float32)
    hidden_entering = low(rms_scale(tokens, mixer_gain))
    queries = low_back(matrix_product(hidden_entering, query_proj)).reshape(N_DP, TOKEN_ROW_SLOTS, HQ, HEAD_DIMENSION)
    key_value_rows = low_back(matrix_product(hidden_entering, key_value_matrix.reshape(MODEL_DIMENSION, 2 * KEY_VALUE_HEADS * HEAD_DIMENSION))).reshape(N_DP, TOKEN_ROW_SLOTS, 2, KEY_VALUE_HEADS, HEAD_DIMENSION)
    inner = low_back(matrix_product(hidden_entering, inner_proj.reshape(MODEL_DIMENSION, 2 * DSSM))).reshape(N_DP, TOKEN_ROW_SLOTS, 2, DSSM)
    state_in = low_back(matrix_product(hidden_entering, state_proj)).reshape(N_DP, TOKEN_ROW_SLOTS, 2 * NS)
    step_raw = low_back(matrix_product(hidden_entering, step_proj)).reshape(N_DP, TOKEN_ROW_SLOTS, NH)
    params = (conv_inner, conv_state, step_bias, decay_log, skip_gain, gated_gain)
    pieces = (queries, key_value_rows[:, :, 0], key_value_rows[:, :, 1], inner[:, :, 0], inner[:, :, 1], state_in, step_raw, segment_ids.reshape(N_DP, TOKEN_ROW_SLOTS), counts)
    attended, normed = lax.map(jax.checkpoint(partial(mixer_block, params)), pieces)
    branch = matrix_product(attended.reshape(TOKENS, HQ * HEAD_DIMENSION), attend_proj) + matrix_product(normed.reshape(TOKENS, DSSM), mamba_proj)
    middle = tokens + low_back(branch * valid_rows)
    hidden_ffn = low(rms_scale(middle, dense_gain))
    gate_up = low_back(matrix_product(hidden_ffn, gateup_proj.reshape(MODEL_DIMENSION, 2 * FF))).reshape(TOKENS, 2, FF)
    activated = low(jax.nn.silu(gate_up[:, 0]) * gate_up[:, 1])
    return middle + low_back(matrix_product(activated, down_proj) * valid_rows)

def reference(tokens, cotangent, segment_ids, counts, mixer_gain, query_proj, key_value_matrix, attend_proj, inner_proj, state_proj, step_proj, conv_inner, conv_state, step_bias, decay_log, skip_gain, gated_gain, mamba_proj, dense_gain, gateup_proj, down_proj):
    inputs = tuple((entry.astype(jnp.float32) for entry in (tokens, mixer_gain, query_proj, key_value_matrix, attend_proj, inner_proj, state_proj, step_proj, conv_inner, conv_state, step_bias, decay_log, skip_gain, gated_gain, mamba_proj, dense_gain, gateup_proj, down_proj)))
    output, pullback = jax.vjp(partial(layer, segment_ids, counts), *inputs)
    grads = pullback(cotangent.astype(jnp.float32))
    return (output.astype(jnp.bfloat16), grads[0], grads[1], grads[2], grads[3], grads[4], grads[5], grads[6], grads[7], grads[8], grads[9], grads[10], grads[11], grads[12], grads[13], grads[14], grads[15], grads[16], grads[17])
```

```python
import functools
import math

import jax
import jax.numpy as jnp
from jax import lax
from jax.experimental import pallas as pl
from jax.experimental.pallas import tpu as pltpu
from jax.sharding import PartitionSpec as P

HP = 64
HEAD_DIMENSION = 128
DSSM = 3072
TILE = 256

EPS = 1e-05
THETA = 100000000000.0


def rounded(values):
    return values.astype(jnp.bfloat16)


def contract(form, left, right):
    return jnp.einsum(form, left, right, preferred_element_type=jnp.float32)


def rms_scale(values, gain):
    return values * lax.rsqrt(jnp.mean(values * values, axis=-1, keepdims=True) + EPS) * gain


def cost(flops, traffic, transcendentals=0):
    return pl.CostEstimate(
        flops=flops, bytes_accessed=traffic, transcendentals=transcendentals
    )


def positions_of(segment):
    row_index = jnp.arange(segment.shape[0], dtype=jnp.int32)
    starts = jnp.concatenate([jnp.ones((1,), jnp.bool_), segment[1:] != segment[:-1]])
    first_row = lax.cummax(jnp.where(starts, row_index, 0), axis=0)
    return row_index - first_row


def silu_parts(values):
    gate = jax.nn.sigmoid(values)
    return values * gate, gate * (1.0 + values * (1.0 - gate))


def dot_nn(left, right):
    return lax.dot_general(left, right, (((1,), (0,)), ((), ())), preferred_element_type=jnp.float32)


def dot_nt(left, right):
    return lax.dot_general(left, right, (((1,), (1,)), ((), ())), preferred_element_type=jnp.float32)


def dot_tn(left, right):
    return lax.dot_general(left, right, (((0,), (0,)), ((), ())), preferred_element_type=jnp.float32)


def shifted_rows(values, lag, same_ref):
    columns = values.shape[1]
    mask = same_ref[lag - 1]
    if columns > mask.shape[1]:
        mask = jnp.concatenate([mask] * (columns // mask.shape[1]), axis=1)
    return mask * pltpu.roll(values, lag, 0)


def conv_rows(values, taps, same_ref):
    total = taps[4:5] + taps[3:4] * values
    for lag in range(1, 4):
        total = total + taps[3 - lag : 4 - lag] * shifted_rows(values, lag, same_ref)
    return total


def conv_rows_back(grad, values, taps, same_ref):
    rows = grad.shape[0]
    total = taps[3:4] * grad
    tap_grads = [None] * 5
    tap_grads[4] = jnp.sum(grad, axis=0, keepdims=True)
    tap_grads[3] = jnp.sum(grad * values, axis=0, keepdims=True)
    for lag in range(1, 4):
        mask = same_ref[lag - 1]
        if grad.shape[1] > mask.shape[1]:
            mask = jnp.concatenate([mask] * (grad.shape[1] // mask.shape[1]), axis=1)
        masked = grad * mask
        total = total + taps[3 - lag : 4 - lag] * pltpu.roll(masked, rows - lag, 0)
        tap_grads[3 - lag] = jnp.sum(
            masked * pltpu.roll(values, lag, 0), axis=0, keepdims=True
        )
    return total, tap_grads


def running_sum(values, backward=False):
    rows = values.shape[0]
    index = lax.broadcasted_iota(jnp.int32, values.shape, 0)
    step = 1
    while step < rows:
        if backward:
            moved = pltpu.roll(values, rows - step, 0)
            values = values + jnp.where(index < rows - step, moved, 0.0)
        else:
            moved = pltpu.roll(values, step, 0)
            values = values + jnp.where(index >= step, moved, 0.0)
        step *= 2
    return values


def step_sizes(raw, extra_ref, live):
    shifted = raw + extra_ref[0:1]
    size = (jnp.maximum(shifted, 0.0) + jnp.log1p(jnp.exp(-jnp.abs(shifted)))) * live
    return shifted, size, -size * extra_ref[1:2]


def lane_column(values, lane):
    lanes = lax.broadcasted_iota(jnp.int32, values.shape, 1)
    return jnp.sum(jnp.where(lanes == lane, values, 0.0), axis=1, keepdims=True)


def ssm_forward_kernel(
    u_ref, z_ref, state_b_ref, state_c_ref, step_ref, wide_ref, conv_ref, extra_ref, live_ref, same_ref, mask_ref,
    y_ref, gated_ref, square_ref, gram, sizes, running, running_t,
):
    pair = pl.program_id(0)
    live = live_ref[...]
    rows = live.shape[0]

    @pl.when(pair == 0)
    def _():
        unused, size, decay = step_sizes(step_ref[...], extra_ref, live)
        total = running_sum(decay)
        sizes[...] = size
        running[...] = total
        running_t[...] = total.T
        width = conv_ref.shape[1]
        wide_live = jnp.concatenate([live] * (width // 128), axis=1)
        state = jnp.concatenate([state_b_ref[...], state_c_ref[...]], axis=1) * wide_live
        inner = conv_rows(state, conv_ref[...], same_ref)
        both = (inner * jax.nn.sigmoid(inner)).astype(jnp.bfloat16)
        gram[...] = dot_nt(both[:, width // 2 :], both[:, : width // 2]) * mask_ref[...]
        square_ref[...] = jnp.zeros_like(square_ref)

    taps = wide_ref[...]
    inner = conv_rows(u_ref[...] * live, taps, same_ref)
    x_in = inner * jax.nn.sigmoid(inner)
    left_lanes = lax.broadcasted_iota(jnp.int32, (rows, 128), 1) < HP
    size = sizes[...]
    size_pair = jnp.where(left_lanes, lane_column(size, 2 * pair), lane_column(size, 2 * pair + 1))
    inflow = (size_pair * x_in).astype(jnp.bfloat16)
    total = running[...]
    columns = [lane_column(total, 2 * pair + k) for k in range(2)]
    row_vectors = [running_t[pl.ds(2 * pair + k, 1), :] for k in range(2)]
    skipped = taps[5:6] * x_in
    gate = z_ref[...]
    gate = gate * jax.nn.sigmoid(gate)
    for block in range(rows // TILE):
        top, end = block * TILE, (block + 1) * TILE
        parts = []
        for k in range(2):
            gaps = columns[k][top:end] - row_vectors[k][:, :end]
            mixing = (gram[top:end, :end] * jnp.exp(jnp.minimum(gaps, 0.0))).astype(jnp.bfloat16)
            parts.append(dot_nn(mixing, inflow[:end]))
        mixed = jnp.where(left_lanes[top:end], parts[0], parts[1]) + skipped[top:end]
        y_ref[top:end, :] = mixed
        gated = mixed * gate[top:end]
        gated_ref[top:end, :] = gated
        square_ref[top:end, :] += gated * gated


def ssm_forward(projected, wide, conv_state, extra, live, same, mask, offsets):
    rows = projected.shape[0]
    pairs = wide.shape[1] // 128
    width = conv_state.shape[1]
    const2 = lambda i: (0, 0)
    at = lambda name, size: offsets[name] // size
    block = lambda name: pl.BlockSpec((rows, 128), lambda i, o=at(name, 128): (0, o + i))
    return pl.pallas_call(
        ssm_forward_kernel,
        grid=(pairs,),
        in_specs=[
            block("u"),
            block("z"),
            pl.BlockSpec((rows, width // 2), lambda i: (0, at("state", width // 2))),
            pl.BlockSpec((rows, width // 2), lambda i: (0, at("state", width // 2) + 1)),
            pl.BlockSpec((rows, 128), lambda i: (0, at("step", 128))),
            pl.BlockSpec((8, 128), lambda i: (0, i)),
            pl.BlockSpec((8, width), const2),
            pl.BlockSpec((8, 128), const2),
            pl.BlockSpec((rows, 128), const2),
            pl.BlockSpec((3, rows, 128), lambda i: (0, 0, 0)),
            pl.BlockSpec((rows, rows), const2),
        ],
        out_specs=[
            pl.BlockSpec((rows, 128), lambda i: (0, i)),
            pl.BlockSpec((rows, 128), lambda i: (0, i)),
            pl.BlockSpec((rows, 128), const2),
        ],
        out_shape=[
            jax.ShapeDtypeStruct((rows, pairs * 128), jnp.float32),
            jax.ShapeDtypeStruct((rows, pairs * 128), jnp.float32),
            jax.ShapeDtypeStruct((rows, 128), jnp.float32),
        ],
        scratch_shapes=[
            pltpu.VMEM((rows, rows), jnp.float32),
            pltpu.VMEM((rows, 128), jnp.float32),
            pltpu.VMEM((rows, 128), jnp.float32),
            pltpu.VMEM((128, rows), jnp.float32),
        ],
        compiler_params=pltpu.CompilerParams(vmem_limit_bytes=40 * 2**20),
        name="ssm_forward",
    )(projected, projected, projected, projected, projected, wide, conv_state, extra, live, same, mask)


def ssm_backward_kernel(
    dn_ref, y_ref, u_ref, z_ref, state_b_ref, state_c_ref, step_ref, inverse_ref, own_ref, other_ref,
    wide_ref, conv_ref, extra_ref, live_ref, same_ref, mask_t_ref,
    dz_ref, du_ref, ds_ref, dr_ref, wide_grad_ref, conv_grad_ref, extra_grad_ref,
    gram_t, gram_grad, sizes, decays, running, running_t, size_grad, total_grad, states, state_slopes,
):
    pair = pl.program_id(0)
    live = live_ref[...]
    rows = live.shape[0]
    width = conv_ref.shape[1]
    wide_live = jnp.concatenate([live] * (width // 128), axis=1)

    @pl.when(pair == 0)
    def _():
        unused, size, decay = step_sizes(step_ref[...], extra_ref, live)
        total = running_sum(decay)
        sizes[...] = size
        decays[...] = decay
        running[...] = total
        running_t[...] = total.T
        state = jnp.concatenate([state_b_ref[...], state_c_ref[...]], axis=1) * wide_live
        inner = conv_rows(state, conv_ref[...], same_ref)
        value, slope = silu_parts(inner)
        both = value.astype(jnp.bfloat16)
        states[...] = both
        state_slopes[...] = slope
        gram_t[...] = dot_nt(both[:, : width // 2], both[:, width // 2 :]) * mask_t_ref[...]
        gram_grad[...] = jnp.zeros_like(gram_grad)
        size_grad[...] = jnp.zeros_like(size_grad)
        total_grad[...] = jnp.zeros_like(total_grad)

    taps = wide_ref[...]
    u_live = u_ref[...] * live
    inner = conv_rows(u_live, taps, same_ref)
    x_in, x_slope = silu_parts(inner)
    gate, gate_slope = silu_parts(z_ref[...])
    mixed = y_ref[...]
    gated = mixed * gate
    inverse = inverse_ref[:, 0:1]
    pull = (own_ref[:, 0:1] + other_ref[:, 0:1]) * inverse * inverse * inverse / DSSM
    grad_gated = taps[6:7] * dn_ref[...] * inverse - gated * pull
    grad_mixed = grad_gated * gate
    dz_ref[...] = (grad_gated * mixed * gate_slope).astype(dz_ref.dtype)
    grad_mixed_b = grad_mixed.astype(jnp.bfloat16)
    lanes = lax.broadcasted_iota(jnp.int32, (rows, 128), 1)
    left_lanes = lanes < HP
    size = sizes[...]
    size_pair = jnp.where(left_lanes, lane_column(size, 2 * pair), lane_column(size, 2 * pair + 1))
    inflow = (size_pair * x_in).astype(jnp.bfloat16)
    zero = jnp.zeros_like(inflow)
    inflow_heads = [jnp.where(left_lanes, inflow, zero), jnp.where(left_lanes, zero, inflow)]
    total = running[...]
    columns = [lane_column(total, 2 * pair + k) for k in range(2)]
    row_vectors = [running_t[pl.ds(2 * pair + k, 1), :] for k in range(2)]
    blocks = []
    for block in range(rows // TILE):
        top, end = block * TILE, (block + 1) * TILE
        parts = []
        gram_part = None
        for k in range(2):
            gaps = row_vectors[k][:, top:] - columns[k][top:end]
            decay = jnp.exp(jnp.minimum(gaps, 0.0))
            mixing_t = (gram_t[top:end, top:] * decay).astype(jnp.bfloat16)
            parts.append(dot_nn(mixing_t, grad_mixed_b[top:]))
            term = dot_nt(inflow_heads[k][top:end], grad_mixed_b[top:]) * decay
            gram_part = term if gram_part is None else gram_part + term
        gram_grad[top:end, top:] += gram_part
        blocks.append(jnp.where(left_lanes[top:end], parts[0], parts[1]))
    grad_inflow = jnp.concatenate(blocks, axis=0)
    grad_x = grad_mixed * taps[5:6] + grad_inflow * size_pair
    by_size = grad_inflow * x_in
    mixed_only = mixed - taps[5:6] * x_in
    by_total = grad_mixed_b.astype(jnp.float32) * mixed_only - grad_inflow * inflow.astype(jnp.float32)
    size_sum, total_sum = size_grad[...], total_grad[...]
    for k in range(2):
        mine = left_lanes if k == 0 else jnp.logical_not(left_lanes)
        here = lanes == 2 * pair + k
        size_sum = jnp.where(
            here, jnp.sum(jnp.where(mine, by_size, 0.0), axis=1, keepdims=True), size_sum
        )
        total_sum = jnp.where(
            here, jnp.sum(jnp.where(mine, by_total, 0.0), axis=1, keepdims=True), total_sum
        )
    size_grad[...] = size_sum
    total_grad[...] = total_sum
    grad_u, tap_grads = conv_rows_back(grad_x * x_slope, u_live, taps, same_ref)
    du_ref[...] = (grad_u * live).astype(du_ref.dtype)
    skip_grad = jnp.sum(grad_mixed * x_in, axis=0, keepdims=True)
    wide_grad_ref[...] = jnp.concatenate(
        tap_grads + [skip_grad, jnp.zeros((2, 128), jnp.float32)], axis=0
    )

    @pl.when(pair == pl.num_programs(0) - 1)
    def _():
        half = width // 2
        gram_grad_b = (gram_grad[...] * mask_t_ref[...]).astype(jnp.bfloat16)
        grad_b = dot_nn(gram_grad_b, states[:, half:])
        grad_c = dot_tn(gram_grad_b, states[:, :half])
        grad_bc = jnp.concatenate([grad_b, grad_c], axis=1) * state_slopes[...]
        state = jnp.concatenate([state_b_ref[...], state_c_ref[...]], axis=1) * wide_live
        grad_in, state_taps = conv_rows_back(grad_bc, state, conv_ref[...], same_ref)
        ds_ref[...] = (grad_in * wide_live).astype(ds_ref.dtype)
        conv_grad_ref[...] = jnp.concatenate(
            state_taps + [jnp.zeros((3, width), jnp.float32)], axis=0
        )
        decay_grad = running_sum(total_grad[...], backward=True)
        shifted = step_ref[...] + extra_ref[0:1]
        grad_size = size_grad[...] - decay_grad * extra_ref[1:2]
        grad_raw = grad_size * live * jax.nn.sigmoid(shifted)
        dr_ref[...] = grad_raw.astype(dr_ref.dtype)
        extra_grad_ref[...] = jnp.concatenate(
            [
                jnp.sum(grad_raw, axis=0, keepdims=True),
                jnp.sum(decay_grad * decays[...], axis=0, keepdims=True),
                jnp.zeros((6, 128), jnp.float32),
            ],
            axis=0,
        )


def ssm_backward(
    grad_normed, mixed, projected, inverse, own, other, wide, conv_state, extra, live, same, mask_t, offsets
):
    rows = projected.shape[0]
    pairs = wide.shape[1] // 128
    width = conv_state.shape[1]
    const2 = lambda i: (0, 0)
    at = lambda name, size: offsets[name] // size
    block = lambda name: pl.BlockSpec((rows, 128), lambda i, o=at(name, 128): (0, o + i))
    plain = pl.BlockSpec((rows, 128), lambda i: (0, i))
    f32, b16 = jnp.float32, jnp.bfloat16
    return pl.pallas_call(
        ssm_backward_kernel,
        grid=(pairs,),
        in_specs=[
            plain,
            plain,
            block("u"),
            block("z"),
            pl.BlockSpec((rows, width // 2), lambda i: (0, at("state", width // 2))),
            pl.BlockSpec((rows, width // 2), lambda i: (0, at("state", width // 2) + 1)),
            pl.BlockSpec((rows, 128), lambda i: (0, at("step", 128))),
            pl.BlockSpec((rows, 128), const2),
            pl.BlockSpec((rows, 128), const2),
            pl.BlockSpec((rows, 128), const2),
            pl.BlockSpec((8, 128), lambda i: (0, i)),
            pl.BlockSpec((8, width), const2),
            pl.BlockSpec((8, 128), const2),
            pl.BlockSpec((rows, 128), const2),
            pl.BlockSpec((3, rows, 128), lambda i: (0, 0, 0)),
            pl.BlockSpec((rows, rows), const2),
        ],
        out_specs=[
            plain,
            plain,
            pl.BlockSpec((rows, width), const2),
            pl.BlockSpec((rows, 128), const2),
            pl.BlockSpec((8, 128), lambda i: (0, i)),
            pl.BlockSpec((8, width), const2),
            pl.BlockSpec((8, 128), const2),
        ],
        out_shape=[
            jax.ShapeDtypeStruct((rows, pairs * 128), b16),
            jax.ShapeDtypeStruct((rows, pairs * 128), b16),
            jax.ShapeDtypeStruct((rows, width), b16),
            jax.ShapeDtypeStruct((rows, 128), b16),
            jax.ShapeDtypeStruct((8, pairs * 128), f32),
            jax.ShapeDtypeStruct((8, width), f32),
            jax.ShapeDtypeStruct((8, 128), f32),
        ],
        scratch_shapes=[
            pltpu.VMEM((rows, rows), f32),
            pltpu.VMEM((rows, rows), f32),
            pltpu.VMEM((rows, 128), f32),
            pltpu.VMEM((rows, 128), f32),
            pltpu.VMEM((rows, 128), f32),
            pltpu.VMEM((128, rows), f32),
            pltpu.VMEM((rows, 128), f32),
            pltpu.VMEM((rows, 128), f32),
            pltpu.VMEM((rows, width), b16),
            pltpu.VMEM((rows, width), f32),
        ],
        compiler_params=pltpu.CompilerParams(vmem_limit_bytes=48 * 2**20),
        cost_estimate=cost(1, 1),
        name="ssm_backward",
    )(
        grad_normed, mixed, projected, projected, projected, projected, projected, inverse, own, other,
        wide, conv_state, extra, live, same, mask_t,
    )


def turned(values, cos_ref, sin_ref):
    return values * cos_ref[...] + pltpu.roll(values, HEAD_DIMENSION // 2, 1) * sin_ref[...]


def attention_forward_kernel(
    q_ref, k_ref, v_ref, cos_ref, sin_ref, mask_ref, out_ref, query_ref, key_ref, value_ref, log_ref
):
    head = pl.program_id(0)
    rows = q_ref.shape[0]
    scale = HEAD_DIMENSION**-0.5

    @pl.when(head == 0)
    def _():
        key_ref[...] = turned(k_ref[...], cos_ref, sin_ref).astype(jnp.bfloat16)
        value_ref[...] = v_ref[...].astype(jnp.bfloat16)

    query = turned(q_ref[...], cos_ref, sin_ref).astype(jnp.bfloat16)
    query_ref[...] = query
    for block in range(rows // TILE):
        top, end = block * TILE, (block + 1) * TILE
        scores = dot_nt(query[top:end], key_ref[:end, :]) * scale
        scores = jnp.where(mask_ref[top:end, :end] > 0.0, scores, -1e30)
        largest = jnp.max(scores, axis=1, keepdims=True)
        weights = jnp.exp(scores - largest)
        total = jnp.sum(weights, axis=1, keepdims=True)
        probs = (weights / total).astype(jnp.bfloat16)
        out_ref[top:end, :] = dot_nn(probs, value_ref[:end, :]).astype(out_ref.dtype)
        log_ref[top:end, :] = jnp.broadcast_to(largest + jnp.log(total), (TILE, 128))


def attention_forward(projected, cos, sin, mask, offsets, heads):
    rows = projected.shape[0]
    at = lambda name: offsets[name] // 128
    const2 = lambda i: (0, 0)
    one = pl.BlockSpec((rows, 128), const2)
    each = pl.BlockSpec((rows, 128), lambda i: (0, i))
    b16 = jnp.bfloat16
    return pl.pallas_call(
        attention_forward_kernel,
        grid=(heads,),
        in_specs=[
            pl.BlockSpec((rows, 128), lambda i: (0, at("q") + i)),
            pl.BlockSpec((rows, 128), lambda i: (0, at("kv"))),
            pl.BlockSpec((rows, 128), lambda i: (0, at("kv") + 1)),
            one,
            one,
            pl.BlockSpec((rows, rows), const2),
        ],
        out_specs=[each, each, one, one, each],
        out_shape=[
            jax.ShapeDtypeStruct((rows, heads * 128), b16),
            jax.ShapeDtypeStruct((rows, heads * 128), b16),
            jax.ShapeDtypeStruct((rows, 128), b16),
            jax.ShapeDtypeStruct((rows, 128), b16),
            jax.ShapeDtypeStruct((rows, heads * 128), jnp.float32),
        ],
        compiler_params=pltpu.CompilerParams(vmem_limit_bytes=24 * 2**20),
        name="attention_forward",
    )(projected, projected, projected, cos, sin, mask)


def attention_backward_kernel(
    grad_ref, query_ref, key_ref, value_ref, log_ref, cos_ref, sin_ref, mask_ref,
    dq_ref, dk_ref, dv_ref, key_sum, value_sum,
):
    head = pl.program_id(0)
    rows = query_ref.shape[0]
    scale = HEAD_DIMENSION**-0.5

    @pl.when(head == 0)
    def _():
        key_sum[...] = jnp.zeros_like(key_sum)
        value_sum[...] = jnp.zeros_like(value_sum)

    for block in range(rows // TILE):
        top, end = block * TILE, (block + 1) * TILE
        query = query_ref[top:end, :]
        grad = grad_ref[top:end, :]
        scores = dot_nt(query, key_ref[:end, :]) * scale
        scores = jnp.where(mask_ref[top:end, :end] > 0.0, scores, -1e30)
        probs = jnp.exp(scores - log_ref[top:end, 0:1])
        grad_probs = dot_nt(grad, value_ref[:end, :])
        inner = jnp.sum(grad_probs * probs, axis=1, keepdims=True)
        grad_scores = (probs * (grad_probs - inner)).astype(jnp.bfloat16)
        dq = dot_nn(grad_scores, key_ref[:end, :]) * scale
        dq_ref[top:end, :] = (
            dq * cos_ref[top:end, :]
            - pltpu.roll(dq, HEAD_DIMENSION // 2, 1) * sin_ref[top:end, :]
        ).astype(dq_ref.dtype)
        key_sum[:end, :] += dot_tn(grad_scores, query)
        value_sum[:end, :] += dot_tn(probs.astype(jnp.bfloat16), grad)

    @pl.when(head == pl.num_programs(0) - 1)
    def _():
        dk = key_sum[...] * scale
        dk_ref[...] = (
            dk * cos_ref[...] - pltpu.roll(dk, HEAD_DIMENSION // 2, 1) * sin_ref[...]
        ).astype(dk_ref.dtype)
        dv_ref[...] = value_sum[...].astype(dv_ref.dtype)


def attention_backward(grad, query, key, value, logs, cos, sin, mask):
    rows = query.shape[0]
    heads = query.shape[1] // 128
    const2 = lambda i: (0, 0)
    one = pl.BlockSpec((rows, 128), const2)
    each = pl.BlockSpec((rows, 128), lambda i: (0, i))
    b16 = jnp.bfloat16
    return pl.pallas_call(
        attention_backward_kernel,
        grid=(heads,),
        in_specs=[each, each, one, one, each, one, one, pl.BlockSpec((rows, rows), const2)],
        out_specs=[each, one, one],
        out_shape=[
            jax.ShapeDtypeStruct((rows, heads * 128), b16),
            jax.ShapeDtypeStruct((rows, 128), b16),
            jax.ShapeDtypeStruct((rows, 128), b16),
        ],
        scratch_shapes=[pltpu.VMEM((rows, 128), jnp.float32), pltpu.VMEM((rows, 128), jnp.float32)],
        compiler_params=pltpu.CompilerParams(vmem_limit_bytes=24 * 2**20),
        cost_estimate=cost(1, 1),
        name="attention_backward",
    )(grad, query, key, value, logs, cos, sin, mask)


def feed_forward_kernel(in_ref, gate_w_ref, up_w_ref, act_ref, gate_ref, up_ref):
    gate = dot_nn(in_ref[...], gate_w_ref[...])
    up = dot_nn(in_ref[...], up_w_ref[...])
    gate_ref[...] = gate
    up_ref[...] = up
    act_ref[...] = (gate * jax.nn.sigmoid(gate) * up).astype(act_ref.dtype)


def feed_forward(ffn_in, weights, first, hidden, tile=256):
    rows, model = ffn_in.shape
    steps = hidden // tile
    each = pl.BlockSpec((rows, tile), lambda i: (0, i))
    return pl.pallas_call(
        feed_forward_kernel,
        grid=(steps,),
        in_specs=[
            pl.BlockSpec((rows, model), lambda i: (0, 0)),
            pl.BlockSpec((model, tile), lambda i: (0, first // tile + i)),
            pl.BlockSpec((model, tile), lambda i: (0, first // tile + steps + i)),
        ],
        out_specs=[each, each, each],
        out_shape=[
            jax.ShapeDtypeStruct((rows, hidden), jnp.bfloat16),
            jax.ShapeDtypeStruct((rows, hidden), jnp.float32),
            jax.ShapeDtypeStruct((rows, hidden), jnp.float32),
        ],
        compiler_params=pltpu.CompilerParams(vmem_limit_bytes=32 * 2**20),
        cost_estimate=cost(4 * rows * model * hidden, 4 * model * hidden + 12 * rows * hidden),
        name="feed_forward",
    )(ffn_in, weights, weights)


def feed_forward_back_kernel(
    grad_ref, down_ref, gate_ref, up_ref, gate_w_ref, up_w_ref, dgate_ref, dup_ref, din_ref, total
):
    step = pl.program_id(0)

    @pl.when(step == 0)
    def _():
        total[...] = jnp.zeros_like(total)

    grad_act = dot_nn(grad_ref[...], down_ref[...])
    gate = gate_ref[...]
    value, slope = silu_parts(gate)
    dgate = (grad_act * up_ref[...] * slope).astype(jnp.bfloat16)
    dup = (grad_act * value).astype(jnp.bfloat16)
    dgate_ref[...] = dgate
    dup_ref[...] = dup
    total[...] += dot_nt(dgate, gate_w_ref[...]) + dot_nt(dup, up_w_ref[...])

    @pl.when(step == pl.num_programs(0) - 1)
    def _():
        din_ref[...] = total[...].astype(din_ref.dtype)


def feed_forward_back(grad, down_t, gate, up, weights, first, tile=512):
    rows, model = grad.shape
    hidden = gate.shape[1]
    steps = hidden // tile
    each = pl.BlockSpec((rows, tile), lambda i: (0, i))
    whole = pl.BlockSpec((rows, model), lambda i: (0, 0))
    b16 = jnp.bfloat16
    return pl.pallas_call(
        feed_forward_back_kernel,
        grid=(steps,),
        in_specs=[
            whole,
            pl.BlockSpec((model, tile), lambda i: (0, first // tile + 2 * steps + i)),
            each,
            each,
            pl.BlockSpec((model, tile), lambda i: (0, first // tile + i)),
            pl.BlockSpec((model, tile), lambda i: (0, first // tile + steps + i)),
        ],
        out_specs=[each, each, whole],
        out_shape=[
            jax.ShapeDtypeStruct((rows, hidden), b16),
            jax.ShapeDtypeStruct((rows, hidden), b16),
            jax.ShapeDtypeStruct((rows, model), b16),
        ],
        scratch_shapes=[pltpu.VMEM((rows, model), jnp.float32)],
        compiler_params=pltpu.CompilerParams(vmem_limit_bytes=40 * 2**20),
        cost_estimate=cost(1, 1),
        name="feed_forward_back",
    )(grad, down_t, gate, up, weights, weights)


def norm_back_kernel(
    grad_ref, weight_ref, gated_ref, inverse_ref, gain_ref, dn_ref, row_ref, column_ref
):
    step = pl.program_id(0)

    @pl.when(step == 0)
    def _():
        row_ref[...] = jnp.zeros_like(row_ref)

    grad = dot_nn(grad_ref[...], weight_ref[...])
    dn_ref[...] = grad
    product = grad * gated_ref[...]
    scaled = product * gain_ref[0:1]
    part = scaled[:, :128]
    for k in range(1, scaled.shape[1] // 128):
        part = part + scaled[:, k * 128 : (k + 1) * 128]
    row_ref[...] += part
    total = jnp.sum(product * inverse_ref[:, 0:1], axis=0, keepdims=True)
    column_ref[...] = jnp.broadcast_to(total, column_ref.shape)

    @pl.when(step == pl.num_programs(0) - 1)
    def _():
        row_ref[...] = jnp.broadcast_to(
            jnp.sum(row_ref[...], axis=1, keepdims=True), row_ref.shape
        )


def norm_back(grad, weights, first, gated, inverse, gains, tile=256):
    rows, model = grad.shape
    width = gated.shape[1]
    each = pl.BlockSpec((rows, tile), lambda i: (0, i))
    f32 = jnp.float32
    return pl.pallas_call(
        norm_back_kernel,
        grid=(width // tile,),
        in_specs=[
            pl.BlockSpec((rows, model), lambda i: (0, 0)),
            pl.BlockSpec((model, tile), lambda i: (0, first // tile + i)),
            each,
            pl.BlockSpec((rows, 128), lambda i: (0, 0)),
            pl.BlockSpec((8, tile), lambda i: (0, i)),
        ],
        out_specs=[
            each,
            pl.BlockSpec((rows, 128), lambda i: (0, 0)),
            pl.BlockSpec((8, tile), lambda i: (0, i)),
        ],
        out_shape=[
            jax.ShapeDtypeStruct((rows, width), f32),
            jax.ShapeDtypeStruct((rows, 128), f32),
            jax.ShapeDtypeStruct((8, width), f32),
        ],
        compiler_params=pltpu.CompilerParams(vmem_limit_bytes=24 * 2**20),
        cost_estimate=cost(1, 1),
        name="norm_back",
    )(grad, weights, gated, inverse, gains)


def reorder_kernel(order_ref, in_ref, out_ref):
    width = in_ref.shape[1] // order_ref.shape[0]
    for place in range(order_ref.shape[0]):
        column = pl.multiple_of(order_ref[place] * width, width)
        out_ref[:, place * width : (place + 1) * width] = in_ref[:, pl.ds(column, width)]


def reorder_columns(values, order):
    rows, model = values.shape
    count = order.shape[0]
    width = model // count
    if width % 128:
        return jnp.take(values.reshape(rows, count, width), order, axis=1).reshape(rows, model)
    return pl.pallas_call(
        reorder_kernel,
        in_specs=[
            pl.BlockSpec(memory_space=pltpu.SMEM),
            pl.BlockSpec(memory_space=pltpu.VMEM),
        ],
        out_specs=pl.BlockSpec(memory_space=pltpu.VMEM),
        out_shape=jax.ShapeDtypeStruct(values.shape, values.dtype),
        compiler_params=pltpu.CompilerParams(vmem_limit_bytes=16 * 2**20),
        cost_estimate=cost(1, 1),
        name="reorder_columns",
    )(order, values)


def scatter_part_kernel(left_ref, right_ref, *refs):
    got_refs, out_ref, turned_left = refs[:-2], refs[-2], refs[-1]

    @pl.when(pl.program_id(0) == 0)
    def _():
        turned_left[...] = left_ref[...].T

    total = dot_nn(turned_left[...], right_ref[...])
    for got_ref in got_refs:
        total = total + got_ref[...].astype(jnp.float32)
    out_ref[...] = total.astype(out_ref.dtype)


def scatter_part(left, right, gots, first, size, dtype):
    rows, width = right.shape
    if size % 128 or first % size:
        total = contract("tm,tn->mn", left[:, first : first + size], right)
        for got, start in gots:
            total = total + got[start : start + size].astype(jnp.float32)
        return total.astype(dtype)
    tile = max(t for t in (128, 256, 384, 512) if width % t == 0)
    return pl.pallas_call(
        scatter_part_kernel,
        grid=(width // tile,),
        in_specs=[
            pl.BlockSpec((rows, size), lambda i: (0, first // size)),
            pl.BlockSpec((rows, tile), lambda i: (0, i)),
        ]
        + [
            pl.BlockSpec((size, tile), lambda i, at=start // size: (at, i)) for unused, start in gots
        ],
        out_specs=pl.BlockSpec((size, tile), lambda i: (0, i)),
        out_shape=jax.ShapeDtypeStruct((size, width), dtype),
        scratch_shapes=[pltpu.VMEM((size, rows), jnp.bfloat16)],
        compiler_params=pltpu.CompilerParams(vmem_limit_bytes=32 * 2**20),
        cost_estimate=cost(1, 1),
        name="scatter_part",
    )(left, right, *[got for got, unused in gots])


def product_kernel(left_ref, right_ref, out_ref):
    out_ref[...] = dot_nn(left_ref[...], right_ref[...]).astype(out_ref.dtype)


def product(left, right, first, width, tile=256):
    rows, model = left.shape
    return pl.pallas_call(
        product_kernel,
        grid=(width // tile,),
        in_specs=[
            pl.BlockSpec((rows, model), lambda i: (0, 0)),
            pl.BlockSpec((model, tile), lambda i: (0, first // tile + i)),
        ],
        out_specs=pl.BlockSpec((rows, tile), lambda i: (0, i)),
        out_shape=jax.ShapeDtypeStruct((rows, width), jnp.bfloat16),
        compiler_params=pltpu.CompilerParams(vmem_limit_bytes=24 * 2**20),
        cost_estimate=cost(1, 1),
        name="product",
    )(left, right)


def product_back_kernel(left_ref, right_ref, out_ref):
    out_ref[...] = dot_nt(left_ref[...], right_ref[...]).astype(out_ref.dtype)


def product_back(left, right, first, tile=512):
    rows, width = left.shape
    model = right.shape[0]
    return pl.pallas_call(
        product_back_kernel,
        grid=(model // tile,),
        in_specs=[
            pl.BlockSpec((rows, width), lambda i: (0, 0)),
            pl.BlockSpec((tile, width), lambda i: (i, first // width)),
        ],
        out_specs=pl.BlockSpec((rows, tile), lambda i: (0, i)),
        out_shape=jax.ShapeDtypeStruct((rows, model), jnp.bfloat16),
        compiler_params=pltpu.CompilerParams(vmem_limit_bytes=40 * 2**20),
        cost_estimate=cost(1, 1),
        name="product_back",
    )(left, right)


def join_kernel(ready_ref, got_ref, out_ref):
    out_ref[...] = (ready_ref[...] + got_ref[...].astype(jnp.float32)).astype(out_ref.dtype)


def join_parts(ready, got, start, dtype):
    size, width = ready.shape
    if size % 128 or start % size:
        return (ready + got[start : start + size].astype(jnp.float32)).astype(dtype)
    tile = max(t for t in (128, 256, 384, 512, 768, 1024) if width % t == 0)
    return pl.pallas_call(
        join_kernel,
        grid=(width // tile,),
        in_specs=[
            pl.BlockSpec((size, tile), lambda i: (0, i)),
            pl.BlockSpec((size, tile), lambda i: (start // size, i)),
        ],
        out_specs=pl.BlockSpec((size, tile), lambda i: (0, i)),
        out_shape=jax.ShapeDtypeStruct((size, width), dtype),
        compiler_params=pltpu.CompilerParams(vmem_limit_bytes=24 * 2**20),
        cost_estimate=cost(1, 1),
        name="join_parts",
    )(ready, got)


def rms_back_kernel(value_ref, gain_ref, own_ref, other_ref, base_ref, live_ref, *out_refs):
    values = value_ref[...].astype(jnp.float32)
    gain = gain_ref[0:1]
    grad = own_ref[...].astype(jnp.float32) + other_ref[...].astype(jnp.float32)
    scale = lax.rsqrt(jnp.mean(values * values, axis=1, keepdims=True) + EPS)
    unit = values * scale
    scaled = grad * gain
    pull = jnp.mean(scaled * unit, axis=1, keepdims=True)
    total = base_ref[...].astype(jnp.float32) + (scaled - unit * pull) * scale
    out_refs[0][...] = total
    if len(out_refs) == 3:
        out_refs[2][...] = (total * live_ref[:, 0:1]).astype(jnp.bfloat16)
    gain_grad = jnp.broadcast_to(jnp.sum(grad * unit, axis=0, keepdims=True), out_refs[1].shape)

    @pl.when(pl.program_id(0) == 0)
    def _():
        out_refs[1][...] = gain_grad

    @pl.when(pl.program_id(0) > 0)
    def _():
        out_refs[1][...] += gain_grad


def rms_back(values, gain, own, other, base, live, with_rounded, tile=128):
    rows, model = values.shape
    each = pl.BlockSpec((tile, model), lambda i: (i, 0))
    whole = pl.BlockSpec((8, model), lambda i: (0, 0))
    shapes = [
        jax.ShapeDtypeStruct((rows, model), jnp.float32),
        jax.ShapeDtypeStruct((8, model), jnp.float32),
    ]
    if with_rounded:
        shapes.append(jax.ShapeDtypeStruct((rows, model), jnp.bfloat16))
    return pl.pallas_call(
        rms_back_kernel,
        grid=(rows // tile,),
        in_specs=[each, whole, each, each, each, pl.BlockSpec((tile, 128), lambda i: (i, 0))],
        out_specs=[each, whole, each][: len(shapes)],
        out_shape=shapes,
        compiler_params=pltpu.CompilerParams(vmem_limit_bytes=32 * 2**20),
        cost_estimate=cost(1, 1),
        name="rms_back",
    )(values, gain, own, other, base, live)


def beside_kernel(widths, *refs):
    out_ref, place, refs = refs[-1], 0, list(refs[:-1])
    for width, terms in widths:
        total = refs.pop(0)[...]
        if terms == 2:
            total = total.astype(jnp.float32) + refs.pop(0)[...].astype(jnp.float32)
        out_ref[:, place : place + width] = total.astype(out_ref.dtype)
        place += width
    if place < out_ref.shape[1]:
        out_ref[:, place:] = jnp.zeros((out_ref.shape[0], out_ref.shape[1] - place), out_ref.dtype)


def beside(width, *columns, tile=128):
    groups = [c if isinstance(c, tuple) else (c,) for c in columns]
    widths = tuple((g[0].shape[1], len(g)) for g in groups)
    arrays = [a for g in groups for a in g]
    rows = arrays[0].shape[0]
    return pl.pallas_call(
        functools.partial(beside_kernel, widths),
        grid=(rows // tile,),
        in_specs=[pl.BlockSpec((tile, a.shape[1]), lambda i: (i, 0)) for a in arrays],
        out_specs=pl.BlockSpec((tile, width), lambda i: (i, 0)),
        out_shape=jax.ShapeDtypeStruct((rows, width), jnp.bfloat16),
        compiler_params=pltpu.CompilerParams(vmem_limit_bytes=24 * 2**20),
        cost_estimate=cost(1, 1),
        name="beside",
    )(*arrays)


def hidden_back_kernel(first_ref, second_ref, keep_ref, weight_ref, out_ref, total):
    step = pl.program_id(0)
    half = pl.num_programs(0) // 2

    @pl.when(step == 0)
    def _():
        total[...] = jnp.zeros_like(total)

    left = jnp.where(step < half, first_ref[...], second_ref[...] * keep_ref[0:1])
    total[...] += dot_nt(left, weight_ref[...])

    @pl.when(step == pl.num_programs(0) - 1)
    def _():
        out_ref[...] = total[...].astype(out_ref.dtype)


def hidden_back(first, second, keep, weights, tile=768):
    rows, width = first.shape
    model = weights.shape[0]
    steps = width // tile
    return pl.pallas_call(
        hidden_back_kernel,
        grid=(2 * steps,),
        in_specs=[
            pl.BlockSpec((rows, tile), lambda i: (0, jnp.minimum(i, steps - 1))),
            pl.BlockSpec((rows, tile), lambda i: (0, jnp.maximum(i - steps, 0))),
            pl.BlockSpec((8, tile), lambda i: (0, jnp.maximum(i - steps, 0))),
            pl.BlockSpec((model, tile), lambda i: (0, i)),
        ],
        out_specs=pl.BlockSpec((rows, model), lambda i: (0, 0)),
        out_shape=jax.ShapeDtypeStruct((rows, model), jnp.bfloat16),
        scratch_shapes=[pltpu.VMEM((rows, model), jnp.float32)],
        compiler_params=pltpu.CompilerParams(vmem_limit_bytes=32 * 2**20),
        cost_estimate=cost(1, 1),
        name="hidden_back",
    )(first, second, keep, weights)


def rms_forward_kernel(base_ref, own_ref, other_ref, live_ref, gain_ref, middle_ref, out_ref):
    added = own_ref[...].astype(jnp.float32) + other_ref[...].astype(jnp.float32)
    values = base_ref[...].astype(jnp.float32) + added * live_ref[:, 0:1]
    middle_ref[...] = values
    scale = lax.rsqrt(jnp.mean(values * values, axis=1, keepdims=True) + EPS)
    out_ref[...] = (values * scale * gain_ref[0:1]).astype(out_ref.dtype)


def rms_forward(base, own, other, live, gain, tile=128):
    rows, model = base.shape
    each = pl.BlockSpec((tile, model), lambda i: (i, 0))
    return pl.pallas_call(
        rms_forward_kernel,
        grid=(rows // tile,),
        in_specs=[
            each,
            each,
            each,
            pl.BlockSpec((tile, 128), lambda i: (i, 0)),
            pl.BlockSpec((8, model), lambda i: (0, 0)),
        ],
        out_specs=[each, each],
        out_shape=[
            jax.ShapeDtypeStruct((rows, model), jnp.float32),
            jax.ShapeDtypeStruct((rows, model), jnp.bfloat16),
        ],
        compiler_params=pltpu.CompilerParams(vmem_limit_bytes=32 * 2**20),
        cost_estimate=cost(1, 1),
        name="rms_forward",
    )(base, own, other, live, gain)


def output_kernel(base_ref, own_ref, other_ref, live_ref, out_ref):
    added = own_ref[...].astype(jnp.float32) + other_ref[...].astype(jnp.float32)
    out_ref[...] = (base_ref[...] + added * live_ref[:, 0:1]).astype(out_ref.dtype)


def output_rows(base, own, other, live, tile=128):
    rows, model = base.shape
    each = pl.BlockSpec((tile, model), lambda i: (i, 0))
    return pl.pallas_call(
        output_kernel,
        grid=(rows // tile,),
        in_specs=[each, each, each, pl.BlockSpec((tile, 128), lambda i: (i, 0))],
        out_specs=each,
        out_shape=jax.ShapeDtypeStruct((rows, model), jnp.bfloat16),
        compiler_params=pltpu.CompilerParams(vmem_limit_bytes=24 * 2**20),
        cost_estimate=cost(1, 1),
        name="output_rows",
    )(base, own, other, live)


def stack_kernel(counts, *refs):
    out_ref, place = refs[-1], 0
    out_ref[...] = jnp.zeros_like(out_ref)
    for count, ref in zip(counts, refs):
        out_ref[place : place + count, : ref.shape[1]] = ref[:count, :]
        place += count


def stack_rows(width, *parts):
    counts = tuple(count for unused, count in parts)
    total = -(-sum(counts) // 8) * 8
    vmem = pl.BlockSpec(memory_space=pltpu.VMEM)
    return pl.pallas_call(
        functools.partial(stack_kernel, counts),
        in_specs=[vmem] * len(parts),
        out_specs=vmem,
        out_shape=jax.ShapeDtypeStruct((total, width), jnp.float32),
        compiler_params=pltpu.CompilerParams(vmem_limit_bytes=8 * 2**20),
        cost_estimate=cost(1, 1),
        name="stack_rows",
    )(*[part for part, unused in parts])


def tie(*values):
    return lax.optimization_barrier(values)


def pair_swap(values):
    return lax.ppermute(values, "tensor", [(0, 1), (1, 0)])


def pair_sum(values):
    own = lax.reduce_precision(values.astype(jnp.float32), 8, 7)
    return own + pair_swap(own.astype(jnp.bfloat16)).astype(jnp.float32)


def pair_join(values):
    other = pair_swap(values)
    first = lax.axis_index("tensor") == 0
    return jnp.concatenate(
        [jnp.where(first, values, other), jnp.where(first, other, values)], axis=0
    )


def after(values, *earlier):
    return lax.optimization_barrier((values, *earlier))[0]


def bits_of(count):
    return tuple(1 << place for place in range(count.bit_length() - 1))


def owner_order(bits):
    offsets = [0]
    for bit in reversed(bits):
        offsets = [offset | bit for offset in offsets] + offsets
    return lax.axis_index("dp") ^ jnp.array(offsets, jnp.int32)


def across(values, bit):
    count = lax.axis_size("dp")
    return lax.ppermute(values, "dp", [(i, i ^ bit) for i in range(count)])


class Scatter:
    def __init__(self, left, right, bits):
        self.left, self.right, self.bits = left, right, bits
        self.rows = left.shape[1] // 2 ** len(bits)
        self.got = []
        self.total = None

    def place(self, step):
        count = 2 ** len(self.bits)
        return count - (count >> step), max(count >> (step + 1), 1)

    def meets(self, past, step):
        return (self.place(step)[0] - self.place(past + 1)[0]) * self.rows

    def begin(self, *earlier):
        first, size = self.place(0)
        left = after(self.left, *earlier)
        self.held = scatter_part(left, self.right, [], 0, size * self.rows, jnp.bfloat16)
        return self.held

    def send(self, *earlier):
        self.got.append(across(after(self.held, *earlier), self.bits[len(self.got)]))
        return self.got[-1]

    def prepare(self, *earlier):
        step = len(self.got)
        first, size = self.place(step)
        gots = [(got, self.meets(past, step)) for past, got in enumerate(self.got[:-1])]
        left = after(self.left, *earlier)
        self.ready = scatter_part(
            left, self.right, gots, first * self.rows, size * self.rows, jnp.float32
        )
        return self.ready

    def join(self, *earlier):
        step = len(self.got)
        done = step == len(self.bits)
        self.held = join_parts(
            after(self.ready, *earlier),
            self.got[-1],
            self.meets(step - 1, step),
            jnp.float32 if done else jnp.bfloat16,
        )
        if done:
            self.total = self.held
        return self.held

    def finish(self):
        while self.total is None:
            self.send()
            self.prepare()
            self.join()
        return self.total


def local(
    tokens,
    cotangent,
    segment_ids,
    counts,
    mixer_gain,
    query_proj,
    key_value_matrix,
    attend_proj,
    inner_proj,
    state_proj,
    step_proj,
    conv_inner,
    conv_state,
    step_bias,
    decay_log,
    skip_gain,
    gated_gain,
    mamba_proj,
    dense_gain,
    gateup_proj,
    down_proj,
):
    row_count, model_width = tokens.shape
    shard_rows = query_proj.shape[0]
    dp_count = lax.axis_size("dp")
    bf16, f32 = jnp.bfloat16, jnp.float32
    heads_m = step_proj.shape[1]
    heads_q = query_proj.shape[1] // HEAD_DIMENSION
    q_cols = query_proj.shape[1]
    kv_cols = 2 * key_value_matrix.shape[2]
    x_cols = inner_proj.shape[2]
    state_cols = state_proj.shape[1]
    o_cols = attend_proj.shape[0]
    hidden_cols = gateup_proj.shape[2]
    tap_count = conv_state.shape[0]
    pair_width = conv_state.shape[1]

    small = jnp.concatenate(
        [mixer_gain[:, None], dense_gain[:, None], jnp.zeros((mixer_gain.shape[0], 126), bf16)],
        axis=1,
    )
    small = lax.dynamic_update_slice(small, conv_state.T, (0, 2))
    joined = pair_join(jnp.concatenate([state_proj, small], axis=1))
    step_pad = jnp.zeros((shard_rows, 128 - heads_m), bf16)
    group_mix = jnp.concatenate(
        [
            query_proj,
            key_value_matrix.reshape(shard_rows, -1),
            inner_proj.reshape(shard_rows, -1),
            joined[:, :state_cols],
            step_proj,
            step_pad,
            joined[:, state_cols:],
            attend_proj.T,
            mamba_proj.T,
        ],
        axis=1,
    )
    offsets, place = {}, 0
    for name, width in (
        ("q", q_cols),
        ("kv", kv_cols),
        ("z", x_cols),
        ("u", x_cols),
        ("state", state_cols),
        ("step", 128),
        ("end", 0),
    ):
        offsets[name] = place
        place += width
    out_first = offsets["end"] + 128
    group_ffn = jnp.concatenate([gateup_proj.reshape(shard_rows, -1), down_proj.T], axis=1)
    mix_full = lax.all_gather(group_mix, "dp", axis=0, tiled=True)
    ffn_full = lax.all_gather(after(group_ffn, mix_full), "dp", axis=0, tiled=True)
    out_t = mix_full[:, out_first:]
    down_t = ffn_full[:, 2 * hidden_cols :]

    small_full = mix_full[:, offsets["end"] : out_first]
    w_proj = mix_full[:, : offsets["end"]]
    gain_mix = small_full[:, 0].astype(f32)
    gain_dense = small_full[:, 1].astype(f32)
    conv_full = small_full[:, 2 : 2 + tap_count].reshape(
        dp_count, 2, shard_rows // 2, tap_count
    )[:, :, :pair_width]
    conv_full = conv_full.reshape(dp_count * 2 * pair_width, tap_count).T.astype(f32)
    conv_full = jnp.concatenate([conv_full, jnp.zeros((8 - tap_count, state_cols), f32)], axis=0)
    gain_gated = gated_gain.astype(f32)
    wide = jnp.concatenate(
        [
            conv_inner.astype(f32),
            jnp.repeat(skip_gain.astype(f32), HP)[None],
            gain_gated[None],
            jnp.zeros((1, x_cols), f32),
        ],
        axis=0,
    )
    extra = jnp.zeros((8, 128), f32)
    extra = extra.at[0, :heads_m].set(step_bias.astype(f32))
    extra = extra.at[1, :heads_m].set(jnp.exp(decay_log.astype(f32)))

    row_index = jnp.arange(row_count, dtype=jnp.int32)
    valid_rows = (row_index < counts[0]).astype(f32)[:, None]
    live = jnp.broadcast_to(valid_rows, (row_count, 128))
    position = positions_of(segment_ids)
    causal = (row_index[None, :] <= row_index[:, None]) & (
        segment_ids[None, :] == segment_ids[:, None]
    )
    mask = causal.astype(f32)
    mask_t = (
        (row_index[None, :] >= row_index[:, None]) & (segment_ids[None, :] == segment_ids[:, None])
    ).astype(f32)
    mask_qk = (causal & (row_index[None, :] < counts[0])).astype(f32)
    same = jnp.stack(
        [
            jnp.broadcast_to(((row_index >= lag) & (position >= lag)).astype(f32)[:, None], live.shape)
            for lag in range(1, tap_count - 1)
        ]
    )
    half = HEAD_DIMENSION // 2
    frequency = jnp.exp(
        jnp.arange(half, dtype=f32) * (-2.0 * math.log(THETA) / HEAD_DIMENSION)
    )
    angles = position.astype(f32)[:, None] * frequency[None, :]
    cos = jnp.cos(angles)
    sin = jnp.sin(angles)
    cos = jnp.concatenate([cos, cos], axis=1)
    sin = jnp.concatenate([-sin, sin], axis=1)
    bits = bits_of(dp_count)
    order = owner_order(bits)
    stream = tokens.astype(f32)
    upstream = cotangent.astype(f32)
    dense_grad_b = rounded(upstream * valid_rows)
    dense_split = reorder_columns(dense_grad_b, order)

    gain_dense_rows = jnp.broadcast_to(gain_dense[None], (8, model_width))
    gain_mix_rows = jnp.broadcast_to(gain_mix[None], (8, model_width))

    hidden_b = rounded(rms_scale(stream, gain_mix))
    projected = contract("td,dc->tc", hidden_b, w_proj)
    hidden_split = reorder_columns(hidden_b, order)
    mixed, gated, squares = ssm_forward(
        projected, wide, conv_full, extra, live, same, mask, offsets
    )
    own_squares = jnp.sum(squares, axis=-1)
    other_squares = pair_swap(own_squares)
    attended_b, query_b, key_b, value_b, logs = attention_forward(
        projected, cos, sin, mask_qk, offsets, heads_q
    )
    inverse = lax.rsqrt((own_squares + other_squares) / DSSM + EPS)
    normed_b = rounded(gated * inverse[:, None] * gain_gated)
    branch_in = jnp.concatenate([attended_b, normed_b], axis=1)
    branch_own = rounded(contract("tc,dc->td", branch_in, out_t))
    branch_other = pair_swap(branch_own)
    middle, ffn_in_b = rms_forward(tokens, branch_own, branch_other, live, gain_dense_rows)
    activated_b, gate, up = feed_forward(ffn_in_b, ffn_full, 0, hidden_cols)
    inverse_b = jnp.broadcast_to(inverse[:, None], live.shape)
    gated_rows = jnp.broadcast_to(gain_gated[None], (8, x_cols))
    first = (lax.axis_index("tensor") == 0).astype(bf16)
    early_cols = q_cols + kv_cols + x_cols
    column_at = jnp.arange(early_cols) - x_cols
    keep = jnp.where((column_at >= 0) & (column_at < state_cols), first, jnp.ones((), bf16))
    keep = jnp.broadcast_to(keep[None], (8, early_cols))
    down = Scatter(dense_split, activated_b, bits)
    held = down.begin()

    down.send()
    grad_gate_b, grad_up_b, grad_ffn_part = feed_forward_back(
        after(dense_grad_b, held), ffn_full, gate, up, ffn_full, 0
    )
    ready = down.prepare(grad_ffn_part)

    held = down.join(ready)
    down.send()
    grad_ffn_other = pair_swap(after(grad_ffn_part, held))
    gate_sum = Scatter(reorder_columns(ffn_in_b, order), grad_gate_b, bits)
    up_sum = Scatter(gate_sum.left, grad_up_b, bits)
    held = gate_sum.begin(held)
    gate_sum.send()
    held = up_sum.begin(held)
    up_sum.send()
    ready = down.prepare(held)
    dense_own = product_back(after(activated_b, ready), ffn_full, 2 * hidden_cols)
    ready = gate_sum.prepare(dense_own)

    held = gate_sum.join(ready, down.got[-1], up_sum.got[-1], grad_ffn_other)
    gate_sum.send()
    held = down.join(held)
    down.send()
    dense_other = pair_swap(after(dense_own, held))
    grad_middle, grad_dense_gain, mixer_grad_b = rms_back(
        middle, gain_dense_rows, after(grad_ffn_part, held), grad_ffn_other, cotangent, live, True
    )
    grad_normed, own_rows, column_part = norm_back(
        mixer_grad_b, mix_full, out_first + o_cols, gated, inverse_b, gated_rows
    )
    other_rows = pair_swap(own_rows)
    branch = Scatter(reorder_columns(mixer_grad_b, order), branch_in, bits)
    held = branch.begin(own_rows)
    ready = up_sum.prepare(held)
    held = up_sum.join(ready)
    ready = gate_sum.prepare(held)
    grad_attended_b = product(after(mixer_grad_b, ready), mix_full, out_first, o_cols)
    ready = down.prepare(grad_attended_b)
    grad_query_b, grad_key_b, grad_value_b = attention_backward(
        after(grad_attended_b, ready), query_b, key_b, value_b, logs, cos, sin, mask_qk
    )
    ready = grad_query_b

    round_end = (ready, gate_sum.got[-1], down.got[-1], other_rows, dense_other)
    up_sum.send(*round_end)
    branch.send(*round_end)
    held = gate_sum.join(*round_end)
    gate_sum.send()
    held = down.join(held)
    down.send()
    grad_z_b, grad_u_b, grad_state_part, grad_step_b, wide_grad, conv_grad, extra_grad = (
        ssm_backward(
            after(grad_normed, held),
            mixed,
            projected,
            inverse_b,
            own_rows,
            other_rows,
            wide,
            conv_full,
            extra,
            live,
            same,
            mask_t,
            offsets,
        )
    )
    ready = up_sum.prepare(grad_state_part)
    ready = gate_sum.prepare(ready)
    grad_z_b = after(grad_z_b, ready)
    early_b = beside(early_cols, grad_query_b, grad_key_b, grad_value_b, grad_z_b)
    early = Scatter(hidden_split, early_b, bits)
    held = early.begin()
    ready = branch.prepare(held)
    ready = down.prepare(ready)

    round_end = (ready, up_sum.got[-1], gate_sum.got[-1], down.got[-1], branch.got[-1])
    held = branch.join(*round_end)
    branch.send()
    early.send(*round_end)
    grad_state_other = pair_swap(after(grad_state_part, *round_end))
    held = up_sum.join(held)
    up_sum.send()
    held = gate_sum.join(held)
    gate_sum.send()
    held = down.join(held)
    late_b = beside(
        early_cols, grad_u_b, (grad_state_part, after(grad_state_other, held)), grad_step_b
    )
    late = Scatter(hidden_split, late_b, bits)
    held = late.begin()
    ready = early.prepare(held)
    ready = branch.prepare(ready)
    ready = up_sum.prepare(ready)
    ready = gate_sum.prepare(ready)

    round_end = (ready, branch.got[-1], up_sum.got[-1], gate_sum.got[-1], early.got[-1])
    held = early.join(*round_end)
    early.send()
    late.send(*round_end)
    held = branch.join(held)
    branch.send()
    held = up_sum.join(held)
    up_sum.send()
    held = gate_sum.join(held)
    grad_hidden_own = hidden_back(after(early_b, held), late_b, keep, mix_full)
    ready = late.prepare(grad_hidden_own)
    ready = early.prepare(ready)
    ready = branch.prepare(ready)
    ready = up_sum.prepare(ready)

    round_end = (ready, early.got[-1], branch.got[-1], up_sum.got[-1], late.got[-1])
    held = late.join(*round_end)
    late.send()
    grad_hidden_other = pair_swap(after(grad_hidden_own, *round_end))
    held = early.join(held)
    early.send()
    held = branch.join(held)
    branch.send()
    held = up_sum.join(held)
    output = output_rows(middle, after(dense_own, held), dense_other, live)
    ready = late.prepare(output)
    ready = early.prepare(ready)
    ready = branch.prepare(ready)

    round_end = (ready, late.got[-1], early.got[-1], branch.got[-1], grad_hidden_other)
    held = late.join(*round_end)
    late.send()
    held = early.join(held)
    early.send()
    grad_tokens, grad_mixer_gain = rms_back(
        tokens, gain_mix_rows, after(grad_hidden_own, held), grad_hidden_other, grad_middle, live, False
    )
    own_sums = stack_rows(
        model_width,
        (grad_mixer_gain, 1),
        (grad_dense_gain, 1),
        (wide_grad, tap_count + 1),
        (column_part, 1),
        (conv_grad, tap_count),
        (extra_grad, 2),
    )
    sums = own_sums + across(own_sums, bits[0])
    held = branch.join(sums)
    ready = late.prepare(held)
    ready = early.prepare(ready)
    others = across(after(sums, ready), bits[1])

    held = late.join(ready, early.got[-1], others)
    late.send()
    sums = after(sums, held) + others
    for bit in bits[2:]:
        sums = sums + across(sums, bit)
    held = early.join(sums)
    late.prepare(held)
    late.join()
    at = 2 + tap_count + 2
    conv_sum = sums[at : at + tap_count, :state_cols]
    conv_sum = conv_sum + pair_swap(conv_sum)
    at += tap_count
    skip_sum = jnp.sum(sums[2 + tap_count, :x_cols].reshape(heads_m, HP), axis=1)
    owner = lax.axis_index("dp") * 2 + lax.axis_index("tensor")

    def own_part(values, axis_dim):
        width = values.shape[axis_dim] // (2 * dp_count)
        return lax.dynamic_slice_in_dim(values, owner * width, width, axis_dim)

    red_early, red_late, red_branch = early.finish(), late.finish(), branch.finish()
    state_rows = shard_rows // 2
    red_state = lax.dynamic_slice_in_dim(
        red_late[:, x_cols : x_cols + state_cols],
        lax.axis_index("tensor") * state_rows,
        state_rows,
        0,
    )
    return (
        output,
        grad_tokens,
        own_part(sums[0], 0),
        red_early[:, :q_cols],
        red_early[:, q_cols : q_cols + kv_cols].reshape(shard_rows, 2, -1),
        red_branch[:, :o_cols].T,
        jnp.stack([red_early[:, q_cols + kv_cols :], red_late[:, :x_cols]], axis=1),
        red_state,
        red_late[:, x_cols + state_cols : x_cols + state_cols + heads_m],
        sums[2 : 2 + tap_count, :x_cols],
        own_part(conv_sum, 1),
        sums[at, :heads_m],
        sums[at + 1, :heads_m],
        skip_sum,
        sums[3 + tap_count, :x_cols],
        red_branch[:, o_cols:].T,
        own_part(sums[1], 0),
        jnp.stack([gate_sum.finish(), up_sum.finish()], axis=1),
        down.finish().T,
    )


def solution(mesh):
    placed = (
        P("dp", None),
        P("dp", None),
        P("dp"),
        P("dp"),
        P(("dp", "tensor")),
        P("dp", "tensor"),
        P("dp", None, "tensor"),
        P("tensor", "dp"),
        P("dp", None, "tensor"),
        P(("dp", "tensor"), None),
        P("dp", "tensor"),
        P(None, "tensor"),
        P(None, ("dp", "tensor")),
        P("tensor"),
        P("tensor"),
        P("tensor"),
        P("tensor"),
        P("tensor", "dp"),
        P(("dp", "tensor")),
        P("dp", None, "tensor"),
        P("tensor", "dp"),
    )
    return jax.shard_map(
        local,
        mesh=mesh,
        in_specs=placed,
        out_specs=(
            P("dp", None),
            P("dp", None),
            P(("dp", "tensor")),
            P("dp", "tensor"),
            P("dp", None, "tensor"),
            P("tensor", "dp"),
            P("dp", None, "tensor"),
            P(("dp", "tensor"), None),
            P("dp", "tensor"),
            P(None, "tensor"),
            P(None, ("dp", "tensor")),
            P("tensor"),
            P("tensor"),
            P("tensor"),
            P("tensor"),
            P("tensor", "dp"),
            P(("dp", "tensor")),
            P("dp", None, "tensor"),
            P("tensor", "dp"),
        ),
        check_vma=False,
    )
```

```python
import functools
import math

import jax
import jax.numpy as jnp
from jax import lax
from jax.experimental import pallas as pl
from jax.experimental.pallas import tpu as pltpu
from jax.sharding import PartitionSpec as P

HP = 64
HEAD_DIMENSION = 128
DSSM = 3072
TILE = 256

EPS = 1e-05
THETA = 100000000000.0


def rounded(values):
    return values.astype(jnp.bfloat16)


def contract(form, left, right):
    return jnp.einsum(form, left, right, preferred_element_type=jnp.float32)


def rms_scale(values, gain):
    return values * lax.rsqrt(jnp.mean(values * values, axis=-1, keepdims=True) + EPS) * gain


def cost(flops, traffic, transcendentals=0):
    return pl.CostEstimate(
        flops=flops, bytes_accessed=traffic, transcendentals=transcendentals
    )


def positions_of(segment):
    row_index = jnp.arange(segment.shape[0], dtype=jnp.int32)
    starts = jnp.concatenate([jnp.ones((1,), jnp.bool_), segment[1:] != segment[:-1]])
    first_row = lax.cummax(jnp.where(starts, row_index, 0), axis=0)
    return row_index - first_row


def silu_parts(values):
    gate = jax.nn.sigmoid(values)
    return values * gate, gate * (1.0 + values * (1.0 - gate))


def dot_nn(left, right):
    return lax.dot_general(left, right, (((1,), (0,)), ((), ())), preferred_element_type=jnp.float32)


def dot_nt(left, right):
    return lax.dot_general(left, right, (((1,), (1,)), ((), ())), preferred_element_type=jnp.float32)


def dot_tn(left, right):
    return lax.dot_general(left, right, (((0,), (0,)), ((), ())), preferred_element_type=jnp.float32)


def shifted_rows(values, lag, same_ref):
    columns = values.shape[1]
    mask = same_ref[lag - 1]
    if columns > mask.shape[1]:
        mask = jnp.concatenate([mask] * (columns // mask.shape[1]), axis=1)
    return mask * pltpu.roll(values, lag, 0)


def conv_rows(values, taps, same_ref):
    total = taps[4:5] + taps[3:4] * values
    for lag in range(1, 4):
        total = total + taps[3 - lag : 4 - lag] * shifted_rows(values, lag, same_ref)
    return total


def conv_rows_back(grad, values, taps, same_ref):
    rows = grad.shape[0]
    total = taps[3:4] * grad
    tap_grads = [None] * 5
    tap_grads[4] = jnp.sum(grad, axis=0, keepdims=True)
    tap_grads[3] = jnp.sum(grad * values, axis=0, keepdims=True)
    for lag in range(1, 4):
        mask = same_ref[lag - 1]
        if grad.shape[1] > mask.shape[1]:
            mask = jnp.concatenate([mask] * (grad.shape[1] // mask.shape[1]), axis=1)
        masked = grad * mask
        total = total + taps[3 - lag : 4 - lag] * pltpu.roll(masked, rows - lag, 0)
        tap_grads[3 - lag] = jnp.sum(
            masked * pltpu.roll(values, lag, 0), axis=0, keepdims=True
        )
    return total, tap_grads


def running_sum(values, backward=False):
    rows = values.shape[0]
    index = lax.broadcasted_iota(jnp.int32, values.shape, 0)
    step = 1
    while step < rows:
        if backward:
            moved = pltpu.roll(values, rows - step, 0)
            values = values + jnp.where(index < rows - step, moved, 0.0)
        else:
            moved = pltpu.roll(values, step, 0)
            values = values + jnp.where(index >= step, moved, 0.0)
        step *= 2
    return values


def step_sizes(raw, extra_ref, live):
    shifted = raw + extra_ref[0:1]
    size = (jnp.maximum(shifted, 0.0) + jnp.log1p(jnp.exp(-jnp.abs(shifted)))) * live
    return shifted, size, -size * extra_ref[1:2]


def lane_column(values, lane):
    lanes = lax.broadcasted_iota(jnp.int32, values.shape, 1)
    return jnp.sum(jnp.where(lanes == lane, values, 0.0), axis=1, keepdims=True)


def ssm_forward_kernel(
    u_ref, z_ref, state_b_ref, state_c_ref, step_ref, wide_ref, conv_ref, extra_ref, live_ref, same_ref, mask_ref,
    y_ref, gated_ref, square_ref, gram, sizes, running, running_t,
):
    step = pl.program_id(0)
    live = live_ref[...]
    rows = live.shape[0]

    @pl.when(step == 0)
    def _():
        unused, size, decay = step_sizes(step_ref[...], extra_ref, live)
        total = running_sum(decay)
        sizes[...] = size
        running[...] = total
        running_t[...] = total.T
        width = conv_ref.shape[1]
        wide_live = jnp.concatenate([live] * (width // 128), axis=1)
        state = jnp.concatenate([state_b_ref[...], state_c_ref[...]], axis=1) * wide_live
        inner = conv_rows(state, conv_ref[...], same_ref)
        both = (inner * jax.nn.sigmoid(inner)).astype(jnp.bfloat16)
        gram[...] = dot_nt(both[:, width // 2 :], both[:, : width // 2]) * mask_ref[...]
        square_ref[...] = jnp.zeros_like(square_ref)

    for part in range(2):
        pair = 2 * step + part
        at = slice(part * 128, (part + 1) * 128)
        taps = wide_ref[:, at]
        inner = conv_rows(u_ref[:, at] * live, taps, same_ref)
        x_in = inner * jax.nn.sigmoid(inner)
        left_lanes = lax.broadcasted_iota(jnp.int32, (rows, 128), 1) < HP
        size = sizes[...]
        size_pair = jnp.where(left_lanes, lane_column(size, 2 * pair), lane_column(size, 2 * pair + 1))
        inflow = (size_pair * x_in).astype(jnp.bfloat16)
        total = running[...]
        columns = [lane_column(total, 2 * pair + k) for k in range(2)]
        row_vectors = [running_t[pl.ds(2 * pair + k, 1), :] for k in range(2)]
        skipped = taps[5:6] * x_in
        gate = z_ref[:, at]
        gate = gate * jax.nn.sigmoid(gate)
        for block in range(rows // TILE):
            top, end = block * TILE, (block + 1) * TILE
            parts = []
            for k in range(2):
                gaps = columns[k][top:end] - row_vectors[k][:, :end]
                mixing = (gram[top:end, :end] * jnp.exp(jnp.minimum(gaps, 0.0))).astype(jnp.bfloat16)
                parts.append(dot_nn(mixing, inflow[:end]))
            mixed = jnp.where(left_lanes[top:end], parts[0], parts[1]) + skipped[top:end]
            y_ref[top:end, at] = mixed
            gated = mixed * gate[top:end]
            gated_ref[top:end, at] = gated
            square_ref[top:end, :] += gated * gated


def ssm_forward(projected, wide, conv_state, extra, live, same, mask, offsets):
    rows = projected.shape[0]
    pairs = wide.shape[1] // 128
    width = conv_state.shape[1]
    const2 = lambda i: (0, 0)
    at = lambda name, size: offsets[name] // size
    block = lambda name: pl.BlockSpec((rows, 128 * 2), lambda i, o=at(name, 128 * 2): (0, o + i))
    return pl.pallas_call(
        ssm_forward_kernel,
        grid=(pairs // 2,),
        in_specs=[
            block("u"),
            block("z"),
            pl.BlockSpec((rows, width // 2), lambda i: (0, at("state", width // 2))),
            pl.BlockSpec((rows, width // 2), lambda i: (0, at("state", width // 2) + 1)),
            pl.BlockSpec((rows, 128), lambda i: (0, at("step", 128))),
            pl.BlockSpec((8, 128 * 2), lambda i: (0, i)),
            pl.BlockSpec((8, width), const2),
            pl.BlockSpec((8, 128), const2),
            pl.BlockSpec((rows, 128), const2),
            pl.BlockSpec((3, rows, 128), lambda i: (0, 0, 0)),
            pl.BlockSpec((rows, rows), const2),
        ],
        out_specs=[
            pl.BlockSpec((rows, 128 * 2), lambda i: (0, i)),
            pl.BlockSpec((rows, 128 * 2), lambda i: (0, i)),
            pl.BlockSpec((rows, 128), const2),
        ],
        out_shape=[
            jax.ShapeDtypeStruct((rows, pairs * 128), jnp.float32),
            jax.ShapeDtypeStruct((rows, pairs * 128), jnp.float32),
            jax.ShapeDtypeStruct((rows, 128), jnp.float32),
        ],
        scratch_shapes=[
            pltpu.VMEM((rows, rows), jnp.float32),
            pltpu.VMEM((rows, 128), jnp.float32),
            pltpu.VMEM((rows, 128), jnp.float32),
            pltpu.VMEM((128, rows), jnp.float32),
        ],
        compiler_params=pltpu.CompilerParams(vmem_limit_bytes=28 * 2**20),
        name="ssm_forward",
    )(projected, projected, projected, projected, projected, wide, conv_state, extra, live, same, mask)


def ssm_backward_kernel(
    dn_ref, y_ref, u_ref, z_ref, state_b_ref, state_c_ref, step_ref, inverse_ref, own_ref, other_ref,
    wide_ref, conv_ref, extra_ref, live_ref, same_ref, mask_t_ref,
    dz_ref, du_ref, ds_ref, dr_ref, wide_grad_ref, conv_grad_ref, extra_grad_ref,
    gram_t, gram_grad, sizes, decays, running, running_t, size_grad, total_grad, states, state_slopes,
):
    step = pl.program_id(0)
    live = live_ref[...]
    rows = live.shape[0]
    width = conv_ref.shape[1]
    wide_live = jnp.concatenate([live] * (width // 128), axis=1)

    @pl.when(step == 0)
    def _():
        unused, size, decay = step_sizes(step_ref[...], extra_ref, live)
        total = running_sum(decay)
        sizes[...] = size
        decays[...] = decay
        running[...] = total
        running_t[...] = total.T
        state = jnp.concatenate([state_b_ref[...], state_c_ref[...]], axis=1) * wide_live
        inner = conv_rows(state, conv_ref[...], same_ref)
        value, slope = silu_parts(inner)
        both = value.astype(jnp.bfloat16)
        states[...] = both
        state_slopes[...] = slope
        gram_t[...] = dot_nt(both[:, : width // 2], both[:, width // 2 :]) * mask_t_ref[...]
        gram_grad[...] = jnp.zeros_like(gram_grad)
        size_grad[...] = jnp.zeros_like(size_grad)
        total_grad[...] = jnp.zeros_like(total_grad)

    for part in range(2):
        pair = 2 * step + part
        at = slice(part * 128, (part + 1) * 128)
        taps = wide_ref[:, at]
        u_live = u_ref[:, at] * live
        inner = conv_rows(u_live, taps, same_ref)
        x_in, x_slope = silu_parts(inner)
        gate, gate_slope = silu_parts(z_ref[:, at])
        mixed = y_ref[:, at]
        gated = mixed * gate
        inverse = inverse_ref[:, 0:1]
        pull = (own_ref[:, 0:1] + other_ref[:, 0:1]) * inverse * inverse * inverse / DSSM
        grad_gated = taps[6:7] * dn_ref[:, at] * inverse - gated * pull
        grad_mixed = grad_gated * gate
        dz_ref[:, at] = (grad_gated * mixed * gate_slope).astype(dz_ref.dtype)
        grad_mixed_b = grad_mixed.astype(jnp.bfloat16)
        lanes = lax.broadcasted_iota(jnp.int32, (rows, 128), 1)
        left_lanes = lanes < HP
        size = sizes[...]
        size_pair = jnp.where(left_lanes, lane_column(size, 2 * pair), lane_column(size, 2 * pair + 1))
        inflow = (size_pair * x_in).astype(jnp.bfloat16)
        zero = jnp.zeros_like(inflow)
        inflow_heads = [jnp.where(left_lanes, inflow, zero), jnp.where(left_lanes, zero, inflow)]
        total = running[...]
        columns = [lane_column(total, 2 * pair + k) for k in range(2)]
        row_vectors = [running_t[pl.ds(2 * pair + k, 1), :] for k in range(2)]
        blocks = []
        for block in range(rows // TILE):
            top, end = block * TILE, (block + 1) * TILE
            parts = []
            gram_part = None
            for k in range(2):
                gaps = row_vectors[k][:, top:] - columns[k][top:end]
                decay = jnp.exp(jnp.minimum(gaps, 0.0))
                mixing_t = (gram_t[top:end, top:] * decay).astype(jnp.bfloat16)
                parts.append(dot_nn(mixing_t, grad_mixed_b[top:]))
                term = dot_nt(inflow_heads[k][top:end], grad_mixed_b[top:]) * decay
                gram_part = term if gram_part is None else gram_part + term
            gram_grad[top:end, top:] += gram_part
            blocks.append(jnp.where(left_lanes[top:end], parts[0], parts[1]))
        grad_inflow = jnp.concatenate(blocks, axis=0)
        grad_x = grad_mixed * taps[5:6] + grad_inflow * size_pair
        by_size = grad_inflow * x_in
        mixed_only = mixed - taps[5:6] * x_in
        by_total = grad_mixed_b.astype(jnp.float32) * mixed_only - grad_inflow * inflow.astype(jnp.float32)
        size_sum, total_sum = size_grad[...], total_grad[...]
        for k in range(2):
            mine = left_lanes if k == 0 else jnp.logical_not(left_lanes)
            here = lanes == 2 * pair + k
            size_sum = jnp.where(
                here, jnp.sum(jnp.where(mine, by_size, 0.0), axis=1, keepdims=True), size_sum
            )
            total_sum = jnp.where(
                here, jnp.sum(jnp.where(mine, by_total, 0.0), axis=1, keepdims=True), total_sum
            )
        size_grad[...] = size_sum
        total_grad[...] = total_sum
        grad_u, tap_grads = conv_rows_back(grad_x * x_slope, u_live, taps, same_ref)
        du_ref[:, at] = (grad_u * live).astype(du_ref.dtype)
        skip_grad = jnp.sum(grad_mixed * x_in, axis=0, keepdims=True)
        wide_grad_ref[:, at] = jnp.concatenate(
            tap_grads + [skip_grad, jnp.zeros((2, 128), jnp.float32)], axis=0
        )

    @pl.when(step == pl.num_programs(0) - 1)
    def _():
        half = width // 2
        gram_grad_b = (gram_grad[...] * mask_t_ref[...]).astype(jnp.bfloat16)
        grad_b = dot_nn(gram_grad_b, states[:, half:])
        grad_c = dot_tn(gram_grad_b, states[:, :half])
        grad_bc = jnp.concatenate([grad_b, grad_c], axis=1) * state_slopes[...]
        state = jnp.concatenate([state_b_ref[...], state_c_ref[...]], axis=1) * wide_live
        grad_in, state_taps = conv_rows_back(grad_bc, state, conv_ref[...], same_ref)
        ds_ref[...] = (grad_in * wide_live).astype(ds_ref.dtype)
        conv_grad_ref[...] = jnp.concatenate(
            state_taps + [jnp.zeros((3, width), jnp.float32)], axis=0
        )
        decay_grad = running_sum(total_grad[...], backward=True)
        shifted = step_ref[...] + extra_ref[0:1]
        grad_size = size_grad[...] - decay_grad * extra_ref[1:2]
        grad_raw = grad_size * live * jax.nn.sigmoid(shifted)
        dr_ref[...] = grad_raw.astype(dr_ref.dtype)
        extra_grad_ref[...] = jnp.concatenate(
            [
                jnp.sum(grad_raw, axis=0, keepdims=True),
                jnp.sum(decay_grad * decays[...], axis=0, keepdims=True),
                jnp.zeros((6, 128), jnp.float32),
            ],
            axis=0,
        )


def ssm_backward(
    grad_normed, mixed, projected, inverse, own, other, wide, conv_state, extra, live, same, mask_t, offsets
):
    rows = projected.shape[0]
    pairs = wide.shape[1] // 128
    width = conv_state.shape[1]
    const2 = lambda i: (0, 0)
    at = lambda name, size: offsets[name] // size
    block = lambda name: pl.BlockSpec((rows, 128 * 2), lambda i, o=at(name, 128 * 2): (0, o + i))
    plain = pl.BlockSpec((rows, 128 * 2), lambda i: (0, i))
    f32, b16 = jnp.float32, jnp.bfloat16
    return pl.pallas_call(
        ssm_backward_kernel,
        grid=(pairs // 2,),
        in_specs=[
            plain,
            plain,
            block("u"),
            block("z"),
            pl.BlockSpec((rows, width // 2), lambda i: (0, at("state", width // 2))),
            pl.BlockSpec((rows, width // 2), lambda i: (0, at("state", width // 2) + 1)),
            pl.BlockSpec((rows, 128), lambda i: (0, at("step", 128))),
            pl.BlockSpec((rows, 128), const2),
            pl.BlockSpec((rows, 128), const2),
            pl.BlockSpec((rows, 128), const2),
            pl.BlockSpec((8, 128 * 2), lambda i: (0, i)),
            pl.BlockSpec((8, width), const2),
            pl.BlockSpec((8, 128), const2),
            pl.BlockSpec((rows, 128), const2),
            pl.BlockSpec((3, rows, 128), lambda i: (0, 0, 0)),
            pl.BlockSpec((rows, rows), const2),
        ],
        out_specs=[
            plain,
            plain,
            pl.BlockSpec((rows, width), const2),
            pl.BlockSpec((rows, 128), const2),
            pl.BlockSpec((8, 128 * 2), lambda i: (0, i)),
            pl.BlockSpec((8, width), const2),
            pl.BlockSpec((8, 128), const2),
        ],
        out_shape=[
            jax.ShapeDtypeStruct((rows, pairs * 128), b16),
            jax.ShapeDtypeStruct((rows, pairs * 128), b16),
            jax.ShapeDtypeStruct((rows, width), b16),
            jax.ShapeDtypeStruct((rows, 128), b16),
            jax.ShapeDtypeStruct((8, pairs * 128), f32),
            jax.ShapeDtypeStruct((8, width), f32),
            jax.ShapeDtypeStruct((8, 128), f32),
        ],
        scratch_shapes=[
            pltpu.VMEM((rows, rows), f32),
            pltpu.VMEM((rows, rows), f32),
            pltpu.VMEM((rows, 128), f32),
            pltpu.VMEM((rows, 128), f32),
            pltpu.VMEM((rows, 128), f32),
            pltpu.VMEM((128, rows), f32),
            pltpu.VMEM((rows, 128), f32),
            pltpu.VMEM((rows, 128), f32),
            pltpu.VMEM((rows, width), b16),
            pltpu.VMEM((rows, width), f32),
        ],
        compiler_params=pltpu.CompilerParams(vmem_limit_bytes=32 * 2**20),
        cost_estimate=cost(1, 1),
        name="ssm_backward",
    )(
        grad_normed, mixed, projected, projected, projected, projected, projected, inverse, own, other,
        wide, conv_state, extra, live, same, mask_t,
    )


def turned(values, cos_ref, sin_ref):
    return values * cos_ref[...] + pltpu.roll(values, HEAD_DIMENSION // 2, 1) * sin_ref[...]


def attention_forward_kernel(
    q_ref, k_ref, v_ref, cos_ref, sin_ref, mask_ref, out_ref, query_ref, key_ref, value_ref, log_ref
):
    head = pl.program_id(0)
    rows = q_ref.shape[0]
    scale = HEAD_DIMENSION**-0.5

    @pl.when(head == 0)
    def _():
        key_ref[...] = turned(k_ref[...], cos_ref, sin_ref).astype(jnp.bfloat16)
        value_ref[...] = v_ref[...].astype(jnp.bfloat16)

    query = turned(q_ref[...], cos_ref, sin_ref).astype(jnp.bfloat16)
    query_ref[...] = query
    for block in range(rows // TILE):
        top, end = block * TILE, (block + 1) * TILE
        scores = dot_nt(query[top:end], key_ref[:end, :]) * scale
        scores = jnp.where(mask_ref[top:end, :end] > 0.0, scores, -1e30)
        largest = jnp.max(scores, axis=1, keepdims=True)
        weights = jnp.exp(scores - largest)
        total = jnp.sum(weights, axis=1, keepdims=True)
        probs = (weights / total).astype(jnp.bfloat16)
        out_ref[top:end, :] = dot_nn(probs, value_ref[:end, :]).astype(out_ref.dtype)
        log_ref[top:end, :] = jnp.broadcast_to(largest + jnp.log(total), (TILE, 128))


def attention_forward(projected, cos, sin, mask, offsets, heads):
    rows = projected.shape[0]
    at = lambda name: offsets[name] // 128
    const2 = lambda i: (0, 0)
    one = pl.BlockSpec((rows, 128), const2)
    each = pl.BlockSpec((rows, 128), lambda i: (0, i))
    b16 = jnp.bfloat16
    return pl.pallas_call(
        attention_forward_kernel,
        grid=(heads,),
        in_specs=[
            pl.BlockSpec((rows, 128), lambda i: (0, at("q") + i)),
            pl.BlockSpec((rows, 128), lambda i: (0, at("kv"))),
            pl.BlockSpec((rows, 128), lambda i: (0, at("kv") + 1)),
            one,
            one,
            pl.BlockSpec((rows, rows), const2),
        ],
        out_specs=[each, each, one, one, each],
        out_shape=[
            jax.ShapeDtypeStruct((rows, heads * 128), b16),
            jax.ShapeDtypeStruct((rows, heads * 128), b16),
            jax.ShapeDtypeStruct((rows, 128), b16),
            jax.ShapeDtypeStruct((rows, 128), b16),
            jax.ShapeDtypeStruct((rows, heads * 128), jnp.float32),
        ],
        compiler_params=pltpu.CompilerParams(vmem_limit_bytes=24 * 2**20),
        name="attention_forward",
    )(projected, projected, projected, cos, sin, mask)


def attention_backward_kernel(
    grad_ref, query_ref, key_ref, value_ref, log_ref, cos_ref, sin_ref, mask_ref,
    dq_ref, dk_ref, dv_ref, key_sum, value_sum,
):
    head = pl.program_id(0)
    rows = query_ref.shape[0]
    scale = HEAD_DIMENSION**-0.5

    @pl.when(head == 0)
    def _():
        key_sum[...] = jnp.zeros_like(key_sum)
        value_sum[...] = jnp.zeros_like(value_sum)

    for block in range(rows // TILE):
        top, end = block * TILE, (block + 1) * TILE
        query = query_ref[top:end, :]
        grad = grad_ref[top:end, :]
        scores = dot_nt(query, key_ref[:end, :]) * scale
        scores = jnp.where(mask_ref[top:end, :end] > 0.0, scores, -1e30)
        probs = jnp.exp(scores - log_ref[top:end, 0:1])
        grad_probs = dot_nt(grad, value_ref[:end, :])
        inner = jnp.sum(grad_probs * probs, axis=1, keepdims=True)
        grad_scores = (probs * (grad_probs - inner)).astype(jnp.bfloat16)
        dq = dot_nn(grad_scores, key_ref[:end, :]) * scale
        dq_ref[top:end, :] = (
            dq * cos_ref[top:end, :]
            - pltpu.roll(dq, HEAD_DIMENSION // 2, 1) * sin_ref[top:end, :]
        ).astype(dq_ref.dtype)
        key_sum[:end, :] += dot_tn(grad_scores, query)
        value_sum[:end, :] += dot_tn(probs.astype(jnp.bfloat16), grad)

    @pl.when(head == pl.num_programs(0) - 1)
    def _():
        dk = key_sum[...] * scale
        dk_ref[...] = (
            dk * cos_ref[...] - pltpu.roll(dk, HEAD_DIMENSION // 2, 1) * sin_ref[...]
        ).astype(dk_ref.dtype)
        dv_ref[...] = value_sum[...].astype(dv_ref.dtype)


def attention_backward(grad, query, key, value, logs, cos, sin, mask):
    rows = query.shape[0]
    heads = query.shape[1] // 128
    const2 = lambda i: (0, 0)
    one = pl.BlockSpec((rows, 128), const2)
    each = pl.BlockSpec((rows, 128), lambda i: (0, i))
    b16 = jnp.bfloat16
    return pl.pallas_call(
        attention_backward_kernel,
        grid=(heads,),
        in_specs=[each, each, one, one, each, one, one, pl.BlockSpec((rows, rows), const2)],
        out_specs=[each, one, one],
        out_shape=[
            jax.ShapeDtypeStruct((rows, heads * 128), b16),
            jax.ShapeDtypeStruct((rows, 128), b16),
            jax.ShapeDtypeStruct((rows, 128), b16),
        ],
        scratch_shapes=[pltpu.VMEM((rows, 128), jnp.float32), pltpu.VMEM((rows, 128), jnp.float32)],
        compiler_params=pltpu.CompilerParams(vmem_limit_bytes=24 * 2**20),
        cost_estimate=cost(1, 1),
        name="attention_backward",
    )(grad, query, key, value, logs, cos, sin, mask)


def feed_forward_kernel(
    in_ref, grad_ref, gate_w_ref, up_w_ref, down_ref, act_ref, dgate_ref, dup_ref, din_ref, total
):
    step = pl.program_id(0)

    @pl.when(step == 0)
    def _():
        total[...] = jnp.zeros_like(total)

    gate = dot_nn(in_ref[...], gate_w_ref[...])
    up = dot_nn(in_ref[...], up_w_ref[...])
    grad_act = dot_nn(grad_ref[...], down_ref[...])
    value, slope = silu_parts(gate)
    act_ref[...] = (value * up).astype(act_ref.dtype)
    dgate = (grad_act * up * slope).astype(jnp.bfloat16)
    dup = (grad_act * value).astype(jnp.bfloat16)
    dgate_ref[...] = dgate
    dup_ref[...] = dup
    total[...] += dot_nt(dgate, gate_w_ref[...]) + dot_nt(dup, up_w_ref[...])

    @pl.when(step == pl.num_programs(0) - 1)
    def _():
        din_ref[...] = total[...].astype(din_ref.dtype)


def feed_forward(ffn_in, grad, weights, hidden, tile=512):
    rows, model = grad.shape
    steps = hidden // tile
    each = pl.BlockSpec((rows, tile), lambda i: (0, i))
    whole = pl.BlockSpec((rows, model), lambda i: (0, 0))
    b16 = jnp.bfloat16
    return pl.pallas_call(
        feed_forward_kernel,
        grid=(steps,),
        in_specs=[
            whole,
            whole,
            pl.BlockSpec((model, tile), lambda i: (0, i)),
            pl.BlockSpec((model, tile), lambda i: (0, steps + i)),
            pl.BlockSpec((model, tile), lambda i: (0, 2 * steps + i)),
        ],
        out_specs=[each, each, each, whole],
        out_shape=[
            jax.ShapeDtypeStruct((rows, hidden), b16),
            jax.ShapeDtypeStruct((rows, hidden), b16),
            jax.ShapeDtypeStruct((rows, hidden), b16),
            jax.ShapeDtypeStruct((rows, model), b16),
        ],
        scratch_shapes=[pltpu.VMEM((rows, model), jnp.float32)],
        compiler_params=pltpu.CompilerParams(vmem_limit_bytes=44 * 2**20),
        cost_estimate=cost(1, 1),
        name="feed_forward",
    )(ffn_in, grad, weights, weights, weights)


def norm_back_kernel(
    grad_ref, weight_ref, gated_ref, inverse_ref, gain_ref, dout_ref, dn_ref, row_ref, column_ref, *, split
):
    step = pl.program_id(0)

    @pl.when(step == 0)
    def _():
        row_ref[...] = jnp.zeros_like(row_ref)

    grad = dot_nn(grad_ref[...], weight_ref[...])

    @pl.when(step < split)
    def _():
        dout_ref[...] = grad.astype(dout_ref.dtype)

    @pl.when(step >= split)
    def _():
        dn_ref[...] = grad
        product = grad * gated_ref[...]
        scaled = product * gain_ref[0:1]
        part = scaled[:, :128]
        for k in range(1, scaled.shape[1] // 128):
            part = part + scaled[:, k * 128 : (k + 1) * 128]
        row_ref[...] += part
        total = jnp.sum(product * inverse_ref[:, 0:1], axis=0, keepdims=True)
        column_ref[...] = jnp.broadcast_to(total, column_ref.shape)

    @pl.when(step == pl.num_programs(0) - 1)
    def _():
        row_ref[...] = jnp.broadcast_to(
            jnp.sum(row_ref[...], axis=1, keepdims=True), row_ref.shape
        )


def norm_back(grad, weights, first, attended, gated, inverse, gains, tile=512):
    rows, model = grad.shape
    width = gated.shape[1]
    split = attended // tile
    later = lambda i: (0, jnp.maximum(i - split, 0))
    f32 = jnp.float32
    return pl.pallas_call(
        functools.partial(norm_back_kernel, split=split),
        grid=((attended + width) // tile,),
        in_specs=[
            pl.BlockSpec((rows, model), lambda i: (0, 0)),
            pl.BlockSpec((model, tile), lambda i: (0, first // tile + i)),
            pl.BlockSpec((rows, tile), later),
            pl.BlockSpec((rows, 128), lambda i: (0, 0)),
            pl.BlockSpec((8, tile), later),
        ],
        out_specs=[
            pl.BlockSpec((rows, tile), lambda i: (0, jnp.minimum(i, split - 1))),
            pl.BlockSpec((rows, tile), later),
            pl.BlockSpec((rows, 128), lambda i: (0, 0)),
            pl.BlockSpec((8, tile), later),
        ],
        out_shape=[
            jax.ShapeDtypeStruct((rows, attended), jnp.bfloat16),
            jax.ShapeDtypeStruct((rows, width), f32),
            jax.ShapeDtypeStruct((rows, 128), f32),
            jax.ShapeDtypeStruct((8, width), f32),
        ],
        compiler_params=pltpu.CompilerParams(vmem_limit_bytes=40 * 2**20),
        cost_estimate=cost(1, 1),
        name="norm_back",
    )(grad, weights, gated, inverse, gains)


def reorder_kernel(order_ref, in_ref, out_ref):
    width = in_ref.shape[1] // order_ref.shape[0]
    for place in range(order_ref.shape[0]):
        column = pl.multiple_of(order_ref[place] * width, width)
        out_ref[:, place * width : (place + 1) * width] = in_ref[:, pl.ds(column, width)]


def reorder_columns(values, order):
    rows, model = values.shape
    count = order.shape[0]
    width = model // count
    if width % 128:
        return jnp.take(values.reshape(rows, count, width), order, axis=1).reshape(rows, model)
    return pl.pallas_call(
        reorder_kernel,
        in_specs=[
            pl.BlockSpec(memory_space=pltpu.SMEM),
            pl.BlockSpec(memory_space=pltpu.VMEM),
        ],
        out_specs=pl.BlockSpec(memory_space=pltpu.VMEM),
        out_shape=jax.ShapeDtypeStruct(values.shape, values.dtype),
        compiler_params=pltpu.CompilerParams(vmem_limit_bytes=8 * 2**20),
        cost_estimate=cost(1, 1),
        name="reorder_columns",
    )(order, values)


def scatter_part_kernel(left_ref, right_ref, *refs):
    got_refs, out_ref, turned_left = refs[:-2], refs[-2], refs[-1]

    @pl.when(pl.program_id(0) == 0)
    def _():
        turned_left[...] = left_ref[...].T

    total = dot_nn(turned_left[...], right_ref[...])
    for got_ref in got_refs:
        total = total + got_ref[...].astype(jnp.float32)
    out_ref[...] = total.astype(out_ref.dtype)


def scatter_part(left, right, gots, first, size, dtype):
    rows, width = right.shape
    if size % 128 or first % size:
        total = contract("tm,tn->mn", left[:, first : first + size], right)
        for got, start in gots:
            total = total + got[start : start + size].astype(jnp.float32)
        return total.astype(dtype)
    tile = max(t for t in (128, 256, 384, 512) if width % t == 0)
    return pl.pallas_call(
        scatter_part_kernel,
        grid=(width // tile,),
        in_specs=[
            pl.BlockSpec((rows, size), lambda i: (0, first // size)),
            pl.BlockSpec((rows, tile), lambda i: (0, i)),
        ]
        + [
            pl.BlockSpec((size, tile), lambda i, at=start // size: (at, i)) for unused, start in gots
        ],
        out_specs=pl.BlockSpec((size, tile), lambda i: (0, i)),
        out_shape=jax.ShapeDtypeStruct((size, width), dtype),
        scratch_shapes=[pltpu.VMEM((size, rows), jnp.bfloat16)],
        compiler_params=pltpu.CompilerParams(vmem_limit_bytes=16 * 2**20),
        cost_estimate=cost(1, 1),
        name="scatter_part",
    )(left, right, *[got for got, unused in gots])


def product_back_kernel(left_ref, right_ref, out_ref):
    out_ref[...] = dot_nt(left_ref[...], right_ref[...]).astype(out_ref.dtype)


def product_back(left, right, first, tile=512):
    rows, width = left.shape
    model = right.shape[0]
    return pl.pallas_call(
        product_back_kernel,
        grid=(model // tile,),
        in_specs=[
            pl.BlockSpec((rows, width), lambda i: (0, 0)),
            pl.BlockSpec((tile, width), lambda i: (i, first // width)),
        ],
        out_specs=pl.BlockSpec((rows, tile), lambda i: (0, i)),
        out_shape=jax.ShapeDtypeStruct((rows, model), jnp.bfloat16),
        compiler_params=pltpu.CompilerParams(vmem_limit_bytes=44 * 2**20),
        cost_estimate=cost(1, 1),
        name="product_back",
    )(left, right)


def join_kernel(ready_ref, got_ref, out_ref):
    out_ref[...] = (ready_ref[...] + got_ref[...].astype(jnp.float32)).astype(out_ref.dtype)


def join_parts(ready, got, start, dtype):
    size, width = ready.shape
    if size % 128 or start % size:
        return (ready + got[start : start + size].astype(jnp.float32)).astype(dtype)
    tile = max(t for t in (128, 256, 384, 512, 768, 1024) if width % t == 0)
    return pl.pallas_call(
        join_kernel,
        grid=(width // tile,),
        in_specs=[
            pl.BlockSpec((size, tile), lambda i: (0, i)),
            pl.BlockSpec((size, tile), lambda i: (start // size, i)),
        ],
        out_specs=pl.BlockSpec((size, tile), lambda i: (0, i)),
        out_shape=jax.ShapeDtypeStruct((size, width), dtype),
        compiler_params=pltpu.CompilerParams(vmem_limit_bytes=16 * 2**20),
        cost_estimate=cost(1, 1),
        name="join_parts",
    )(ready, got)


def rms_back_kernel(value_ref, gain_ref, own_ref, other_ref, base_ref, live_ref, *out_refs):
    values = value_ref[...].astype(jnp.float32)
    gain = gain_ref[0:1]
    grad = own_ref[...].astype(jnp.float32) + other_ref[...].astype(jnp.float32)
    scale = lax.rsqrt(jnp.mean(values * values, axis=1, keepdims=True) + EPS)
    unit = values * scale
    scaled = grad * gain
    pull = jnp.mean(scaled * unit, axis=1, keepdims=True)
    total = base_ref[...].astype(jnp.float32) + (scaled - unit * pull) * scale
    out_refs[0][...] = total
    if len(out_refs) == 3:
        out_refs[2][...] = (total * live_ref[:, 0:1]).astype(jnp.bfloat16)
    gain_grad = jnp.broadcast_to(jnp.sum(grad * unit, axis=0, keepdims=True), out_refs[1].shape)

    @pl.when(pl.program_id(0) == 0)
    def _():
        out_refs[1][...] = gain_grad

    @pl.when(pl.program_id(0) > 0)
    def _():
        out_refs[1][...] += gain_grad


def rms_back(values, gain, own, other, base, live, with_rounded, tile=128):
    rows, model = values.shape
    each = pl.BlockSpec((tile, model), lambda i: (i, 0))
    whole = pl.BlockSpec((8, model), lambda i: (0, 0))
    shapes = [
        jax.ShapeDtypeStruct((rows, model), jnp.float32),
        jax.ShapeDtypeStruct((8, model), jnp.float32),
    ]
    if with_rounded:
        shapes.append(jax.ShapeDtypeStruct((rows, model), jnp.bfloat16))
    return pl.pallas_call(
        rms_back_kernel,
        grid=(rows // tile,),
        in_specs=[each, whole, each, each, each, pl.BlockSpec((tile, 128), lambda i: (i, 0))],
        out_specs=[each, whole, each][: len(shapes)],
        out_shape=shapes,
        compiler_params=pltpu.CompilerParams(vmem_limit_bytes=24 * 2**20),
        cost_estimate=cost(1, 1),
        name="rms_back",
    )(values, gain, own, other, base, live)


def beside_kernel(widths, *refs):
    out_ref, place, refs = refs[-1], 0, list(refs[:-1])
    for width, terms in widths:
        total = refs.pop(0)[...]
        if terms == 2:
            total = total.astype(jnp.float32) + refs.pop(0)[...].astype(jnp.float32)
        out_ref[:, place : place + width] = total.astype(out_ref.dtype)
        place += width
    if place < out_ref.shape[1]:
        out_ref[:, place:] = jnp.zeros((out_ref.shape[0], out_ref.shape[1] - place), out_ref.dtype)


def beside(width, *columns, tile=128):
    groups = [c if isinstance(c, tuple) else (c,) for c in columns]
    widths = tuple((g[0].shape[1], len(g)) for g in groups)
    arrays = [a for g in groups for a in g]
    rows = arrays[0].shape[0]
    return pl.pallas_call(
        functools.partial(beside_kernel, widths),
        grid=(rows // tile,),
        in_specs=[pl.BlockSpec((tile, a.shape[1]), lambda i: (i, 0)) for a in arrays],
        out_specs=pl.BlockSpec((tile, width), lambda i: (i, 0)),
        out_shape=jax.ShapeDtypeStruct((rows, width), jnp.bfloat16),
        compiler_params=pltpu.CompilerParams(vmem_limit_bytes=12 * 2**20),
        cost_estimate=cost(1, 1),
        name="beside",
    )(*arrays)


def hidden_back_kernel(first_ref, second_ref, third_ref, keep_ref, weight_ref, out_ref, total):
    step = pl.program_id(0)
    third = pl.num_programs(0) // 3

    @pl.when(step == 0)
    def _():
        total[...] = jnp.zeros_like(total)

    left = jnp.where(
        step < third,
        first_ref[...],
        jnp.where(step < 2 * third, second_ref[...], third_ref[...] * keep_ref[0:1]),
    )
    total[...] += dot_nt(left, weight_ref[...])

    @pl.when(step == pl.num_programs(0) - 1)
    def _():
        out_ref[...] = total[...].astype(out_ref.dtype)


def hidden_back(first, second, third, keep, weights, tile=768):
    rows, width = first.shape
    model = weights.shape[0]
    steps = width // tile
    block = lambda part: pl.BlockSpec(
        (rows, tile), lambda i: (0, jnp.clip(i - part * steps, 0, steps - 1))
    )
    return pl.pallas_call(
        hidden_back_kernel,
        grid=(3 * steps,),
        in_specs=[
            block(0),
            block(1),
            block(2),
            pl.BlockSpec((8, tile), lambda i: (0, jnp.maximum(i - 2 * steps, 0))),
            pl.BlockSpec((model, tile), lambda i: (0, i)),
        ],
        out_specs=pl.BlockSpec((rows, model), lambda i: (0, 0)),
        out_shape=jax.ShapeDtypeStruct((rows, model), jnp.bfloat16),
        scratch_shapes=[pltpu.VMEM((rows, model), jnp.float32)],
        compiler_params=pltpu.CompilerParams(vmem_limit_bytes=40 * 2**20),
        cost_estimate=cost(1, 1),
        name="hidden_back",
    )(first, second, third, keep, weights)


def rms_forward_kernel(base_ref, own_ref, other_ref, live_ref, gain_ref, middle_ref, out_ref):
    added = own_ref[...].astype(jnp.float32) + other_ref[...].astype(jnp.float32)
    values = base_ref[...].astype(jnp.float32) + added * live_ref[:, 0:1]
    middle_ref[...] = values
    scale = lax.rsqrt(jnp.mean(values * values, axis=1, keepdims=True) + EPS)
    out_ref[...] = (values * scale * gain_ref[0:1]).astype(out_ref.dtype)


def rms_forward(base, own, other, live, gain, tile=128):
    rows, model = base.shape
    each = pl.BlockSpec((tile, model), lambda i: (i, 0))
    return pl.pallas_call(
        rms_forward_kernel,
        grid=(rows // tile,),
        in_specs=[
            each,
            each,
            each,
            pl.BlockSpec((tile, 128), lambda i: (i, 0)),
            pl.BlockSpec((8, model), lambda i: (0, 0)),
        ],
        out_specs=[each, each],
        out_shape=[
            jax.ShapeDtypeStruct((rows, model), jnp.float32),
            jax.ShapeDtypeStruct((rows, model), jnp.bfloat16),
        ],
        compiler_params=pltpu.CompilerParams(vmem_limit_bytes=20 * 2**20),
        cost_estimate=cost(1, 1),
        name="rms_forward",
    )(base, own, other, live, gain)


def output_kernel(base_ref, own_ref, other_ref, live_ref, out_ref):
    added = own_ref[...].astype(jnp.float32) + other_ref[...].astype(jnp.float32)
    out_ref[...] = (base_ref[...] + added * live_ref[:, 0:1]).astype(out_ref.dtype)


def output_rows(base, own, other, live, tile=128):
    rows, model = base.shape
    each = pl.BlockSpec((tile, model), lambda i: (i, 0))
    return pl.pallas_call(
        output_kernel,
        grid=(rows // tile,),
        in_specs=[each, each, each, pl.BlockSpec((tile, 128), lambda i: (i, 0))],
        out_specs=each,
        out_shape=jax.ShapeDtypeStruct((rows, model), jnp.bfloat16),
        compiler_params=pltpu.CompilerParams(vmem_limit_bytes=16 * 2**20),
        cost_estimate=cost(1, 1),
        name="output_rows",
    )(base, own, other, live)


def stack_kernel(counts, *refs):
    out_ref, place = refs[-1], 0
    out_ref[...] = jnp.zeros_like(out_ref)
    for count, ref in zip(counts, refs):
        out_ref[place : place + count, : ref.shape[1]] = ref[:count, :]
        place += count


def stack_rows(width, *parts):
    counts = tuple(count for unused, count in parts)
    total = -(-sum(counts) // 8) * 8
    vmem = pl.BlockSpec(memory_space=pltpu.VMEM)
    return pl.pallas_call(
        functools.partial(stack_kernel, counts),
        in_specs=[vmem] * len(parts),
        out_specs=vmem,
        out_shape=jax.ShapeDtypeStruct((total, width), jnp.float32),
        compiler_params=pltpu.CompilerParams(vmem_limit_bytes=8 * 2**20),
        cost_estimate=cost(1, 1),
        name="stack_rows",
    )(*[part for part, unused in parts])


def tie(*values):
    return lax.optimization_barrier(values)


def pair_swap(values):
    return lax.ppermute(values, "tensor", [(0, 1), (1, 0)])


def pair_sum(values):
    own = lax.reduce_precision(values.astype(jnp.float32), 8, 7)
    return own + pair_swap(own.astype(jnp.bfloat16)).astype(jnp.float32)


def pair_join(values):
    other = pair_swap(values)
    first = lax.axis_index("tensor") == 0
    return jnp.concatenate(
        [jnp.where(first, values, other), jnp.where(first, other, values)], axis=0
    )


def after(values, *earlier):
    return lax.optimization_barrier((values, *earlier))[0]


def bits_of(count):
    return tuple(1 << place for place in range(count.bit_length() - 1))


def owner_order(bits):
    offsets = [0]
    for bit in reversed(bits):
        offsets = [offset | bit for offset in offsets] + offsets
    return lax.axis_index("dp") ^ jnp.array(offsets, jnp.int32)


def across(values, bit):
    count = lax.axis_size("dp")
    return lax.ppermute(values, "dp", [(i, i ^ bit) for i in range(count)])


class Scatter:
    def __init__(self, left, right, bits):
        self.left, self.right, self.bits = left, right, bits
        self.rows = left.shape[1] // 2 ** len(bits)
        self.got = []
        self.total = None

    def place(self, step):
        count = 2 ** len(self.bits)
        return count - (count >> step), max(count >> (step + 1), 1)

    def meets(self, past, step):
        return (self.place(step)[0] - self.place(past + 1)[0]) * self.rows

    def begin(self, *earlier):
        first, size = self.place(0)
        left = after(self.left, *earlier)
        self.held = scatter_part(left, self.right, [], 0, size * self.rows, jnp.bfloat16)
        return self.held

    def send(self, *earlier):
        self.got.append(across(after(self.held, *earlier), self.bits[len(self.got)]))
        return self.got[-1]

    def prepare(self, *earlier):
        step = len(self.got)
        first, size = self.place(step)
        gots = [(got, self.meets(past, step)) for past, got in enumerate(self.got[:-1])]
        left = after(self.left, *earlier)
        self.ready = scatter_part(
            left, self.right, gots, first * self.rows, size * self.rows, jnp.float32
        )
        return self.ready

    def make(self, *earlier):
        step = len(self.got)
        first, size = self.place(step)
        gots = [(got, self.meets(past, step)) for past, got in enumerate(self.got)]
        done = step == len(self.bits)
        self.held = scatter_part(
            after(self.left, *earlier),
            self.right,
            gots,
            first * self.rows,
            size * self.rows,
            jnp.float32 if done else jnp.bfloat16,
        )
        if done:
            self.total = self.held
        return self.held

    def join(self, *earlier):
        step = len(self.got)
        done = step == len(self.bits)
        self.held = join_parts(
            after(self.ready, *earlier),
            self.got[-1],
            self.meets(step - 1, step),
            jnp.float32 if done else jnp.bfloat16,
        )
        if done:
            self.total = self.held
        return self.held

    def finish(self):
        while self.total is None:
            self.send()
            self.make()
        return self.total


def local(
    tokens,
    cotangent,
    segment_ids,
    counts,
    mixer_gain,
    query_proj,
    key_value_matrix,
    attend_proj,
    inner_proj,
    state_proj,
    step_proj,
    conv_inner,
    conv_state,
    step_bias,
    decay_log,
    skip_gain,
    gated_gain,
    mamba_proj,
    dense_gain,
    gateup_proj,
    down_proj,
):
    row_count, model_width = tokens.shape
    shard_rows = query_proj.shape[0]
    dp_count = lax.axis_size("dp")
    bf16, f32 = jnp.bfloat16, jnp.float32
    heads_m = step_proj.shape[1]
    heads_q = query_proj.shape[1] // HEAD_DIMENSION
    q_cols = query_proj.shape[1]
    kv_cols = 2 * key_value_matrix.shape[2]
    x_cols = inner_proj.shape[2]
    state_cols = state_proj.shape[1]
    o_cols = attend_proj.shape[0]
    hidden_cols = gateup_proj.shape[2]
    tap_count = conv_state.shape[0]
    pair_width = conv_state.shape[1]

    small = jnp.concatenate(
        [mixer_gain[:, None], dense_gain[:, None], jnp.zeros((mixer_gain.shape[0], 126), bf16)],
        axis=1,
    )
    small = lax.dynamic_update_slice(small, conv_state.T, (0, 2))
    joined = pair_join(jnp.concatenate([state_proj, small], axis=1))
    step_pad = jnp.zeros((shard_rows, 128 - heads_m), bf16)
    group_mix = jnp.concatenate(
        [
            inner_proj.reshape(shard_rows, -1),
            query_proj,
            key_value_matrix.reshape(shard_rows, -1),
            joined[:, :state_cols],
            step_proj,
            step_pad,
            joined[:, state_cols:],
            attend_proj.T,
            mamba_proj.T,
        ],
        axis=1,
    )
    offsets, place = {}, 0
    for name, width in (
        ("z", x_cols),
        ("u", x_cols),
        ("q", q_cols),
        ("kv", kv_cols),
        ("state", state_cols),
        ("step", 128),
        ("end", 0),
    ):
        offsets[name] = place
        place += width
    out_first = offsets["end"] + 128
    group_ffn = jnp.concatenate([gateup_proj.reshape(shard_rows, -1), down_proj.T], axis=1)
    mix_full = lax.all_gather(group_mix, "dp", axis=0, tiled=True)
    ffn_full = lax.all_gather(after(group_ffn, mix_full), "dp", axis=0, tiled=True)
    out_t = mix_full[:, out_first:]
    down_t = ffn_full[:, 2 * hidden_cols :]

    small_full = mix_full[:, offsets["end"] : out_first]
    w_proj = mix_full[:, : offsets["end"]]
    gain_mix = small_full[:, 0].astype(f32)
    gain_dense = small_full[:, 1].astype(f32)
    conv_full = small_full[:, 2 : 2 + tap_count].reshape(
        dp_count, 2, shard_rows // 2, tap_count
    )[:, :, :pair_width]
    conv_full = conv_full.reshape(dp_count * 2 * pair_width, tap_count).T.astype(f32)
    conv_full = jnp.concatenate([conv_full, jnp.zeros((8 - tap_count, state_cols), f32)], axis=0)
    gain_gated = gated_gain.astype(f32)
    wide = jnp.concatenate(
        [
            conv_inner.astype(f32),
            jnp.repeat(skip_gain.astype(f32), HP)[None],
            gain_gated[None],
            jnp.zeros((1, x_cols), f32),
        ],
        axis=0,
    )
    extra = jnp.zeros((8, 128), f32)
    extra = extra.at[0, :heads_m].set(step_bias.astype(f32))
    extra = extra.at[1, :heads_m].set(jnp.exp(decay_log.astype(f32)))

    row_index = jnp.arange(row_count, dtype=jnp.int32)
    valid_rows = (row_index < counts[0]).astype(f32)[:, None]
    live = jnp.broadcast_to(valid_rows, (row_count, 128))
    position = positions_of(segment_ids)
    causal = (row_index[None, :] <= row_index[:, None]) & (
        segment_ids[None, :] == segment_ids[:, None]
    )
    mask = causal.astype(f32)
    mask_t = (
        (row_index[None, :] >= row_index[:, None]) & (segment_ids[None, :] == segment_ids[:, None])
    ).astype(f32)
    mask_qk = (causal & (row_index[None, :] < counts[0])).astype(f32)
    same = jnp.stack(
        [
            jnp.broadcast_to(((row_index >= lag) & (position >= lag)).astype(f32)[:, None], live.shape)
            for lag in range(1, tap_count - 1)
        ]
    )
    half = HEAD_DIMENSION // 2
    frequency = jnp.exp(
        jnp.arange(half, dtype=f32) * (-2.0 * math.log(THETA) / HEAD_DIMENSION)
    )
    angles = position.astype(f32)[:, None] * frequency[None, :]
    cos = jnp.cos(angles)
    sin = jnp.sin(angles)
    cos = jnp.concatenate([cos, cos], axis=1)
    sin = jnp.concatenate([-sin, sin], axis=1)
    bits = bits_of(dp_count)
    order = owner_order(bits)
    stream = tokens.astype(f32)
    upstream = cotangent.astype(f32)
    dense_grad_b = rounded(upstream * valid_rows)
    dense_split = reorder_columns(dense_grad_b, order)

    gain_dense_rows = jnp.broadcast_to(gain_dense[None], (8, model_width))
    gain_mix_rows = jnp.broadcast_to(gain_mix[None], (8, model_width))

    hidden_b = rounded(rms_scale(stream, gain_mix))
    projected = contract("td,dc->tc", hidden_b, w_proj)
    hidden_split = reorder_columns(hidden_b, order)
    mixed, gated, squares = ssm_forward(
        projected, wide, conv_full, extra, live, same, mask, offsets
    )
    own_squares = jnp.sum(squares, axis=-1)
    other_squares = pair_swap(own_squares)
    attended_b, query_b, key_b, value_b, logs = attention_forward(
        projected, cos, sin, mask_qk, offsets, heads_q
    )
    inverse = lax.rsqrt((own_squares + other_squares) / DSSM + EPS)
    normed_b = rounded(gated * inverse[:, None] * gain_gated)
    branch_in = jnp.concatenate([attended_b, normed_b], axis=1)
    branch_own = rounded(contract("tc,dc->td", branch_in, out_t))
    branch_other = pair_swap(branch_own)
    middle, ffn_in_b = rms_forward(tokens, branch_own, branch_other, live, gain_dense_rows)
    inverse_b = jnp.broadcast_to(inverse[:, None], live.shape)
    gated_rows = jnp.broadcast_to(gain_gated[None], (8, x_cols))
    first = (lax.axis_index("tensor") == 0).astype(bf16)
    column_at = jnp.arange(x_cols) - (q_cols + kv_cols)
    keep = jnp.where((column_at >= 0) & (column_at < state_cols), first, jnp.ones((), bf16))
    keep = jnp.broadcast_to(keep[None], (8, x_cols))
    ffn_split = reorder_columns(ffn_in_b, order)

    activated_b, grad_gate_b, grad_up_b, grad_ffn_part = feed_forward(
        ffn_in_b, after(dense_grad_b, ffn_split, dense_split), ffn_full, hidden_cols
    )
    down = Scatter(dense_split, activated_b, bits)
    gate_sum = Scatter(ffn_split, grad_gate_b, bits)
    up_sum = Scatter(ffn_split, grad_up_b, bits)
    held = down.begin()
    down.send()
    held = gate_sum.begin(held)
    ready = down.prepare(held)

    held = down.join(ready)
    down.send()
    grad_ffn_other = pair_swap(after(grad_ffn_part, ready))
    gate_sum.send(ready)
    held = up_sum.begin(held)
    ready = down.prepare(held)
    dense_own = product_back(after(activated_b, ready), ffn_full, 2 * hidden_cols)
    ready = gate_sum.prepare(dense_own)

    round_end = (ready, down.got[-1], gate_sum.got[-1], grad_ffn_other)
    held = gate_sum.join(*round_end)
    gate_sum.send()
    up_sum.send(*round_end)
    held = down.make(held)
    down.send()
    grad_middle, grad_dense_gain, mixer_grad_b = rms_back(
        middle, gain_dense_rows, after(grad_ffn_part, held), grad_ffn_other, cotangent, live, True
    )
    grad_attended_b, grad_normed, own_rows, column_part = norm_back(
        mixer_grad_b, mix_full, out_first, o_cols, gated, inverse_b, gated_rows
    )
    other_rows = pair_swap(own_rows)
    branch = Scatter(reorder_columns(mixer_grad_b, order), branch_in, bits)
    held = branch.begin(own_rows)
    ready = up_sum.prepare(held)
    grad_query_b, grad_key_b, grad_value_b = attention_backward(
        after(grad_attended_b, ready), query_b, key_b, value_b, logs, cos, sin, mask_qk
    )
    ready = grad_query_b

    round_end = (ready, gate_sum.got[-1], up_sum.got[-1], down.got[-1], other_rows)
    held = up_sum.join(*round_end)
    up_sum.send()
    branch.send(*round_end)
    held = gate_sum.make(held)
    gate_sum.send()
    held = down.make(held)
    down.send()
    dense_other = pair_swap(after(dense_own, *round_end))
    grad_z_b, grad_u_b, grad_state_part, grad_step_b, wide_grad, conv_grad, extra_grad = (
        ssm_backward(
            after(grad_normed, held),
            mixed,
            projected,
            inverse_b,
            own_rows,
            other_rows,
            wide,
            conv_full,
            extra,
            live,
            same,
            mask_t,
            offsets,
        )
    )
    z_sum = Scatter(hidden_split, grad_z_b, bits)
    u_sum = Scatter(hidden_split, grad_u_b, bits)
    held = z_sum.begin(grad_state_part)
    ready = branch.prepare(held)

    round_end = (ready, up_sum.got[-1], gate_sum.got[-1], branch.got[-1], down.got[-1], dense_other)
    held = branch.join(*round_end)
    branch.send()
    z_sum.send(*round_end)
    grad_state_other = pair_swap(after(grad_state_part, *round_end))
    held = up_sum.make(held)
    up_sum.send()
    held = gate_sum.make(held)
    gate_sum.send()
    held = down.make(held)
    held = u_sum.begin(held)
    other_b = beside(
        x_cols,
        grad_query_b,
        grad_key_b,
        grad_value_b,
        (grad_state_part, after(grad_state_other, held)),
        grad_step_b,
    )
    other_sum = Scatter(hidden_split, other_b, bits)
    grad_hidden_own = hidden_back(after(grad_z_b, other_b), grad_u_b, other_b, keep, mix_full)
    held = other_sum.begin(grad_hidden_own)
    ready = z_sum.prepare(held)

    round_end = (ready, branch.got[-1], up_sum.got[-1], gate_sum.got[-1], z_sum.got[-1])
    held = z_sum.join(*round_end)
    z_sum.send()
    u_sum.send(*round_end)
    half_rows = row_count // 2
    hidden_top = pair_swap(after(grad_hidden_own[:half_rows], *round_end))
    held = branch.make(held)
    branch.send()
    held = up_sum.make(held)
    up_sum.send()
    held = gate_sum.make(held)
    ready = u_sum.prepare(held)

    round_end = (ready, z_sum.got[-1], u_sum.got[-1], branch.got[-1], up_sum.got[-1], hidden_top)
    held = u_sum.join(*round_end)
    u_sum.send()
    other_sum.send(*round_end)
    hidden_end = pair_swap(after(grad_hidden_own[half_rows:], *round_end))
    held = z_sum.make(held)
    z_sum.send()
    held = branch.make(held)
    branch.send()
    held = up_sum.make(held)
    output = output_rows(middle, after(dense_own, held), dense_other, live)
    ready = other_sum.prepare(output)

    round_end = (ready, u_sum.got[-1], other_sum.got[-1], z_sum.got[-1], branch.got[-1], hidden_end)
    held = other_sum.join(*round_end)
    other_sum.send()
    held = u_sum.make(held)
    u_sum.send()
    held = z_sum.make(held)
    z_sum.send()
    grad_hidden_other = jnp.concatenate([hidden_top, hidden_end], axis=0)
    grad_tokens, grad_mixer_gain = rms_back(
        tokens, gain_mix_rows, after(grad_hidden_own, held), grad_hidden_other, grad_middle, live, False
    )
    own_sums = stack_rows(
        model_width,
        (grad_mixer_gain, 1),
        (grad_dense_gain, 1),
        (wide_grad, tap_count + 1),
        (column_part, 1),
        (conv_grad, tap_count),
        (extra_grad, 2),
    )
    sums = own_sums + across(own_sums, bits[0])
    held = branch.make(sums)
    ready = other_sum.prepare(held)
    ready = u_sum.prepare(ready)
    ready = z_sum.prepare(ready)
    others = across(after(sums, ready), bits[1])

    round_end = (ready, other_sum.got[-1], u_sum.got[-1], z_sum.got[-1], others)
    held = other_sum.join(*round_end)
    other_sum.send()
    held = u_sum.join(held)
    u_sum.send()
    sums = after(sums, held) + others
    others = across(sums, bits[2])
    held = z_sum.join(sums)
    ready = other_sum.prepare(held)
    ready = u_sum.prepare(ready)

    held = other_sum.join(ready, other_sum.got[-1], u_sum.got[-1], others)
    other_sum.send()
    sums = after(sums, held) + others
    for bit in bits[3:]:
        sums = sums + across(sums, bit)
    held = u_sum.join(held)
    other_sum.prepare(held)
    other_sum.join(sums)
    at = 2 + tap_count + 2
    conv_sum = sums[at : at + tap_count, :state_cols]
    conv_sum = conv_sum + pair_swap(conv_sum)
    at += tap_count
    skip_sum = jnp.sum(sums[2 + tap_count, :x_cols].reshape(heads_m, HP), axis=1)
    owner = lax.axis_index("dp") * 2 + lax.axis_index("tensor")

    def own_part(values, axis_dim):
        width = values.shape[axis_dim] // (2 * dp_count)
        return lax.dynamic_slice_in_dim(values, owner * width, width, axis_dim)

    red_branch, red_other = branch.finish(), other_sum.finish()
    state_rows = shard_rows // 2
    state_first = q_cols + kv_cols
    red_state = lax.dynamic_slice_in_dim(
        red_other[:, state_first : state_first + state_cols],
        lax.axis_index("tensor") * state_rows,
        state_rows,
        0,
    )
    return (
        output,
        grad_tokens,
        own_part(sums[0], 0),
        red_other[:, :q_cols],
        red_other[:, q_cols:state_first].reshape(shard_rows, 2, -1),
        red_branch[:, :o_cols].T,
        jnp.stack([z_sum.finish(), u_sum.finish()], axis=1),
        red_state,
        red_other[:, state_first + state_cols : state_first + state_cols + heads_m],
        sums[2 : 2 + tap_count, :x_cols],
        own_part(conv_sum, 1),
        sums[at, :heads_m],
        sums[at + 1, :heads_m],
        skip_sum,
        sums[3 + tap_count, :x_cols],
        red_branch[:, o_cols:].T,
        own_part(sums[1], 0),
        jnp.stack([gate_sum.finish(), up_sum.finish()], axis=1),
        down.finish().T,
    )


def solution(mesh):
    placed = (
        P("dp", None),
        P("dp", None),
        P("dp"),
        P("dp"),
        P(("dp", "tensor")),
        P("dp", "tensor"),
        P("dp", None, "tensor"),
        P("tensor", "dp"),
        P("dp", None, "tensor"),
        P(("dp", "tensor"), None),
        P("dp", "tensor"),
        P(None, "tensor"),
        P(None, ("dp", "tensor")),
        P("tensor"),
        P("tensor"),
        P("tensor"),
        P("tensor"),
        P("tensor", "dp"),
        P(("dp", "tensor")),
        P("dp", None, "tensor"),
        P("tensor", "dp"),
    )
    return jax.shard_map(
        local,
        mesh=mesh,
        in_specs=placed,
        out_specs=(
            P("dp", None),
            P("dp", None),
            P(("dp", "tensor")),
            P("dp", "tensor"),
            P("dp", None, "tensor"),
            P("tensor", "dp"),
            P("dp", None, "tensor"),
            P(("dp", "tensor"), None),
            P("dp", "tensor"),
            P(None, "tensor"),
            P(None, ("dp", "tensor")),
            P("tensor"),
            P("tensor"),
            P("tensor"),
            P("tensor"),
            P("tensor", "dp"),
            P(("dp", "tensor")),
            P("dp", None, "tensor"),
            P("tensor", "dp"),
        ),
        check_vma=False,
    )
```

```python
import functools
import math

import jax
import jax.numpy as jnp
from jax import lax
from jax.experimental import pallas as pl
from jax.experimental.pallas import tpu as pltpu
from jax.experimental.layout import Layout, with_layout_constraint
from jax.sharding import PartitionSpec as P

HP = 64
HEAD_DIMENSION = 128
DSSM = 3072
TILE = 256

EPS = 1e-05
THETA = 100000000000.0


def rounded(values):
    return values.astype(jnp.bfloat16)


def contract(form, left, right):
    return jnp.einsum(form, left, right, preferred_element_type=jnp.float32)


def rms_scale(values, gain):
    return values * lax.rsqrt(jnp.mean(values * values, axis=-1, keepdims=True) + EPS) * gain


def cost(flops, traffic, transcendentals=0):
    return pl.CostEstimate(
        flops=flops, bytes_accessed=traffic, transcendentals=transcendentals
    )


def positions_of(segment):
    row_index = jnp.arange(segment.shape[0], dtype=jnp.int32)
    starts = jnp.concatenate([jnp.ones((1,), jnp.bool_), segment[1:] != segment[:-1]])
    first_row = lax.cummax(jnp.where(starts, row_index, 0), axis=0)
    return row_index - first_row


def silu_parts(values):
    gate = jax.nn.sigmoid(values)
    return values * gate, gate * (1.0 + values * (1.0 - gate))


def dot_nn(left, right):
    return lax.dot_general(left, right, (((1,), (0,)), ((), ())), preferred_element_type=jnp.float32)


def dot_nt(left, right):
    return lax.dot_general(left, right, (((1,), (1,)), ((), ())), preferred_element_type=jnp.float32)


def dot_tn(left, right):
    return lax.dot_general(left, right, (((0,), (0,)), ((), ())), preferred_element_type=jnp.float32)


def shifted_rows(values, lag, same_ref):
    columns = values.shape[1]
    mask = same_ref[lag - 1]
    if columns > mask.shape[1]:
        mask = jnp.concatenate([mask] * (columns // mask.shape[1]), axis=1)
    return mask * pltpu.roll(values, lag, 0)


def conv_rows(values, taps, same_ref):
    total = taps[4:5] + taps[3:4] * values
    for lag in range(1, 4):
        total = total + taps[3 - lag : 4 - lag] * shifted_rows(values, lag, same_ref)
    return total


def conv_rows_back(grad, values, taps, same_ref):
    rows = grad.shape[0]
    total = taps[3:4] * grad
    tap_grads = [None] * 5
    tap_grads[4] = jnp.sum(grad, axis=0, keepdims=True)
    tap_grads[3] = jnp.sum(grad * values, axis=0, keepdims=True)
    for lag in range(1, 4):
        mask = same_ref[lag - 1]
        if grad.shape[1] > mask.shape[1]:
            mask = jnp.concatenate([mask] * (grad.shape[1] // mask.shape[1]), axis=1)
        masked = grad * mask
        total = total + taps[3 - lag : 4 - lag] * pltpu.roll(masked, rows - lag, 0)
        tap_grads[3 - lag] = jnp.sum(
            masked * pltpu.roll(values, lag, 0), axis=0, keepdims=True
        )
    return total, tap_grads


def running_sum(values, backward=False):
    rows = values.shape[0]
    index = lax.broadcasted_iota(jnp.int32, values.shape, 0)
    step = 1
    while step < rows:
        if backward:
            moved = pltpu.roll(values, rows - step, 0)
            values = values + jnp.where(index < rows - step, moved, 0.0)
        else:
            moved = pltpu.roll(values, step, 0)
            values = values + jnp.where(index >= step, moved, 0.0)
        step *= 2
    return values


def step_sizes(raw, extra_ref, live):
    shifted = raw + extra_ref[0:1]
    size = (jnp.maximum(shifted, 0.0) + jnp.log1p(jnp.exp(-jnp.abs(shifted)))) * live
    return shifted, size, -size * extra_ref[1:2]


def lane_column(values, lane):
    lanes = lax.broadcasted_iota(jnp.int32, values.shape, 1)
    return jnp.sum(jnp.where(lanes == lane, values, 0.0), axis=1, keepdims=True)


def head_sums(values, pair):
    lanes = lax.broadcasted_iota(jnp.int32, (128, 128), 0)
    heads = lax.broadcasted_iota(jnp.int32, (128, 128), 1)
    chosen = (heads == 2 * pair + lanes // HP).astype(jnp.bfloat16)
    high = values.astype(jnp.bfloat16)
    low = (values - high.astype(jnp.float32)).astype(jnp.bfloat16)
    return dot_nn(jnp.concatenate([high, low], axis=1), jnp.concatenate([chosen, chosen], axis=0))


def ssm_forward_kernel(
    u_ref, z_ref, state_b_ref, state_c_ref, step_ref, wide_ref, conv_ref, extra_ref, live_ref, same_ref, mask_ref,
    y_ref, gated_ref, square_ref, gram, sizes, running, running_t,
):
    step = pl.program_id(0)
    live = live_ref[...]
    rows = live.shape[0]

    @pl.when(step == 0)
    def _():
        unused, size, decay = step_sizes(step_ref[...], extra_ref, live)
        total = running_sum(decay)
        sizes[...] = size
        running[...] = total
        running_t[...] = total.T
        width = conv_ref.shape[1]
        wide_live = jnp.concatenate([live] * (width // 128), axis=1)
        state = jnp.concatenate([state_b_ref[...], state_c_ref[...]], axis=1) * wide_live
        inner = conv_rows(state, conv_ref[...], same_ref)
        both = (inner * jax.nn.sigmoid(inner)).astype(jnp.bfloat16)
        gram[...] = dot_nt(both[:, width // 2 :], both[:, : width // 2]) * mask_ref[...]
        square_ref[...] = jnp.zeros_like(square_ref)

    for part in range(2):
        pair = 2 * step + part
        at = slice(part * 128, (part + 1) * 128)
        taps = wide_ref[:, at]
        inner = conv_rows(u_ref[:, at] * live, taps, same_ref)
        x_in = inner * jax.nn.sigmoid(inner)
        left_lanes = lax.broadcasted_iota(jnp.int32, (rows, 128), 1) < HP
        size = sizes[...]
        size_pair = jnp.where(left_lanes, lane_column(size, 2 * pair), lane_column(size, 2 * pair + 1))
        inflow = (size_pair * x_in).astype(jnp.bfloat16)
        total = running[...]
        columns = [lane_column(total, 2 * pair + k) for k in range(2)]
        row_vectors = [running_t[pl.ds(2 * pair + k, 1), :] for k in range(2)]
        skipped = taps[5:6] * x_in
        gate = z_ref[:, at]
        gate = gate * jax.nn.sigmoid(gate)
        for block in range(rows // TILE):
            top, end = block * TILE, (block + 1) * TILE
            parts = []
            for k in range(2):
                gaps = columns[k][top:end] - row_vectors[k][:, :end]
                mixing = (gram[top:end, :end] * jnp.exp(jnp.minimum(gaps, 0.0))).astype(jnp.bfloat16)
                parts.append(dot_nn(mixing, inflow[:end]))
            mixed = jnp.where(left_lanes[top:end], parts[0], parts[1]) + skipped[top:end]
            y_ref[top:end, at] = mixed
            gated = mixed * gate[top:end]
            gated_ref[top:end, at] = gated
            square_ref[top:end, :] += gated * gated


def ssm_forward(projected, wide, conv_state, extra, live, same, mask, offsets):
    rows = projected.shape[0]
    pairs = wide.shape[1] // 128
    width = conv_state.shape[1]
    const2 = lambda i: (0, 0)
    at = lambda name, size: offsets[name] // size
    block = lambda name: pl.BlockSpec((rows, 128 * 2), lambda i, o=at(name, 128 * 2): (0, o + i))
    return pl.pallas_call(
        ssm_forward_kernel,
        grid=(pairs // 2,),
        in_specs=[
            block("u"),
            block("z"),
            pl.BlockSpec((rows, width // 2), lambda i: (0, at("state", width // 2))),
            pl.BlockSpec((rows, width // 2), lambda i: (0, at("state", width // 2) + 1)),
            pl.BlockSpec((rows, 128), lambda i: (0, at("step", 128))),
            pl.BlockSpec((8, 128 * 2), lambda i: (0, i)),
            pl.BlockSpec((8, width), const2),
            pl.BlockSpec((8, 128), const2),
            pl.BlockSpec((rows, 128), const2),
            pl.BlockSpec((3, rows, 128), lambda i: (0, 0, 0)),
            pl.BlockSpec((rows, rows), const2),
        ],
        out_specs=[
            pl.BlockSpec((rows, 128 * 2), lambda i: (0, i)),
            pl.BlockSpec((rows, 128 * 2), lambda i: (0, i)),
            pl.BlockSpec((rows, 128), const2),
        ],
        out_shape=[
            jax.ShapeDtypeStruct((rows, pairs * 128), jnp.float32),
            jax.ShapeDtypeStruct((rows, pairs * 128), jnp.float32),
            jax.ShapeDtypeStruct((rows, 128), jnp.float32),
        ],
        scratch_shapes=[
            pltpu.VMEM((rows, rows), jnp.float32),
            pltpu.VMEM((rows, 128), jnp.float32),
            pltpu.VMEM((rows, 128), jnp.float32),
            pltpu.VMEM((128, rows), jnp.float32),
        ],
        compiler_params=pltpu.CompilerParams(vmem_limit_bytes=28 * 2**20),
        name="ssm_forward",
    )(projected, projected, projected, projected, projected, wide, conv_state, extra, live, same, mask)


def ssm_backward_kernel(
    dn_ref, y_ref, u_ref, z_ref, state_b_ref, state_c_ref, step_ref, inverse_ref, own_ref, other_ref,
    wide_ref, conv_ref, extra_ref, live_ref, same_ref, mask_t_ref,
    dz_ref, du_ref, ds_ref, dr_ref, wide_grad_ref, extra_grad_ref,
    gram_t, gram_grad, sizes, decays, running, running_t, size_grad, total_grad, states, state_slopes,
):
    step = pl.program_id(0)
    live = live_ref[...]
    rows = live.shape[0]
    width = conv_ref.shape[1]
    wide_live = jnp.concatenate([live] * (width // 128), axis=1)

    @pl.when(step == 0)
    def _():
        unused, size, decay = step_sizes(step_ref[...], extra_ref, live)
        total = running_sum(decay)
        sizes[...] = size
        decays[...] = decay
        running[...] = total
        running_t[...] = total.T
        state = jnp.concatenate([state_b_ref[...], state_c_ref[...]], axis=1) * wide_live
        inner = conv_rows(state, conv_ref[...], same_ref)
        value, slope = silu_parts(inner)
        both = value.astype(jnp.bfloat16)
        states[...] = both
        state_slopes[...] = slope
        gram_t[...] = dot_nt(both[:, : width // 2], both[:, width // 2 :]) * mask_t_ref[...]
        gram_grad[...] = jnp.zeros_like(gram_grad)
        size_grad[...] = jnp.zeros_like(size_grad)
        total_grad[...] = jnp.zeros_like(total_grad)

    for part in range(2):
        pair = 2 * step + part
        at = slice(part * 128, (part + 1) * 128)
        taps = wide_ref[:, at]
        u_live = u_ref[:, at] * live
        inner = conv_rows(u_live, taps, same_ref)
        x_in, x_slope = silu_parts(inner)
        gate, gate_slope = silu_parts(z_ref[:, at])
        mixed = y_ref[:, at]
        gated = mixed * gate
        inverse = inverse_ref[:, 0:1]
        pull = (own_ref[:, 0:1] + other_ref[:, 0:1]) * inverse * inverse * inverse / DSSM
        grad_gated = taps[6:7] * dn_ref[:, at] * inverse - gated * pull
        grad_mixed = grad_gated * gate
        dz_ref[:, at] = (grad_gated * mixed * gate_slope).astype(dz_ref.dtype)
        grad_mixed_b = grad_mixed.astype(jnp.bfloat16)
        lanes = lax.broadcasted_iota(jnp.int32, (rows, 128), 1)
        left_lanes = lanes < HP
        size = sizes[...]
        size_pair = jnp.where(left_lanes, lane_column(size, 2 * pair), lane_column(size, 2 * pair + 1))
        inflow = (size_pair * x_in).astype(jnp.bfloat16)
        zero = jnp.zeros_like(inflow)
        inflow_heads = [jnp.where(left_lanes, inflow, zero), jnp.where(left_lanes, zero, inflow)]
        total = running[...]
        columns = [lane_column(total, 2 * pair + k) for k in range(2)]
        row_vectors = [running_t[pl.ds(2 * pair + k, 1), :] for k in range(2)]
        blocks = []
        for block in range(rows // TILE):
            top, end = block * TILE, (block + 1) * TILE
            parts = []
            gram_part = None
            for k in range(2):
                gaps = row_vectors[k][:, top:] - columns[k][top:end]
                decay = jnp.exp(jnp.minimum(gaps, 0.0))
                mixing_t = (gram_t[top:end, top:] * decay).astype(jnp.bfloat16)
                parts.append(dot_nn(mixing_t, grad_mixed_b[top:]))
                term = dot_nt(inflow_heads[k][top:end], grad_mixed_b[top:]) * decay
                gram_part = term if gram_part is None else gram_part + term
            gram_grad[top:end, top:] += gram_part
            blocks.append(jnp.where(left_lanes[top:end], parts[0], parts[1]))
        grad_inflow = jnp.concatenate(blocks, axis=0)
        grad_x = grad_mixed * taps[5:6] + grad_inflow * size_pair
        by_size = grad_inflow * x_in
        mixed_only = mixed - taps[5:6] * x_in
        by_total = grad_mixed_b.astype(jnp.float32) * mixed_only - grad_inflow * inflow.astype(jnp.float32)
        size_grad[...] += head_sums(by_size, pair)
        total_grad[...] += head_sums(by_total, pair)
        grad_u, tap_grads = conv_rows_back(grad_x * x_slope, u_live, taps, same_ref)
        du_ref[:, at] = (grad_u * live).astype(du_ref.dtype)
        skip_grad = jnp.sum(grad_mixed * x_in, axis=0, keepdims=True)
        wide_grad_ref[:, at] = jnp.concatenate(
            tap_grads + [skip_grad, jnp.zeros((2, 128), jnp.float32)], axis=0
        )

    @pl.when(step == pl.num_programs(0) - 1)
    def _():
        half = width // 2
        gram_grad_b = (gram_grad[...] * mask_t_ref[...]).astype(jnp.bfloat16)
        grad_b = dot_nn(gram_grad_b, states[:, half:])
        grad_c = dot_tn(gram_grad_b, states[:, :half])
        grad_bc = jnp.concatenate([grad_b, grad_c], axis=1) * state_slopes[...]
        state = jnp.concatenate([state_b_ref[...], state_c_ref[...]], axis=1) * wide_live
        grad_in, state_taps = conv_rows_back(grad_bc, state, conv_ref[...], same_ref)
        ds_ref[:rows, :] = (grad_in * wide_live).astype(ds_ref.dtype)
        ds_ref[rows:, :] = jnp.concatenate(
            state_taps + [jnp.zeros((11, width), jnp.float32)], axis=0
        ).astype(ds_ref.dtype)
        decay_grad = running_sum(total_grad[...], backward=True)
        shifted = step_ref[...] + extra_ref[0:1]
        grad_size = size_grad[...] - decay_grad * extra_ref[1:2]
        grad_raw = grad_size * live * jax.nn.sigmoid(shifted)
        dr_ref[...] = grad_raw.astype(dr_ref.dtype)
        extra_grad_ref[...] = jnp.concatenate(
            [
                jnp.sum(grad_raw, axis=0, keepdims=True),
                jnp.sum(decay_grad * decays[...], axis=0, keepdims=True),
                jnp.zeros((6, 128), jnp.float32),
            ],
            axis=0,
        )


def ssm_backward(
    grad_normed, mixed, projected, inverse, own, other, wide, conv_state, extra, live, same, mask_t, offsets
):
    rows = projected.shape[0]
    pairs = wide.shape[1] // 128
    width = conv_state.shape[1]
    const2 = lambda i: (0, 0)
    at = lambda name, size: offsets[name] // size
    block = lambda name: pl.BlockSpec((rows, 128 * 2), lambda i, o=at(name, 128 * 2): (0, o + i))
    plain = pl.BlockSpec((rows, 128 * 2), lambda i: (0, i))
    f32, b16 = jnp.float32, jnp.bfloat16
    return pl.pallas_call(
        ssm_backward_kernel,
        grid=(pairs // 2,),
        in_specs=[
            plain,
            plain,
            block("u"),
            block("z"),
            pl.BlockSpec((rows, width // 2), lambda i: (0, at("state", width // 2))),
            pl.BlockSpec((rows, width // 2), lambda i: (0, at("state", width // 2) + 1)),
            pl.BlockSpec((rows, 128), lambda i: (0, at("step", 128))),
            pl.BlockSpec((rows, 128), const2),
            pl.BlockSpec((rows, 128), const2),
            pl.BlockSpec((rows, 128), const2),
            pl.BlockSpec((8, 128 * 2), lambda i: (0, i)),
            pl.BlockSpec((8, width), const2),
            pl.BlockSpec((8, 128), const2),
            pl.BlockSpec((rows, 128), const2),
            pl.BlockSpec((3, rows, 128), lambda i: (0, 0, 0)),
            pl.BlockSpec((rows, rows), const2),
        ],
        out_specs=[
            plain,
            plain,
            pl.BlockSpec((rows + 16, width), const2),
            pl.BlockSpec((rows, 128), const2),
            pl.BlockSpec((8, 128 * 2), lambda i: (0, i)),
            pl.BlockSpec((8, 128), const2),
        ],
        out_shape=[
            jax.ShapeDtypeStruct((rows, pairs * 128), b16),
            jax.ShapeDtypeStruct((rows, pairs * 128), b16),
            jax.ShapeDtypeStruct((rows + 16, width), b16),
            jax.ShapeDtypeStruct((rows, 128), b16),
            jax.ShapeDtypeStruct((8, pairs * 128), f32),
            jax.ShapeDtypeStruct((8, 128), f32),
        ],
        scratch_shapes=[
            pltpu.VMEM((rows, rows), f32),
            pltpu.VMEM((rows, rows), f32),
            pltpu.VMEM((rows, 128), f32),
            pltpu.VMEM((rows, 128), f32),
            pltpu.VMEM((rows, 128), f32),
            pltpu.VMEM((128, rows), f32),
            pltpu.VMEM((rows, 128), f32),
            pltpu.VMEM((rows, 128), f32),
            pltpu.VMEM((rows, width), b16),
            pltpu.VMEM((rows, width), f32),
        ],
        compiler_params=pltpu.CompilerParams(vmem_limit_bytes=32 * 2**20),
        cost_estimate=cost(1, 1),
        name="ssm_backward",
    )(
        grad_normed, mixed, projected, projected, projected, projected, projected, inverse, own, other,
        wide, conv_state, extra, live, same, mask_t,
    )


def turned(values, cos_ref, sin_ref):
    return values * cos_ref[...] + pltpu.roll(values, HEAD_DIMENSION // 2, 1) * sin_ref[...]


def attention_forward_kernel(
    q_ref, k_ref, v_ref, cos_ref, sin_ref, mask_ref, out_ref, query_ref, key_ref, value_ref, log_ref
):
    head = pl.program_id(0)
    rows = q_ref.shape[0]
    scale = HEAD_DIMENSION**-0.5

    @pl.when(head == 0)
    def _():
        key_ref[...] = turned(k_ref[...], cos_ref, sin_ref).astype(jnp.bfloat16)
        value_ref[...] = v_ref[...].astype(jnp.bfloat16)

    query = turned(q_ref[...], cos_ref, sin_ref).astype(jnp.bfloat16)
    query_ref[...] = query
    for block in range(rows // TILE):
        top, end = block * TILE, (block + 1) * TILE
        scores = dot_nt(query[top:end], key_ref[:end, :]) * scale
        scores = jnp.where(mask_ref[top:end, :end] > 0.0, scores, -1e30)
        largest = jnp.max(scores, axis=1, keepdims=True)
        weights = jnp.exp(scores - largest)
        total = jnp.sum(weights, axis=1, keepdims=True)
        probs = (weights / total).astype(jnp.bfloat16)
        out_ref[top:end, :] = dot_nn(probs, value_ref[:end, :]).astype(out_ref.dtype)
        log_ref[top:end, :] = jnp.broadcast_to(largest + jnp.log(total), (TILE, 128))


def attention_forward(projected, cos, sin, mask, offsets, heads):
    rows = projected.shape[0]
    at = lambda name: offsets[name] // 128
    const2 = lambda i: (0, 0)
    one = pl.BlockSpec((rows, 128), const2)
    each = pl.BlockSpec((rows, 128), lambda i: (0, i))
    b16 = jnp.bfloat16
    return pl.pallas_call(
        attention_forward_kernel,
        grid=(heads,),
        in_specs=[
            pl.BlockSpec((rows, 128), lambda i: (0, at("q") + i)),
            pl.BlockSpec((rows, 128), lambda i: (0, at("kv"))),
            pl.BlockSpec((rows, 128), lambda i: (0, at("kv") + 1)),
            one,
            one,
            pl.BlockSpec((rows, rows), const2),
        ],
        out_specs=[each, each, one, one, each],
        out_shape=[
            jax.ShapeDtypeStruct((rows, heads * 128), b16),
            jax.ShapeDtypeStruct((rows, heads * 128), b16),
            jax.ShapeDtypeStruct((rows, 128), b16),
            jax.ShapeDtypeStruct((rows, 128), b16),
            jax.ShapeDtypeStruct((rows, heads * 128), jnp.float32),
        ],
        compiler_params=pltpu.CompilerParams(vmem_limit_bytes=24 * 2**20),
        name="attention_forward",
    )(projected, projected, projected, cos, sin, mask)


def attention_backward_kernel(
    grad_ref, query_ref, key_ref, value_ref, log_ref, cos_ref, sin_ref, mask_ref,
    dq_ref, dk_ref, dv_ref, key_sum, value_sum,
):
    head = pl.program_id(0)
    rows = query_ref.shape[0]
    scale = HEAD_DIMENSION**-0.5

    @pl.when(head == 0)
    def _():
        key_sum[...] = jnp.zeros_like(key_sum)
        value_sum[...] = jnp.zeros_like(value_sum)

    for block in range(rows // TILE):
        top, end = block * TILE, (block + 1) * TILE
        query = query_ref[top:end, :]
        grad = grad_ref[top:end, :]
        scores = dot_nt(query, key_ref[:end, :]) * scale
        scores = jnp.where(mask_ref[top:end, :end] > 0.0, scores, -1e30)
        probs = jnp.exp(scores - log_ref[top:end, 0:1])
        grad_probs = dot_nt(grad, value_ref[:end, :])
        inner = jnp.sum(grad_probs * probs, axis=1, keepdims=True)
        grad_scores = (probs * (grad_probs - inner)).astype(jnp.bfloat16)
        dq = dot_nn(grad_scores, key_ref[:end, :]) * scale
        dq_ref[top:end, :] = (
            dq * cos_ref[top:end, :]
            - pltpu.roll(dq, HEAD_DIMENSION // 2, 1) * sin_ref[top:end, :]
        ).astype(dq_ref.dtype)
        key_sum[:end, :] += dot_tn(grad_scores, query)
        value_sum[:end, :] += dot_tn(probs.astype(jnp.bfloat16), grad)

    @pl.when(head == pl.num_programs(0) - 1)
    def _():
        dk = key_sum[...] * scale
        dk_ref[...] = (
            dk * cos_ref[...] - pltpu.roll(dk, HEAD_DIMENSION // 2, 1) * sin_ref[...]
        ).astype(dk_ref.dtype)
        dv_ref[...] = value_sum[...].astype(dv_ref.dtype)


def attention_backward(grad, query, key, value, logs, cos, sin, mask):
    rows = query.shape[0]
    heads = query.shape[1] // 128
    const2 = lambda i: (0, 0)
    one = pl.BlockSpec((rows, 128), const2)
    each = pl.BlockSpec((rows, 128), lambda i: (0, i))
    b16 = jnp.bfloat16
    return pl.pallas_call(
        attention_backward_kernel,
        grid=(heads,),
        in_specs=[each, each, one, one, each, one, one, pl.BlockSpec((rows, rows), const2)],
        out_specs=[each, one, one],
        out_shape=[
            jax.ShapeDtypeStruct((rows, heads * 128), b16),
            jax.ShapeDtypeStruct((rows, 128), b16),
            jax.ShapeDtypeStruct((rows, 128), b16),
        ],
        scratch_shapes=[pltpu.VMEM((rows, 128), jnp.float32), pltpu.VMEM((rows, 128), jnp.float32)],
        compiler_params=pltpu.CompilerParams(vmem_limit_bytes=24 * 2**20),
        cost_estimate=cost(1, 1),
        name="attention_backward",
    )(grad, query, key, value, logs, cos, sin, mask)


def feed_forward_kernel(
    in_ref, grad_ref, gate_w_ref, up_w_ref, down_ref, act_ref, dgate_ref, dup_ref, din_ref, total
):
    step = pl.program_id(0)

    @pl.when(step == 0)
    def _():
        total[...] = jnp.zeros_like(total)

    gate = dot_nn(in_ref[...], gate_w_ref[...])
    up = dot_nn(in_ref[...], up_w_ref[...])
    grad_act = dot_nn(grad_ref[...], down_ref[...])
    value, slope = silu_parts(gate)
    act_ref[...] = (value * up).astype(act_ref.dtype)
    dgate = (grad_act * up * slope).astype(jnp.bfloat16)
    dup = (grad_act * value).astype(jnp.bfloat16)
    dgate_ref[...] = dgate
    dup_ref[...] = dup
    total[...] += dot_nt(dgate, gate_w_ref[...]) + dot_nt(dup, up_w_ref[...])

    @pl.when(step == pl.num_programs(0) - 1)
    def _():
        din_ref[...] = total[...].astype(din_ref.dtype)


def feed_forward(ffn_in, grad, weights, hidden, tile=512):
    rows, model = grad.shape
    steps = hidden // tile
    each = pl.BlockSpec((rows, tile), lambda i: (0, i))
    whole = pl.BlockSpec((rows, model), lambda i: (0, 0))
    b16 = jnp.bfloat16
    return pl.pallas_call(
        feed_forward_kernel,
        grid=(steps,),
        in_specs=[
            whole,
            whole,
            pl.BlockSpec((model, tile), lambda i: (0, i)),
            pl.BlockSpec((model, tile), lambda i: (0, steps + i)),
            pl.BlockSpec((model, tile), lambda i: (0, 2 * steps + i)),
        ],
        out_specs=[each, each, each, whole],
        out_shape=[
            jax.ShapeDtypeStruct((rows, hidden), b16),
            jax.ShapeDtypeStruct((rows, hidden), b16),
            jax.ShapeDtypeStruct((rows, hidden), b16),
            jax.ShapeDtypeStruct((rows, model), b16),
        ],
        scratch_shapes=[pltpu.VMEM((rows, model), jnp.float32)],
        compiler_params=pltpu.CompilerParams(vmem_limit_bytes=44 * 2**20),
        cost_estimate=cost(1, 1),
        name="feed_forward",
    )(ffn_in, grad, weights, weights, weights)


def norm_back_kernel(
    grad_ref, weight_ref, gated_ref, inverse_ref, gain_ref, dout_ref, dn_ref, row_ref, column_ref, *, split
):
    step = pl.program_id(0)

    @pl.when(step == 0)
    def _():
        row_ref[...] = jnp.zeros_like(row_ref)

    grad = dot_nn(grad_ref[...], weight_ref[...])

    @pl.when(step < split)
    def _():
        dout_ref[...] = grad.astype(dout_ref.dtype)

    @pl.when(step >= split)
    def _():
        dn_ref[...] = grad
        product = grad * gated_ref[...]
        scaled = product * gain_ref[0:1]
        part = scaled[:, :128]
        for k in range(1, scaled.shape[1] // 128):
            part = part + scaled[:, k * 128 : (k + 1) * 128]
        row_ref[...] += part
        total = jnp.sum(product * inverse_ref[:, 0:1], axis=0, keepdims=True)
        column_ref[...] = jnp.broadcast_to(total, column_ref.shape)

    @pl.when(step == pl.num_programs(0) - 1)
    def _():
        row_ref[...] = jnp.broadcast_to(
            jnp.sum(row_ref[...], axis=1, keepdims=True), row_ref.shape
        )


def norm_back(grad, weights, first, attended, gated, inverse, gains, tile=512):
    rows, model = grad.shape
    width = gated.shape[1]
    split = attended // tile
    later = lambda i: (0, jnp.maximum(i - split, 0))
    f32 = jnp.float32
    return pl.pallas_call(
        functools.partial(norm_back_kernel, split=split),
        grid=((attended + width) // tile,),
        in_specs=[
            pl.BlockSpec((rows, model), lambda i: (0, 0)),
            pl.BlockSpec((model, tile), lambda i: (0, first // tile + i)),
            pl.BlockSpec((rows, tile), later),
            pl.BlockSpec((rows, 128), lambda i: (0, 0)),
            pl.BlockSpec((8, tile), later),
        ],
        out_specs=[
            pl.BlockSpec((rows, tile), lambda i: (0, jnp.minimum(i, split - 1))),
            pl.BlockSpec((rows, tile), later),
            pl.BlockSpec((rows, 128), lambda i: (0, 0)),
            pl.BlockSpec((8, tile), later),
        ],
        out_shape=[
            jax.ShapeDtypeStruct((rows, attended), jnp.bfloat16),
            jax.ShapeDtypeStruct((rows, width), f32),
            jax.ShapeDtypeStruct((rows, 128), f32),
            jax.ShapeDtypeStruct((8, width), f32),
        ],
        compiler_params=pltpu.CompilerParams(vmem_limit_bytes=40 * 2**20),
        cost_estimate=cost(1, 1),
        name="norm_back",
    )(grad, weights, gated, inverse, gains)


def reorder_kernel(order_ref, in_ref, out_ref):
    width = in_ref.shape[1] // order_ref.shape[0]
    for place in range(order_ref.shape[0]):
        column = pl.multiple_of(order_ref[place] * width, width)
        out_ref[:, place * width : (place + 1) * width] = in_ref[:, pl.ds(column, width)]


def reorder_columns(values, order):
    rows, model = values.shape
    count = order.shape[0]
    width = model // count
    if width % 128:
        return jnp.take(values.reshape(rows, count, width), order, axis=1).reshape(rows, model)
    return pl.pallas_call(
        reorder_kernel,
        in_specs=[
            pl.BlockSpec(memory_space=pltpu.SMEM),
            pl.BlockSpec(memory_space=pltpu.VMEM),
        ],
        out_specs=pl.BlockSpec(memory_space=pltpu.VMEM),
        out_shape=jax.ShapeDtypeStruct(values.shape, values.dtype),
        compiler_params=pltpu.CompilerParams(vmem_limit_bytes=8 * 2**20),
        cost_estimate=cost(1, 1),
        name="reorder_columns",
    )(order, values)


def widest(width, most):
    return max(t for t in range(128, most + 1, 128) if width % t == 0)


def scatter_part_kernel(left_ref, right_ref, *refs):
    got_refs, out_ref, turned_left = refs[:-2], refs[-2], refs[-1]

    @pl.when(pl.program_id(0) == 0)
    def _():
        turned_left[...] = left_ref[...].T

    total = dot_nn(turned_left[...], right_ref[...])
    for got_ref in got_refs:
        total = total + got_ref[...].astype(jnp.float32)
    out_ref[...] = total.astype(out_ref.dtype)


def scatter_part(left, right, gots, first, size, dtype):
    rows, width = right.shape
    if size % 128 or first % size:
        total = contract("tm,tn->mn", left[:, first : first + size], right)
        for got, start in gots:
            total = total + got[start : start + size].astype(jnp.float32)
        return total.astype(dtype)
    tile = widest(width, 2304 if size <= 256 else 1152)
    return pl.pallas_call(
        scatter_part_kernel,
        grid=(width // tile,),
        in_specs=[
            pl.BlockSpec((rows, size), lambda i: (0, first // size)),
            pl.BlockSpec((rows, tile), lambda i: (0, i)),
        ]
        + [
            pl.BlockSpec((size, tile), lambda i, at=start // size: (at, i)) for unused, start in gots
        ],
        out_specs=pl.BlockSpec((size, tile), lambda i: (0, i)),
        out_shape=jax.ShapeDtypeStruct((size, width), dtype),
        scratch_shapes=[pltpu.VMEM((size, rows), jnp.bfloat16)],
        compiler_params=pltpu.CompilerParams(vmem_limit_bytes=24 * 2**20),
        cost_estimate=cost(1, 1),
        name="scatter_part",
    )(left, right, *[got for got, unused in gots])


def product_back_kernel(left_ref, right_ref, out_ref):
    out_ref[...] = dot_nt(left_ref[...], right_ref[...]).astype(out_ref.dtype)


def product_back(left, right, first, tile=512):
    rows, width = left.shape
    model = right.shape[0]
    return pl.pallas_call(
        product_back_kernel,
        grid=(model // tile,),
        in_specs=[
            pl.BlockSpec((rows, width), lambda i: (0, 0)),
            pl.BlockSpec((tile, width), lambda i: (i, first // width)),
        ],
        out_specs=pl.BlockSpec((rows, tile), lambda i: (0, i)),
        out_shape=jax.ShapeDtypeStruct((rows, model), jnp.bfloat16),
        compiler_params=pltpu.CompilerParams(vmem_limit_bytes=44 * 2**20),
        cost_estimate=cost(1, 1),
        name="product_back",
    )(left, right)


def join_kernel(start, ready_ref, got_ref, out_ref):
    size = ready_ref.shape[0]
    got = got_ref[start : start + size, :].astype(jnp.float32)
    out_ref[...] = (ready_ref[...] + got).astype(out_ref.dtype)


def join_parts(ready, got, start, dtype):
    size, width = ready.shape
    if size % 128 or start % size:
        return (ready + got[start : start + size].astype(jnp.float32)).astype(dtype)
    if size > 256:
        tile = widest(width, 1152)
        return pl.pallas_call(
            functools.partial(join_kernel, 0),
            grid=(width // tile,),
            in_specs=[
                pl.BlockSpec((size, tile), lambda i: (0, i)),
                pl.BlockSpec((size, tile), lambda i: (start // size, i)),
            ],
            out_specs=pl.BlockSpec((size, tile), lambda i: (0, i)),
            out_shape=jax.ShapeDtypeStruct((size, width), dtype),
            compiler_params=pltpu.CompilerParams(vmem_limit_bytes=24 * 2**20),
            cost_estimate=cost(1, 1),
            name="join_parts",
        )(ready, got)
    vmem = pl.BlockSpec(memory_space=pltpu.VMEM)
    return pl.pallas_call(
        functools.partial(join_kernel, start),
        in_specs=[vmem, vmem],
        out_specs=vmem,
        out_shape=jax.ShapeDtypeStruct((size, width), dtype),
        compiler_params=pltpu.CompilerParams(vmem_limit_bytes=16 * 2**20),
        cost_estimate=cost(1, 1),
        name="join_parts",
    )(ready, got)


def rms_back_kernel(value_ref, gain_ref, own_ref, other_ref, base_ref, live_ref, *out_refs):
    values = value_ref[...].astype(jnp.float32)
    gain = gain_ref[0:1]
    grad = own_ref[...].astype(jnp.float32) + other_ref[...].astype(jnp.float32)
    scale = lax.rsqrt(jnp.mean(values * values, axis=1, keepdims=True) + EPS)
    unit = values * scale
    scaled = grad * gain
    pull = jnp.mean(scaled * unit, axis=1, keepdims=True)
    total = base_ref[...].astype(jnp.float32) + (scaled - unit * pull) * scale
    out_refs[0][...] = total
    if len(out_refs) == 3:
        out_refs[2][...] = (total * live_ref[:, 0:1]).astype(jnp.bfloat16)
    gain_grad = jnp.broadcast_to(jnp.sum(grad * unit, axis=0, keepdims=True), out_refs[1].shape)

    @pl.when(pl.program_id(0) == 0)
    def _():
        out_refs[1][...] = gain_grad

    @pl.when(pl.program_id(0) > 0)
    def _():
        out_refs[1][...] += gain_grad


def rms_back(values, gain, own, other, base, live, with_rounded, tile=256):
    rows, model = values.shape
    each = pl.BlockSpec((tile, model), lambda i: (i, 0))
    whole = pl.BlockSpec((8, model), lambda i: (0, 0))
    shapes = [
        jax.ShapeDtypeStruct((rows, model), jnp.float32),
        jax.ShapeDtypeStruct((8, model), jnp.float32),
    ]
    if with_rounded:
        shapes.append(jax.ShapeDtypeStruct((rows, model), jnp.bfloat16))
    return pl.pallas_call(
        rms_back_kernel,
        grid=(rows // tile,),
        in_specs=[each, whole, each, each, each, pl.BlockSpec((tile, 128), lambda i: (i, 0))],
        out_specs=[each, whole, each][: len(shapes)],
        out_shape=shapes,
        compiler_params=pltpu.CompilerParams(vmem_limit_bytes=40 * 2**20),
        cost_estimate=cost(1, 1),
        name="rms_back",
    )(values, gain, own, other, base, live)


def beside_kernel(widths, *refs):
    out_ref, place, refs = refs[-1], 0, list(refs[:-1])
    for width, terms in widths:
        total = refs.pop(0)[...]
        if terms == 2:
            total = total.astype(jnp.float32) + refs.pop(0)[...].astype(jnp.float32)
        out_ref[:, place : place + width] = total.astype(out_ref.dtype)
        place += width
    if place < out_ref.shape[1]:
        out_ref[:, place:] = jnp.zeros((out_ref.shape[0], out_ref.shape[1] - place), out_ref.dtype)


def beside(width, *columns, tile=256):
    groups = [c if isinstance(c, tuple) else (c,) for c in columns]
    widths = tuple((g[0].shape[1], len(g)) for g in groups)
    arrays = [a for g in groups for a in g]
    rows = min(a.shape[0] for a in arrays)
    return pl.pallas_call(
        functools.partial(beside_kernel, widths),
        grid=(rows // tile,),
        in_specs=[pl.BlockSpec((tile, a.shape[1]), lambda i: (i, 0)) for a in arrays],
        out_specs=pl.BlockSpec((tile, width), lambda i: (i, 0)),
        out_shape=jax.ShapeDtypeStruct((rows, width), jnp.bfloat16),
        compiler_params=pltpu.CompilerParams(vmem_limit_bytes=16 * 2**20),
        cost_estimate=cost(1, 1),
        name="beside",
    )(*arrays)


def hidden_back_kernel(
    first_ref, second_ref, third_ref, keep_ref, weight_ref, out_ref, total, *, ends
):
    step = pl.program_id(0)

    @pl.when(step == 0)
    def _():
        total[...] = jnp.zeros_like(total)

    left = jnp.where(
        step < ends[0],
        first_ref[...],
        jnp.where(step < ends[1], second_ref[...], third_ref[...] * keep_ref[0:1]),
    )
    total[...] += dot_nt(left, weight_ref[...])

    @pl.when(step == pl.num_programs(0) - 1)
    def _():
        out_ref[...] = total[...].astype(out_ref.dtype)


def hidden_back(first, second, third, keep, weights, tile=768):
    rows = first.shape[0]
    model = weights.shape[0]
    counts = [part.shape[1] // tile for part in (first, second, third)]
    ends = (counts[0], counts[0] + counts[1])
    block = lambda start, count: pl.BlockSpec(
        (rows, tile), lambda i: (0, jnp.clip(i - start, 0, count - 1))
    )
    return pl.pallas_call(
        functools.partial(hidden_back_kernel, ends=ends),
        grid=(sum(counts),),
        in_specs=[
            block(0, counts[0]),
            block(ends[0], counts[1]),
            block(ends[1], counts[2]),
            pl.BlockSpec((8, tile), lambda i: (0, jnp.clip(i - ends[1], 0, counts[2] - 1))),
            pl.BlockSpec((model, tile), lambda i: (0, i)),
        ],
        out_specs=pl.BlockSpec((rows, model), lambda i: (0, 0)),
        out_shape=jax.ShapeDtypeStruct((rows, model), jnp.bfloat16),
        scratch_shapes=[pltpu.VMEM((rows, model), jnp.float32)],
        compiler_params=pltpu.CompilerParams(vmem_limit_bytes=40 * 2**20),
        cost_estimate=cost(1, 1),
        name="hidden_back",
    )(first, second, third, keep, weights)


def rms_forward_kernel(base_ref, own_ref, other_ref, live_ref, gain_ref, middle_ref, out_ref):
    added = own_ref[...].astype(jnp.float32) + other_ref[...].astype(jnp.float32)
    values = base_ref[...].astype(jnp.float32) + added * live_ref[:, 0:1]
    middle_ref[...] = values
    scale = lax.rsqrt(jnp.mean(values * values, axis=1, keepdims=True) + EPS)
    out_ref[...] = (values * scale * gain_ref[0:1]).astype(out_ref.dtype)


def rms_forward(base, own, other, live, gain, tile=256):
    rows, model = base.shape
    each = pl.BlockSpec((tile, model), lambda i: (i, 0))
    return pl.pallas_call(
        rms_forward_kernel,
        grid=(rows // tile,),
        in_specs=[
            each,
            each,
            each,
            pl.BlockSpec((tile, 128), lambda i: (i, 0)),
            pl.BlockSpec((8, model), lambda i: (0, 0)),
        ],
        out_specs=[each, each],
        out_shape=[
            jax.ShapeDtypeStruct((rows, model), jnp.float32),
            jax.ShapeDtypeStruct((rows, model), jnp.bfloat16),
        ],
        compiler_params=pltpu.CompilerParams(vmem_limit_bytes=28 * 2**20),
        cost_estimate=cost(1, 1),
        name="rms_forward",
    )(base, own, other, live, gain)


def output_kernel(base_ref, own_ref, other_ref, live_ref, out_ref):
    added = own_ref[...].astype(jnp.float32) + other_ref[...].astype(jnp.float32)
    out_ref[...] = (base_ref[...] + added * live_ref[:, 0:1]).astype(out_ref.dtype)


def output_rows(base, own, other, live, tile=256):
    rows, model = base.shape
    each = pl.BlockSpec((tile, model), lambda i: (i, 0))
    return pl.pallas_call(
        output_kernel,
        grid=(rows // tile,),
        in_specs=[each, each, each, pl.BlockSpec((tile, 128), lambda i: (i, 0))],
        out_specs=each,
        out_shape=jax.ShapeDtypeStruct((rows, model), jnp.bfloat16),
        compiler_params=pltpu.CompilerParams(vmem_limit_bytes=24 * 2**20),
        cost_estimate=cost(1, 1),
        name="output_rows",
    )(base, own, other, live)


def stack_kernel(layout, *refs):
    out_ref, place, refs = refs[-1], 0, list(refs[:-1])
    out_ref[...] = jnp.zeros_like(out_ref)
    for start, count, terms in layout:
        total = refs.pop(0)[start : start + count, :].astype(jnp.float32)
        if terms == 2:
            total = total + refs.pop(0)[start : start + count, :].astype(jnp.float32)
        out_ref[place : place + count, : total.shape[1]] = total
        place += count


def stack_rows(width, *parts):
    layout = tuple((start, count, len(arrays)) for arrays, start, count in parts)
    total = -(-sum(count for unused, count, terms in layout) // 8) * 8
    vmem = pl.BlockSpec(memory_space=pltpu.VMEM)
    arrays = [array for arrays, start, count in parts for array in arrays]
    return pl.pallas_call(
        functools.partial(stack_kernel, layout),
        in_specs=[vmem] * len(arrays),
        out_specs=vmem,
        out_shape=jax.ShapeDtypeStruct((total, width), jnp.float32),
        compiler_params=pltpu.CompilerParams(vmem_limit_bytes=8 * 2**20),
        cost_estimate=cost(1, 1),
        name="stack_rows",
    )(*arrays)


def add_kernel(left_ref, right_ref, out_ref):
    out_ref[...] = left_ref[...] + right_ref[...]


def add_rows(left, right):
    vmem = pl.BlockSpec(memory_space=pltpu.VMEM)
    return pl.pallas_call(
        add_kernel,
        in_specs=[vmem, vmem],
        out_specs=vmem,
        out_shape=jax.ShapeDtypeStruct(left.shape, left.dtype),
        compiler_params=pltpu.CompilerParams(vmem_limit_bytes=8 * 2**20),
        cost_estimate=cost(1, 1),
        name="add_rows",
    )(left, right)


def turn_kernel(in_ref, out_ref):
    out_ref[...] = in_ref[...].T


def turned_copy(values, tile=512):
    rows, width = values.shape
    return pl.pallas_call(
        turn_kernel,
        grid=(width // tile,),
        in_specs=[pl.BlockSpec((rows, tile), lambda i: (0, i))],
        out_specs=pl.BlockSpec((tile, rows), lambda i: (i, 0)),
        out_shape=jax.ShapeDtypeStruct((width, rows), values.dtype),
        compiler_params=pltpu.CompilerParams(vmem_limit_bytes=8 * 2**20),
        cost_estimate=cost(1, 1),
        name="turned_copy",
    )(values)


def tie(*values):
    return lax.optimization_barrier(values)


def pair_swap(values):
    return lax.ppermute(values, "tensor", [(0, 1), (1, 0)])


def pair_sum(values):
    own = lax.reduce_precision(values.astype(jnp.float32), 8, 7)
    return own + pair_swap(own.astype(jnp.bfloat16)).astype(jnp.float32)


def pair_join(values):
    other = pair_swap(values)
    first = lax.axis_index("tensor") == 0
    return jnp.concatenate(
        [jnp.where(first, values, other), jnp.where(first, other, values)], axis=0
    )


def after(values, *earlier):
    return lax.optimization_barrier((values, *earlier))[0]


def bits_of(count):
    return tuple(1 << place for place in range(count.bit_length() - 1))


def owner_order(bits):
    offsets = [0]
    for bit in reversed(bits):
        offsets = [offset | bit for offset in offsets] + offsets
    return lax.axis_index("dp") ^ jnp.array(offsets, jnp.int32)


def across(values, bit):
    count = lax.axis_size("dp")
    return lax.ppermute(values, "dp", [(i, i ^ bit) for i in range(count)])


class Scatter:
    def __init__(self, left, right, bits):
        self.left, self.right, self.bits = left, right, bits
        self.rows = left.shape[1] // 2 ** len(bits)
        self.got = []
        self.total = None

    def place(self, step):
        count = 2 ** len(self.bits)
        return count - (count >> step), max(count >> (step + 1), 1)

    def meets(self, past, step):
        return (self.place(step)[0] - self.place(past + 1)[0]) * self.rows

    def begin(self, *earlier):
        first, size = self.place(0)
        left = after(self.left, *earlier)
        self.held = scatter_part(left, self.right, [], 0, size * self.rows, jnp.bfloat16)
        return self.held

    def send(self, *earlier):
        self.got.append(across(after(self.held, *earlier), self.bits[len(self.got)]))
        return self.got[-1]

    def prepare(self, *earlier):
        step = len(self.got)
        first, size = self.place(step)
        gots = [(got, self.meets(past, step)) for past, got in enumerate(self.got[:-1])]
        left = after(self.left, *earlier)
        self.ready = scatter_part(
            left, self.right, gots, first * self.rows, size * self.rows, jnp.float32
        )
        return self.ready

    def make(self, *earlier):
        step = len(self.got)
        first, size = self.place(step)
        gots = [(got, self.meets(past, step)) for past, got in enumerate(self.got)]
        done = step == len(self.bits)
        self.held = scatter_part(
            after(self.left, *earlier),
            self.right,
            gots,
            first * self.rows,
            size * self.rows,
            jnp.float32 if done else jnp.bfloat16,
        )
        if done:
            self.total = self.held
        return self.held

    def join(self, *earlier):
        step = len(self.got)
        done = step == len(self.bits)
        self.held = join_parts(
            after(self.ready, *earlier),
            self.got[-1],
            self.meets(step - 1, step),
            jnp.float32 if done else jnp.bfloat16,
        )
        if done:
            self.total = self.held
        return self.held

    def finish(self):
        while self.total is None:
            self.send()
            self.make()
        return self.total


def side_by_side(first, second):
    return with_layout_constraint(
        jnp.stack([first, second], axis=1), Layout(major_to_minor=(0, 1, 2))
    )


def local(
    tokens,
    cotangent,
    segment_ids,
    counts,
    mixer_gain,
    query_proj,
    key_value_matrix,
    attend_proj,
    inner_proj,
    state_proj,
    step_proj,
    conv_inner,
    conv_state,
    step_bias,
    decay_log,
    skip_gain,
    gated_gain,
    mamba_proj,
    dense_gain,
    gateup_proj,
    down_proj,
):
    row_count, model_width = tokens.shape
    shard_rows = query_proj.shape[0]
    dp_count = lax.axis_size("dp")
    bf16, f32 = jnp.bfloat16, jnp.float32
    heads_m = step_proj.shape[1]
    heads_q = query_proj.shape[1] // HEAD_DIMENSION
    q_cols = query_proj.shape[1]
    kv_cols = 2 * key_value_matrix.shape[2]
    x_cols = inner_proj.shape[2]
    state_cols = state_proj.shape[1]
    o_cols = attend_proj.shape[0]
    hidden_cols = gateup_proj.shape[2]
    tap_count = conv_state.shape[0]
    pair_width = conv_state.shape[1]

    small = jnp.concatenate(
        [
            jnp.concatenate([mixer_gain, dense_gain])[None],
            jnp.pad(conv_state, ((0, 0), (0, 2 * mixer_gain.shape[0] - pair_width))),
        ],
        axis=0,
    )
    state_rows_full = pair_join(state_proj)
    small_pair = pair_join(small[None])
    gain_half = mixer_gain.shape[0]
    small_rows = jnp.concatenate(
        [
            small_pair[:, 0, :gain_half].reshape(1, -1),
            small_pair[:, 0, gain_half:].reshape(1, -1),
            jnp.pad(
                jnp.concatenate([small_pair[0, 1:, :pair_width], small_pair[1, 1:, :pair_width]], axis=1),
                ((0, 0), (0, shard_rows - 2 * pair_width)),
            ),
        ],
        axis=0,
    )
    small_block = jnp.pad(
        small_rows, ((0, shard_rows - small_rows.shape[0]), (0, 128 - shard_rows))
    )
    step_pad = jnp.zeros((shard_rows, 128 - heads_m), bf16)
    group_mix = jnp.concatenate(
        [
            inner_proj[:, 0],
            query_proj,
            key_value_matrix.reshape(shard_rows, -1),
            inner_proj[:, 1],
            state_rows_full,
            step_proj,
            step_pad,
            small_block,
            attend_proj.T,
            mamba_proj.T,
        ],
        axis=1,
    )
    offsets, place = {}, 0
    for name, width in (
        ("z", x_cols),
        ("q", q_cols),
        ("kv", kv_cols),
        ("u", x_cols),
        ("state", state_cols),
        ("step", 128),
        ("end", 0),
    ):
        offsets[name] = place
        place += width
    out_first = offsets["end"] + 128
    group_ffn = jnp.concatenate([gateup_proj.reshape(shard_rows, -1), down_proj.T], axis=1)
    mix_full = lax.all_gather(group_mix, "dp", axis=0, tiled=True)
    ffn_full = lax.all_gather(after(group_ffn, mix_full), "dp", axis=0, tiled=True)
    out_t = mix_full[:, out_first:]
    down_t = ffn_full[:, 2 * hidden_cols :]

    small_full = mix_full[:, offsets["end"] : out_first]
    w_proj = mix_full[:, : offsets["end"]]
    small_full = small_full.reshape(dp_count, shard_rows, 128)
    gain_mix = small_full[:, 0, :shard_rows].reshape(-1).astype(f32)
    gain_dense = small_full[:, 1, :shard_rows].reshape(-1).astype(f32)
    conv_full = small_full[:, 2 : 2 + tap_count, : 2 * pair_width].astype(f32)
    conv_full = jnp.swapaxes(conv_full, 0, 1).reshape(tap_count, -1)
    conv_full = jnp.concatenate([conv_full, jnp.zeros((8 - tap_count, state_cols), f32)], axis=0)
    gain_gated = gated_gain.astype(f32)
    wide = jnp.concatenate(
        [
            conv_inner.astype(f32),
            jnp.repeat(skip_gain.astype(f32), HP)[None],
            gain_gated[None],
            jnp.zeros((1, x_cols), f32),
        ],
        axis=0,
    )
    extra = jnp.zeros((8, 128), f32)
    extra = extra.at[0, :heads_m].set(step_bias.astype(f32))
    extra = extra.at[1, :heads_m].set(jnp.exp(decay_log.astype(f32)))

    row_index = jnp.arange(row_count, dtype=jnp.int32)
    valid_rows = (row_index < counts[0]).astype(f32)[:, None]
    live = jnp.broadcast_to(valid_rows, (row_count, 128))
    position = positions_of(segment_ids)
    causal = (row_index[None, :] <= row_index[:, None]) & (
        segment_ids[None, :] == segment_ids[:, None]
    )
    mask = causal.astype(f32)
    mask_t = (
        (row_index[None, :] >= row_index[:, None]) & (segment_ids[None, :] == segment_ids[:, None])
    ).astype(f32)
    mask_qk = (causal & (row_index[None, :] < counts[0])).astype(f32)
    same = jnp.stack(
        [
            jnp.broadcast_to(((row_index >= lag) & (position >= lag)).astype(f32)[:, None], live.shape)
            for lag in range(1, tap_count - 1)
        ]
    )
    half = HEAD_DIMENSION // 2
    frequency = jnp.exp(
        jnp.arange(half, dtype=f32) * (-2.0 * math.log(THETA) / HEAD_DIMENSION)
    )
    angles = position.astype(f32)[:, None] * frequency[None, :]
    cos = jnp.cos(angles)
    sin = jnp.sin(angles)
    cos = jnp.concatenate([cos, cos], axis=1)
    sin = jnp.concatenate([-sin, sin], axis=1)
    bits = bits_of(dp_count)
    order = owner_order(bits)
    stream = tokens.astype(f32)
    upstream = cotangent.astype(f32)
    dense_grad_b = rounded(upstream * valid_rows)
    dense_split = reorder_columns(dense_grad_b, order)

    gain_dense_rows = jnp.broadcast_to(gain_dense[None], (8, model_width))
    gain_mix_rows = jnp.broadcast_to(gain_mix[None], (8, model_width))

    hidden_b = rounded(rms_scale(stream, gain_mix))
    projected = contract("td,dc->tc", hidden_b, w_proj)
    hidden_split = reorder_columns(hidden_b, order)
    mixed, gated, squares = ssm_forward(
        projected, wide, conv_full, extra, live, same, mask, offsets
    )
    own_squares = jnp.sum(squares, axis=-1)
    other_squares = pair_swap(own_squares)
    attended_b, query_b, key_b, value_b, logs = attention_forward(
        projected, cos, sin, mask_qk, offsets, heads_q
    )
    inverse = lax.rsqrt((own_squares + other_squares) / DSSM + EPS)
    normed_b = rounded(gated * inverse[:, None] * gain_gated)
    branch_in = jnp.concatenate([attended_b, normed_b], axis=1)
    branch_own = rounded(contract("tc,dc->td", branch_in, out_t))
    branch_other = pair_swap(branch_own)
    middle, ffn_in_b = rms_forward(tokens, branch_own, branch_other, live, gain_dense_rows)
    inverse_b = jnp.broadcast_to(inverse[:, None], live.shape)
    gated_rows = jnp.broadcast_to(gain_gated[None], (8, x_cols))
    first = (lax.axis_index("tensor") == 0).astype(bf16)
    last_cols = offsets["end"] + 128 - offsets["state"]
    keep = jnp.where(jnp.arange(last_cols) < state_cols, first, jnp.ones((), bf16))
    keep = jnp.broadcast_to(keep[None], (8, last_cols))
    ffn_split = reorder_columns(ffn_in_b, order)

    activated_b, grad_gate_b, grad_up_b, grad_ffn_part = feed_forward(
        ffn_in_b, after(dense_grad_b, ffn_split, dense_split), ffn_full, hidden_cols
    )
    down = Scatter(dense_split, activated_b, bits)
    gate_sum = Scatter(ffn_split, grad_gate_b, bits)
    up_sum = Scatter(ffn_split, grad_up_b, bits)
    held = down.begin()
    down.send()
    held = gate_sum.begin(held)
    ready = down.prepare(held)

    held = down.join(ready)
    down.send()
    grad_ffn_other = pair_swap(after(grad_ffn_part, ready))
    gate_sum.send(ready)
    held = up_sum.begin(held)
    ready = down.prepare(held)
    dense_own = product_back(after(activated_b, ready), ffn_full, 2 * hidden_cols)
    ready = gate_sum.prepare(dense_own)

    round_end = (ready, down.got[-1], gate_sum.got[-1], grad_ffn_other)
    held = gate_sum.join(*round_end)
    gate_sum.send()
    up_sum.send(*round_end)
    held = down.make(held)
    down.send()
    grad_middle, grad_dense_gain, mixer_grad_b = rms_back(
        middle, gain_dense_rows, after(grad_ffn_part, held), grad_ffn_other, cotangent, live, True
    )
    grad_attended_b, grad_normed, own_rows, column_part = norm_back(
        mixer_grad_b, mix_full, out_first, o_cols, gated, inverse_b, gated_rows
    )
    other_rows = pair_swap(own_rows)
    branch = Scatter(reorder_columns(mixer_grad_b, order), branch_in, bits)
    held = branch.begin(own_rows)
    ready = up_sum.prepare(held)
    grad_query_b, grad_key_b, grad_value_b = attention_backward(
        after(grad_attended_b, ready), query_b, key_b, value_b, logs, cos, sin, mask_qk
    )
    ready = grad_query_b

    round_end = (ready, gate_sum.got[-1], up_sum.got[-1], down.got[-1], other_rows)
    held = up_sum.join(*round_end)
    up_sum.send()
    branch.send(*round_end)
    held = gate_sum.make(held)
    gate_sum.send()
    held = down.make(held)
    down.send()
    dense_other = pair_swap(after(dense_own, *round_end))
    grad_z_b, grad_u_b, grad_state_part, grad_step_b, wide_grad, extra_grad = (
        ssm_backward(
            after(grad_normed, held),
            mixed,
            projected,
            inverse_b,
            own_rows,
            other_rows,
            wide,
            conv_full,
            extra,
            live,
            same,
            mask_t,
            offsets,
        )
    )
    head_cols = x_cols + q_cols + kv_cols
    head_b = beside(head_cols, grad_z_b, grad_query_b, grad_key_b, grad_value_b)
    z_sum = Scatter(hidden_split, head_b, bits)
    u_sum = Scatter(hidden_split, grad_u_b, bits)
    held = z_sum.begin(grad_state_part)
    ready = branch.prepare(held)

    round_end = (ready, up_sum.got[-1], gate_sum.got[-1], branch.got[-1], down.got[-1], dense_other)
    held = branch.join(*round_end)
    branch.send()
    z_sum.send(*round_end)
    grad_state_other = pair_swap(after(grad_state_part, *round_end))
    held = up_sum.make(held)
    up_sum.send()
    held = gate_sum.make(held)
    gate_sum.send()
    held = u_sum.begin(held)
    other_b = beside(last_cols, (grad_state_part, after(grad_state_other, held)), grad_step_b)
    other_sum = Scatter(hidden_split, other_b, bits)
    grad_hidden_own = hidden_back(after(head_b, other_b), grad_u_b, other_b, keep, mix_full)
    held = other_sum.begin(grad_hidden_own)
    ready = z_sum.prepare(held)

    round_end = (ready, branch.got[-1], up_sum.got[-1], gate_sum.got[-1], z_sum.got[-1])
    held = z_sum.join(*round_end)
    z_sum.send()
    u_sum.send(*round_end)
    grad_hidden_other = pair_swap(after(grad_hidden_own, *round_end))
    held = branch.make(held)
    branch.send()
    held = up_sum.make(held)
    up_sum.send()
    held = gate_sum.make(held)
    held = down.make(held)
    red_down = turned_copy(after(down.finish(), held))
    output = output_rows(middle, after(dense_own, red_down), dense_other, live)
    ready = u_sum.prepare(output)
    ready = z_sum.prepare(ready)
    ready = branch.prepare(ready)
    ready = up_sum.prepare(ready)

    round_end = (ready, z_sum.got[-1], u_sum.got[-1], branch.got[-1], up_sum.got[-1], grad_hidden_other)
    held = u_sum.join(*round_end)
    u_sum.send()
    other_sum.send(*round_end)
    held = z_sum.join(held)
    z_sum.send()
    held = branch.join(held)
    branch.send()
    held = up_sum.join(held)
    red_gateup = side_by_side(after(gate_sum.finish(), held), up_sum.finish())
    grad_tokens, grad_mixer_gain = rms_back(
        tokens, gain_mix_rows, after(grad_hidden_own, red_gateup), grad_hidden_other, grad_middle, live, False
    )
    own_sums = stack_rows(
        model_width,
        ((grad_mixer_gain,), 0, 1),
        ((grad_dense_gain,), 0, 1),
        ((wide_grad,), 0, tap_count + 1),
        ((column_part,), 0, 1),
        ((grad_state_part, grad_state_other), row_count, tap_count),
        ((extra_grad,), 0, 2),
    )
    sums = add_rows(own_sums, across(own_sums, bits[0]))
    ready = other_sum.prepare(sums)
    ready = u_sum.prepare(ready)
    ready = z_sum.prepare(ready)
    ready = branch.prepare(ready)

    round_end = (ready, u_sum.got[-1], other_sum.got[-1], z_sum.got[-1], branch.got[-1])
    held = other_sum.join(*round_end)
    other_sum.send()
    held = u_sum.join(held)
    u_sum.send()
    others = across(after(sums, *round_end), bits[1])
    held = z_sum.join(held)
    z_sum.send()
    held = branch.join(held)
    red_branch = branch.finish()
    red_attend = turned_copy(after(red_branch[:, :o_cols], held))
    red_mamba = turned_copy(after(red_branch[:, o_cols:], red_attend))
    ready = other_sum.prepare(red_mamba)
    ready = u_sum.prepare(ready)
    ready = z_sum.prepare(ready)

    round_end = (ready, other_sum.got[-1], u_sum.got[-1], z_sum.got[-1], others)
    held = other_sum.join(*round_end)
    other_sum.send()
    sums = add_rows(after(sums, held), others)
    others = across(sums, bits[2])
    held = u_sum.join(sums)
    u_sum.send()
    held = z_sum.join(held)
    ready = other_sum.prepare(held)
    ready = u_sum.prepare(ready)

    held = other_sum.join(ready, other_sum.got[-1], u_sum.got[-1], others)
    other_sum.send()
    sums = add_rows(after(sums, held), others)
    others = across(sums, bits[3])
    held = u_sum.join(sums)
    ready = other_sum.prepare(held)
    held = other_sum.join(ready)
    red_head = after(z_sum.finish(), held)
    red_inner = side_by_side(red_head[:, :x_cols], u_sum.finish())
    sums = add_rows(after(sums, held), others)
    for bit in bits[4:]:
        sums = add_rows(sums, across(sums, bit))
    at = 2 + tap_count + 2
    conv_sum = sums[at : at + tap_count, :state_cols]
    at += tap_count
    skip_sum = jnp.sum(sums[2 + tap_count, :x_cols].reshape(heads_m, HP), axis=1)
    owner = lax.axis_index("dp") * 2 + lax.axis_index("tensor")

    def own_part(values, axis_dim):
        width = values.shape[axis_dim] // (2 * dp_count)
        return lax.dynamic_slice_in_dim(values, owner * width, width, axis_dim)

    red_other = other_sum.finish()
    state_rows = shard_rows // 2
    red_state = lax.dynamic_slice_in_dim(
        red_other[:, :state_cols], lax.axis_index("tensor") * state_rows, state_rows, 0
    )
    kv_first = x_cols + q_cols
    return (
        output,
        grad_tokens,
        own_part(sums[0], 0),
        red_head[:, x_cols:kv_first],
        red_head[:, kv_first:].reshape(shard_rows, 2, -1),
        red_attend,
        red_inner,
        red_state,
        red_other[:, state_cols : state_cols + heads_m],
        sums[2 : 2 + tap_count, :x_cols],
        own_part(conv_sum, 1),
        sums[at, :heads_m],
        sums[at + 1, :heads_m],
        skip_sum,
        sums[3 + tap_count, :x_cols],
        red_mamba,
        own_part(sums[1], 0),
        red_gateup,
        red_down,
    )


def solution(mesh):
    placed = (
        P("dp", None),
        P("dp", None),
        P("dp"),
        P("dp"),
        P(("dp", "tensor")),
        P("dp", "tensor"),
        P("dp", None, "tensor"),
        P("tensor", "dp"),
        P("dp", None, "tensor"),
        P(("dp", "tensor"), None),
        P("dp", "tensor"),
        P(None, "tensor"),
        P(None, ("dp", "tensor")),
        P("tensor"),
        P("tensor"),
        P("tensor"),
        P("tensor"),
        P("tensor", "dp"),
        P(("dp", "tensor")),
        P("dp", None, "tensor"),
        P("tensor", "dp"),
    )
    return jax.shard_map(
        local,
        mesh=mesh,
        in_specs=placed,
        out_specs=(
            P("dp", None),
            P("dp", None),
            P(("dp", "tensor")),
            P("dp", "tensor"),
            P("dp", None, "tensor"),
            P("tensor", "dp"),
            P("dp", None, "tensor"),
            P(("dp", "tensor"), None),
            P("dp", "tensor"),
            P(None, "tensor"),
            P(None, ("dp", "tensor")),
            P("tensor"),
            P("tensor"),
            P("tensor"),
            P("tensor"),
            P("tensor", "dp"),
            P(("dp", "tensor")),
            P("dp", None, "tensor"),
            P("tensor", "dp"),
        ),
        check_vma=False,
    )
```

```python
import functools
import math

import jax
import jax.numpy as jnp
from jax import lax
from jax.experimental import pallas as pl
from jax.experimental.pallas import tpu as pltpu
from jax.experimental.layout import Layout, with_layout_constraint
from jax.sharding import PartitionSpec as P

HP = 64
HEAD_DIMENSION = 128
DSSM = 3072
TILE = 256

EPS = 1e-05
THETA = 100000000000.0


def rounded(values):
    return values.astype(jnp.bfloat16)


def contract(form, left, right):
    return jnp.einsum(form, left, right, preferred_element_type=jnp.float32)


def rms_scale(values, gain):
    return values * lax.rsqrt(jnp.mean(values * values, axis=-1, keepdims=True) + EPS) * gain


def cost(flops, traffic, transcendentals=0):
    return pl.CostEstimate(
        flops=flops, bytes_accessed=traffic, transcendentals=transcendentals
    )


def positions_of(segment):
    row_index = jnp.arange(segment.shape[0], dtype=jnp.int32)
    starts = jnp.concatenate([jnp.ones((1,), jnp.bool_), segment[1:] != segment[:-1]])
    first_row = lax.cummax(jnp.where(starts, row_index, 0), axis=0)
    return row_index - first_row


def silu_parts(values):
    gate = jax.nn.sigmoid(values)
    return values * gate, gate * (1.0 + values * (1.0 - gate))


def dot_nn(left, right):
    return lax.dot_general(left, right, (((1,), (0,)), ((), ())), preferred_element_type=jnp.float32)


def dot_nt(left, right):
    return lax.dot_general(left, right, (((1,), (1,)), ((), ())), preferred_element_type=jnp.float32)


def dot_tn(left, right):
    return lax.dot_general(left, right, (((0,), (0,)), ((), ())), preferred_element_type=jnp.float32)


def shifted_rows(values, lag, same_ref):
    columns = values.shape[1]
    mask = same_ref[lag - 1]
    if columns > mask.shape[1]:
        mask = jnp.concatenate([mask] * (columns // mask.shape[1]), axis=1)
    return mask * pltpu.roll(values, lag, 0)


def conv_rows(values, taps, same_ref):
    total = taps[4:5] + taps[3:4] * values
    for lag in range(1, 4):
        total = total + taps[3 - lag : 4 - lag] * shifted_rows(values, lag, same_ref)
    return total


def conv_rows_back(grad, values, taps, same_ref):
    rows = grad.shape[0]
    total = taps[3:4] * grad
    tap_grads = [None] * 5
    tap_grads[4] = jnp.sum(grad, axis=0, keepdims=True)
    tap_grads[3] = jnp.sum(grad * values, axis=0, keepdims=True)
    for lag in range(1, 4):
        mask = same_ref[lag - 1]
        if grad.shape[1] > mask.shape[1]:
            mask = jnp.concatenate([mask] * (grad.shape[1] // mask.shape[1]), axis=1)
        masked = grad * mask
        total = total + taps[3 - lag : 4 - lag] * pltpu.roll(masked, rows - lag, 0)
        tap_grads[3 - lag] = jnp.sum(
            masked * pltpu.roll(values, lag, 0), axis=0, keepdims=True
        )
    return total, tap_grads


def running_sum(values, backward=False):
    rows = values.shape[0]
    index = lax.broadcasted_iota(jnp.int32, values.shape, 0)
    step = 1
    while step < rows:
        if backward:
            moved = pltpu.roll(values, rows - step, 0)
            values = values + jnp.where(index < rows - step, moved, 0.0)
        else:
            moved = pltpu.roll(values, step, 0)
            values = values + jnp.where(index >= step, moved, 0.0)
        step *= 2
    return values


def step_sizes(raw, extra_ref, live):
    shifted = raw + extra_ref[0:1]
    size = (jnp.maximum(shifted, 0.0) + jnp.log1p(jnp.exp(-jnp.abs(shifted)))) * live
    return shifted, size, -size * extra_ref[1:2]


def lane_column(values, lane):
    lanes = lax.broadcasted_iota(jnp.int32, values.shape, 1)
    return jnp.sum(jnp.where(lanes == lane, values, 0.0), axis=1, keepdims=True)


def head_sums(values, pair):
    lanes = lax.broadcasted_iota(jnp.int32, (128, 128), 0)
    heads = lax.broadcasted_iota(jnp.int32, (128, 128), 1)
    chosen = (heads == 2 * pair + lanes // HP).astype(jnp.bfloat16)
    high = values.astype(jnp.bfloat16)
    low = (values - high.astype(jnp.float32)).astype(jnp.bfloat16)
    return dot_nn(jnp.concatenate([high, low], axis=1), jnp.concatenate([chosen, chosen], axis=0))


def ssm_forward_kernel(
    u_ref, z_ref, state_b_ref, state_c_ref, step_ref, wide_ref, conv_ref, extra_ref, live_ref, same_ref, mask_ref,
    y_ref, gated_ref, square_ref, gram, sizes, running, running_t,
):
    step = pl.program_id(0)
    live = live_ref[...]
    rows = live.shape[0]

    @pl.when(step == 0)
    def _():
        unused, size, decay = step_sizes(step_ref[...], extra_ref, live)
        total = running_sum(decay)
        sizes[...] = size
        running[...] = total
        running_t[...] = total.T
        width = conv_ref.shape[1]
        wide_live = jnp.concatenate([live] * (width // 128), axis=1)
        state = jnp.concatenate([state_b_ref[...], state_c_ref[...]], axis=1) * wide_live
        inner = conv_rows(state, conv_ref[...], same_ref)
        both = (inner * jax.nn.sigmoid(inner)).astype(jnp.bfloat16)
        gram[...] = dot_nt(both[:, width // 2 :], both[:, : width // 2]) * mask_ref[...]
        square_ref[...] = jnp.zeros_like(square_ref)

    for part in range(2):
        pair = 2 * step + part
        at = slice(part * 128, (part + 1) * 128)
        taps = wide_ref[:, at]
        inner = conv_rows(u_ref[:, at] * live, taps, same_ref)
        x_in = inner * jax.nn.sigmoid(inner)
        left_lanes = lax.broadcasted_iota(jnp.int32, (rows, 128), 1) < HP
        size = sizes[...]
        size_pair = jnp.where(left_lanes, lane_column(size, 2 * pair), lane_column(size, 2 * pair + 1))
        inflow = (size_pair * x_in).astype(jnp.bfloat16)
        total = running[...]
        columns = [lane_column(total, 2 * pair + k) for k in range(2)]
        row_vectors = [running_t[pl.ds(2 * pair + k, 1), :] for k in range(2)]
        skipped = taps[5:6] * x_in
        gate = z_ref[:, at]
        gate = gate * jax.nn.sigmoid(gate)
        for block in range(rows // TILE):
            top, end = block * TILE, (block + 1) * TILE
            parts = []
            for k in range(2):
                gaps = columns[k][top:end] - row_vectors[k][:, :end]
                mixing = (gram[top:end, :end] * jnp.exp(jnp.minimum(gaps, 0.0))).astype(jnp.bfloat16)
                parts.append(dot_nn(mixing, inflow[:end]))
            mixed = jnp.where(left_lanes[top:end], parts[0], parts[1]) + skipped[top:end]
            y_ref[top:end, at] = mixed
            gated = mixed * gate[top:end]
            gated_ref[top:end, at] = gated
            square_ref[top:end, :] += gated * gated


def ssm_forward(projected, wide, conv_state, extra, live, same, mask, offsets):
    rows = projected.shape[0]
    pairs = wide.shape[1] // 128
    width = conv_state.shape[1]
    const2 = lambda i: (0, 0)
    at = lambda name, size: offsets[name] // size
    block = lambda name: pl.BlockSpec((rows, 128 * 2), lambda i, o=at(name, 128 * 2): (0, o + i))
    return pl.pallas_call(
        ssm_forward_kernel,
        grid=(pairs // 2,),
        in_specs=[
            block("u"),
            block("z"),
            pl.BlockSpec((rows, width // 2), lambda i: (0, at("state", width // 2))),
            pl.BlockSpec((rows, width // 2), lambda i: (0, at("state", width // 2) + 1)),
            pl.BlockSpec((rows, 128), lambda i: (0, at("step", 128))),
            pl.BlockSpec((8, 128 * 2), lambda i: (0, i)),
            pl.BlockSpec((8, width), const2),
            pl.BlockSpec((8, 128), const2),
            pl.BlockSpec((rows, 128), const2),
            pl.BlockSpec((3, rows, 128), lambda i: (0, 0, 0)),
            pl.BlockSpec((rows, rows), const2),
        ],
        out_specs=[
            pl.BlockSpec((rows, 128 * 2), lambda i: (0, i)),
            pl.BlockSpec((rows, 128 * 2), lambda i: (0, i)),
            pl.BlockSpec((rows, 128), const2),
        ],
        out_shape=[
            jax.ShapeDtypeStruct((rows, pairs * 128), jnp.float32),
            jax.ShapeDtypeStruct((rows, pairs * 128), jnp.float32),
            jax.ShapeDtypeStruct((rows, 128), jnp.float32),
        ],
        scratch_shapes=[
            pltpu.VMEM((rows, rows), jnp.float32),
            pltpu.VMEM((rows, 128), jnp.float32),
            pltpu.VMEM((rows, 128), jnp.float32),
            pltpu.VMEM((128, rows), jnp.float32),
        ],
        compiler_params=pltpu.CompilerParams(vmem_limit_bytes=28 * 2**20),
        name="ssm_forward",
    )(projected, projected, projected, projected, projected, wide, conv_state, extra, live, same, mask)


def ssm_backward_kernel(
    dn_ref, y_ref, u_ref, z_ref, state_b_ref, state_c_ref, step_ref, inverse_ref, own_ref, other_ref,
    wide_ref, conv_ref, extra_ref, live_ref, same_ref, mask_t_ref,
    dz_ref, du_ref, ds_ref, dr_ref, wide_grad_ref, extra_grad_ref,
    gram_t, gram_grad, sizes, decays, running, running_t, size_grad, total_grad, states, state_slopes,
):
    step = pl.program_id(0)
    live = live_ref[...]
    rows = live.shape[0]
    width = conv_ref.shape[1]
    wide_live = jnp.concatenate([live] * (width // 128), axis=1)

    @pl.when(step == 0)
    def _():
        unused, size, decay = step_sizes(step_ref[...], extra_ref, live)
        total = running_sum(decay)
        sizes[...] = size
        decays[...] = decay
        running[...] = total
        running_t[...] = total.T
        state = jnp.concatenate([state_b_ref[...], state_c_ref[...]], axis=1) * wide_live
        inner = conv_rows(state, conv_ref[...], same_ref)
        value, slope = silu_parts(inner)
        both = value.astype(jnp.bfloat16)
        states[...] = both
        state_slopes[...] = slope
        gram_t[...] = dot_nt(both[:, : width // 2], both[:, width // 2 :]) * mask_t_ref[...]
        gram_grad[...] = jnp.zeros_like(gram_grad)
        size_grad[...] = jnp.zeros_like(size_grad)
        total_grad[...] = jnp.zeros_like(total_grad)

    for part in range(2):
        pair = 2 * step + part
        at = slice(part * 128, (part + 1) * 128)
        taps = wide_ref[:, at]
        u_live = u_ref[:, at] * live
        inner = conv_rows(u_live, taps, same_ref)
        x_in, x_slope = silu_parts(inner)
        gate, gate_slope = silu_parts(z_ref[:, at])
        mixed = y_ref[:, at]
        gated = mixed * gate
        inverse = inverse_ref[:, 0:1]
        pull = (own_ref[:, 0:1] + other_ref[:, 0:1]) * inverse * inverse * inverse / DSSM
        grad_gated = taps[6:7] * dn_ref[:, at] * inverse - gated * pull
        grad_mixed = grad_gated * gate
        dz_ref[:, at] = (grad_gated * mixed * gate_slope).astype(dz_ref.dtype)
        grad_mixed_b = grad_mixed.astype(jnp.bfloat16)
        lanes = lax.broadcasted_iota(jnp.int32, (rows, 128), 1)
        left_lanes = lanes < HP
        size = sizes[...]
        size_pair = jnp.where(left_lanes, lane_column(size, 2 * pair), lane_column(size, 2 * pair + 1))
        inflow = (size_pair * x_in).astype(jnp.bfloat16)
        zero = jnp.zeros_like(inflow)
        inflow_heads = [jnp.where(left_lanes, inflow, zero), jnp.where(left_lanes, zero, inflow)]
        total = running[...]
        columns = [lane_column(total, 2 * pair + k) for k in range(2)]
        row_vectors = [running_t[pl.ds(2 * pair + k, 1), :] for k in range(2)]
        blocks = []
        for block in range(rows // TILE):
            top, end = block * TILE, (block + 1) * TILE
            parts = []
            gram_part = None
            for k in range(2):
                gaps = row_vectors[k][:, top:] - columns[k][top:end]
                decay = jnp.exp(jnp.minimum(gaps, 0.0))
                mixing_t = (gram_t[top:end, top:] * decay).astype(jnp.bfloat16)
                parts.append(dot_nn(mixing_t, grad_mixed_b[top:]))
                term = dot_nt(inflow_heads[k][top:end], grad_mixed_b[top:]) * decay
                gram_part = term if gram_part is None else gram_part + term
            gram_grad[top:end, top:] += gram_part
            blocks.append(jnp.where(left_lanes[top:end], parts[0], parts[1]))
        grad_inflow = jnp.concatenate(blocks, axis=0)
        grad_x = grad_mixed * taps[5:6] + grad_inflow * size_pair
        by_size = grad_inflow * x_in
        mixed_only = mixed - taps[5:6] * x_in
        by_total = grad_mixed_b.astype(jnp.float32) * mixed_only - grad_inflow * inflow.astype(jnp.float32)
        size_grad[...] += head_sums(by_size, pair)
        total_grad[...] += head_sums(by_total, pair)
        grad_u, tap_grads = conv_rows_back(grad_x * x_slope, u_live, taps, same_ref)
        du_ref[:, at] = (grad_u * live).astype(du_ref.dtype)
        skip_grad = jnp.sum(grad_mixed * x_in, axis=0, keepdims=True)
        wide_grad_ref[:, at] = jnp.concatenate(
            tap_grads + [skip_grad, jnp.zeros((2, 128), jnp.float32)], axis=0
        )

    @pl.when(step == pl.num_programs(0) - 1)
    def _():
        half = width // 2
        gram_grad_b = (gram_grad[...] * mask_t_ref[...]).astype(jnp.bfloat16)
        grad_b = dot_nn(gram_grad_b, states[:, half:])
        grad_c = dot_tn(gram_grad_b, states[:, :half])
        grad_bc = jnp.concatenate([grad_b, grad_c], axis=1) * state_slopes[...]
        state = jnp.concatenate([state_b_ref[...], state_c_ref[...]], axis=1) * wide_live
        grad_in, state_taps = conv_rows_back(grad_bc, state, conv_ref[...], same_ref)
        ds_ref[:rows, :] = (grad_in * wide_live).astype(ds_ref.dtype)
        ds_ref[rows:, :] = jnp.concatenate(
            state_taps + [jnp.zeros((11, width), jnp.float32)], axis=0
        ).astype(ds_ref.dtype)
        decay_grad = running_sum(total_grad[...], backward=True)
        shifted = step_ref[...] + extra_ref[0:1]
        grad_size = size_grad[...] - decay_grad * extra_ref[1:2]
        grad_raw = grad_size * live * jax.nn.sigmoid(shifted)
        dr_ref[...] = grad_raw.astype(dr_ref.dtype)
        extra_grad_ref[...] = jnp.concatenate(
            [
                jnp.sum(grad_raw, axis=0, keepdims=True),
                jnp.sum(decay_grad * decays[...], axis=0, keepdims=True),
                jnp.zeros((6, 128), jnp.float32),
            ],
            axis=0,
        )


def ssm_backward(
    grad_normed, mixed, projected, inverse, own, other, wide, conv_state, extra, live, same, mask_t, offsets
):
    rows = projected.shape[0]
    pairs = wide.shape[1] // 128
    width = conv_state.shape[1]
    const2 = lambda i: (0, 0)
    at = lambda name, size: offsets[name] // size
    block = lambda name: pl.BlockSpec((rows, 128 * 2), lambda i, o=at(name, 128 * 2): (0, o + i))
    plain = pl.BlockSpec((rows, 128 * 2), lambda i: (0, i))
    f32, b16 = jnp.float32, jnp.bfloat16
    return pl.pallas_call(
        ssm_backward_kernel,
        grid=(pairs // 2,),
        in_specs=[
            plain,
            plain,
            block("u"),
            block("z"),
            pl.BlockSpec((rows, width // 2), lambda i: (0, at("state", width // 2))),
            pl.BlockSpec((rows, width // 2), lambda i: (0, at("state", width // 2) + 1)),
            pl.BlockSpec((rows, 128), lambda i: (0, at("step", 128))),
            pl.BlockSpec((rows, 128), const2),
            pl.BlockSpec((rows, 128), const2),
            pl.BlockSpec((rows, 128), const2),
            pl.BlockSpec((8, 128 * 2), lambda i: (0, i)),
            pl.BlockSpec((8, width), const2),
            pl.BlockSpec((8, 128), const2),
            pl.BlockSpec((rows, 128), const2),
            pl.BlockSpec((3, rows, 128), lambda i: (0, 0, 0)),
            pl.BlockSpec((rows, rows), const2),
        ],
        out_specs=[
            plain,
            plain,
            pl.BlockSpec((rows + 16, width), const2),
            pl.BlockSpec((rows, 128), const2),
            pl.BlockSpec((8, 128 * 2), lambda i: (0, i)),
            pl.BlockSpec((8, 128), const2),
        ],
        out_shape=[
            jax.ShapeDtypeStruct((rows, pairs * 128), b16),
            jax.ShapeDtypeStruct((rows, pairs * 128), b16),
            jax.ShapeDtypeStruct((rows + 16, width), b16),
            jax.ShapeDtypeStruct((rows, 128), b16),
            jax.ShapeDtypeStruct((8, pairs * 128), f32),
            jax.ShapeDtypeStruct((8, 128), f32),
        ],
        scratch_shapes=[
            pltpu.VMEM((rows, rows), f32),
            pltpu.VMEM((rows, rows), f32),
            pltpu.VMEM((rows, 128), f32),
            pltpu.VMEM((rows, 128), f32),
            pltpu.VMEM((rows, 128), f32),
            pltpu.VMEM((128, rows), f32),
            pltpu.VMEM((rows, 128), f32),
            pltpu.VMEM((rows, 128), f32),
            pltpu.VMEM((rows, width), b16),
            pltpu.VMEM((rows, width), f32),
        ],
        compiler_params=pltpu.CompilerParams(vmem_limit_bytes=32 * 2**20),
        cost_estimate=cost(1, 1),
        name="ssm_backward",
    )(
        grad_normed, mixed, projected, projected, projected, projected, projected, inverse, own, other,
        wide, conv_state, extra, live, same, mask_t,
    )


def turned(values, cos_ref, sin_ref):
    return values * cos_ref[...] + pltpu.roll(values, HEAD_DIMENSION // 2, 1) * sin_ref[...]


def attention_forward_kernel(
    q_ref, k_ref, v_ref, cos_ref, sin_ref, mask_ref, out_ref, query_ref, key_ref, value_ref, log_ref
):
    head = pl.program_id(0)
    rows = q_ref.shape[0]
    scale = HEAD_DIMENSION**-0.5

    @pl.when(head == 0)
    def _():
        key_ref[...] = turned(k_ref[...], cos_ref, sin_ref).astype(jnp.bfloat16)
        value_ref[...] = v_ref[...].astype(jnp.bfloat16)

    query = turned(q_ref[...], cos_ref, sin_ref).astype(jnp.bfloat16)
    query_ref[...] = query
    for block in range(rows // TILE):
        top, end = block * TILE, (block + 1) * TILE
        scores = dot_nt(query[top:end], key_ref[:end, :]) * scale
        scores = jnp.where(mask_ref[top:end, :end] > 0.0, scores, -1e30)
        largest = jnp.max(scores, axis=1, keepdims=True)
        weights = jnp.exp(scores - largest)
        total = jnp.sum(weights, axis=1, keepdims=True)
        probs = (weights / total).astype(jnp.bfloat16)
        out_ref[top:end, :] = dot_nn(probs, value_ref[:end, :]).astype(out_ref.dtype)
        log_ref[top:end, :] = jnp.broadcast_to(largest + jnp.log(total), (TILE, 128))


def attention_forward(projected, cos, sin, mask, offsets, heads):
    rows = projected.shape[0]
    at = lambda name: offsets[name] // 128
    const2 = lambda i: (0, 0)
    one = pl.BlockSpec((rows, 128), const2)
    each = pl.BlockSpec((rows, 128), lambda i: (0, i))
    b16 = jnp.bfloat16
    return pl.pallas_call(
        attention_forward_kernel,
        grid=(heads,),
        in_specs=[
            pl.BlockSpec((rows, 128), lambda i: (0, at("q") + i)),
            pl.BlockSpec((rows, 128), lambda i: (0, at("kv"))),
            pl.BlockSpec((rows, 128), lambda i: (0, at("kv") + 1)),
            one,
            one,
            pl.BlockSpec((rows, rows), const2),
        ],
        out_specs=[each, each, one, one, each],
        out_shape=[
            jax.ShapeDtypeStruct((rows, heads * 128), b16),
            jax.ShapeDtypeStruct((rows, heads * 128), b16),
            jax.ShapeDtypeStruct((rows, 128), b16),
            jax.ShapeDtypeStruct((rows, 128), b16),
            jax.ShapeDtypeStruct((rows, heads * 128), jnp.float32),
        ],
        compiler_params=pltpu.CompilerParams(vmem_limit_bytes=24 * 2**20),
        name="attention_forward",
    )(projected, projected, projected, cos, sin, mask)


def attention_backward_kernel(
    grad_ref, query_ref, key_ref, value_ref, log_ref, cos_ref, sin_ref, mask_ref,
    dq_ref, dk_ref, dv_ref, key_sum, value_sum,
):
    head = pl.program_id(0)
    rows = query_ref.shape[0]
    scale = HEAD_DIMENSION**-0.5

    @pl.when(head == 0)
    def _():
        key_sum[...] = jnp.zeros_like(key_sum)
        value_sum[...] = jnp.zeros_like(value_sum)

    for block in range(rows // TILE):
        top, end = block * TILE, (block + 1) * TILE
        query = query_ref[top:end, :]
        grad = grad_ref[top:end, :]
        scores = dot_nt(query, key_ref[:end, :]) * scale
        scores = jnp.where(mask_ref[top:end, :end] > 0.0, scores, -1e30)
        probs = jnp.exp(scores - log_ref[top:end, 0:1])
        grad_probs = dot_nt(grad, value_ref[:end, :])
        inner = jnp.sum(grad_probs * probs, axis=1, keepdims=True)
        grad_scores = (probs * (grad_probs - inner)).astype(jnp.bfloat16)
        dq = dot_nn(grad_scores, key_ref[:end, :]) * scale
        dq_ref[top:end, :] = (
            dq * cos_ref[top:end, :]
            - pltpu.roll(dq, HEAD_DIMENSION // 2, 1) * sin_ref[top:end, :]
        ).astype(dq_ref.dtype)
        key_sum[:end, :] += dot_tn(grad_scores, query)
        value_sum[:end, :] += dot_tn(probs.astype(jnp.bfloat16), grad)

    @pl.when(head == pl.num_programs(0) - 1)
    def _():
        dk = key_sum[...] * scale
        dk_ref[...] = (
            dk * cos_ref[...] - pltpu.roll(dk, HEAD_DIMENSION // 2, 1) * sin_ref[...]
        ).astype(dk_ref.dtype)
        dv_ref[...] = value_sum[...].astype(dv_ref.dtype)


def attention_backward(grad, query, key, value, logs, cos, sin, mask):
    rows = query.shape[0]
    heads = query.shape[1] // 128
    const2 = lambda i: (0, 0)
    one = pl.BlockSpec((rows, 128), const2)
    each = pl.BlockSpec((rows, 128), lambda i: (0, i))
    b16 = jnp.bfloat16
    return pl.pallas_call(
        attention_backward_kernel,
        grid=(heads,),
        in_specs=[each, each, one, one, each, one, one, pl.BlockSpec((rows, rows), const2)],
        out_specs=[each, one, one],
        out_shape=[
            jax.ShapeDtypeStruct((rows, heads * 128), b16),
            jax.ShapeDtypeStruct((rows, 128), b16),
            jax.ShapeDtypeStruct((rows, 128), b16),
        ],
        scratch_shapes=[pltpu.VMEM((rows, 128), jnp.float32), pltpu.VMEM((rows, 128), jnp.float32)],
        compiler_params=pltpu.CompilerParams(vmem_limit_bytes=24 * 2**20),
        cost_estimate=cost(1, 1),
        name="attention_backward",
    )(grad, query, key, value, logs, cos, sin, mask)


def feed_forward_kernel(
    in_ref, grad_ref, gate_w_ref, up_w_ref, down_ref, act_ref, dgate_ref, dup_ref, din_ref, total
):
    step = pl.program_id(0)

    @pl.when(step == 0)
    def _():
        total[...] = jnp.zeros_like(total)

    gate = dot_nn(in_ref[...], gate_w_ref[...])
    up = dot_nn(in_ref[...], up_w_ref[...])
    grad_act = dot_nn(grad_ref[...], down_ref[...])
    value, slope = silu_parts(gate)
    act_ref[...] = (value * up).astype(act_ref.dtype)
    dgate = (grad_act * up * slope).astype(jnp.bfloat16)
    dup = (grad_act * value).astype(jnp.bfloat16)
    dgate_ref[...] = dgate
    dup_ref[...] = dup
    total[...] += dot_nt(dgate, gate_w_ref[...]) + dot_nt(dup, up_w_ref[...])

    @pl.when(step == pl.num_programs(0) - 1)
    def _():
        din_ref[...] = total[...].astype(din_ref.dtype)


def feed_forward(ffn_in, grad, weights, hidden, tile=512):
    rows, model = grad.shape
    steps = hidden // tile
    each = pl.BlockSpec((rows, tile), lambda i: (0, i))
    whole = pl.BlockSpec((rows, model), lambda i: (0, 0))
    b16 = jnp.bfloat16
    return pl.pallas_call(
        feed_forward_kernel,
        grid=(steps,),
        in_specs=[
            whole,
            whole,
            pl.BlockSpec((model, tile), lambda i: (0, i)),
            pl.BlockSpec((model, tile), lambda i: (0, steps + i)),
            pl.BlockSpec((model, tile), lambda i: (0, 2 * steps + i)),
        ],
        out_specs=[each, each, each, whole],
        out_shape=[
            jax.ShapeDtypeStruct((rows, hidden), b16),
            jax.ShapeDtypeStruct((rows, hidden), b16),
            jax.ShapeDtypeStruct((rows, hidden), b16),
            jax.ShapeDtypeStruct((rows, model), b16),
        ],
        scratch_shapes=[pltpu.VMEM((rows, model), jnp.float32)],
        compiler_params=pltpu.CompilerParams(vmem_limit_bytes=44 * 2**20),
        cost_estimate=cost(1, 1),
        name="feed_forward",
    )(ffn_in, grad, weights, weights, weights)


def norm_back_kernel(
    grad_ref, weight_ref, gated_ref, inverse_ref, gain_ref, dout_ref, dn_ref, row_ref, column_ref, *, split
):
    step = pl.program_id(0)

    @pl.when(step == 0)
    def _():
        row_ref[...] = jnp.zeros_like(row_ref)

    grad = dot_nn(grad_ref[...], weight_ref[...])

    @pl.when(step < split)
    def _():
        dout_ref[...] = grad.astype(dout_ref.dtype)

    @pl.when(step >= split)
    def _():
        dn_ref[...] = grad
        product = grad * gated_ref[...]
        scaled = product * gain_ref[0:1]
        part = scaled[:, :128]
        for k in range(1, scaled.shape[1] // 128):
            part = part + scaled[:, k * 128 : (k + 1) * 128]
        row_ref[...] += part
        total = jnp.sum(product * inverse_ref[:, 0:1], axis=0, keepdims=True)
        column_ref[...] = jnp.broadcast_to(total, column_ref.shape)

    @pl.when(step == pl.num_programs(0) - 1)
    def _():
        row_ref[...] = jnp.broadcast_to(
            jnp.sum(row_ref[...], axis=1, keepdims=True), row_ref.shape
        )


def norm_back(grad, weights, first, attended, gated, inverse, gains, tile=512):
    rows, model = grad.shape
    width = gated.shape[1]
    split = attended // tile
    later = lambda i: (0, jnp.maximum(i - split, 0))
    f32 = jnp.float32
    return pl.pallas_call(
        functools.partial(norm_back_kernel, split=split),
        grid=((attended + width) // tile,),
        in_specs=[
            pl.BlockSpec((rows, model), lambda i: (0, 0)),
            pl.BlockSpec((model, tile), lambda i: (0, first // tile + i)),
            pl.BlockSpec((rows, tile), later),
            pl.BlockSpec((rows, 128), lambda i: (0, 0)),
            pl.BlockSpec((8, tile), later),
        ],
        out_specs=[
            pl.BlockSpec((rows, tile), lambda i: (0, jnp.minimum(i, split - 1))),
            pl.BlockSpec((rows, tile), later),
            pl.BlockSpec((rows, 128), lambda i: (0, 0)),
            pl.BlockSpec((8, tile), later),
        ],
        out_shape=[
            jax.ShapeDtypeStruct((rows, attended), jnp.bfloat16),
            jax.ShapeDtypeStruct((rows, width), f32),
            jax.ShapeDtypeStruct((rows, 128), f32),
            jax.ShapeDtypeStruct((8, width), f32),
        ],
        compiler_params=pltpu.CompilerParams(vmem_limit_bytes=40 * 2**20),
        cost_estimate=cost(1, 1),
        name="norm_back",
    )(grad, weights, gated, inverse, gains)


def reorder_kernel(order_ref, in_ref, out_ref):
    width = in_ref.shape[1] // order_ref.shape[0]
    for place in range(order_ref.shape[0]):
        column = pl.multiple_of(order_ref[place] * width, width)
        out_ref[:, place * width : (place + 1) * width] = in_ref[:, pl.ds(column, width)]


def reorder_columns(values, order):
    rows, model = values.shape
    count = order.shape[0]
    width = model // count
    if width % 128:
        return jnp.take(values.reshape(rows, count, width), order, axis=1).reshape(rows, model)
    return pl.pallas_call(
        reorder_kernel,
        in_specs=[
            pl.BlockSpec(memory_space=pltpu.SMEM),
            pl.BlockSpec(memory_space=pltpu.VMEM),
        ],
        out_specs=pl.BlockSpec(memory_space=pltpu.VMEM),
        out_shape=jax.ShapeDtypeStruct(values.shape, values.dtype),
        compiler_params=pltpu.CompilerParams(vmem_limit_bytes=8 * 2**20),
        cost_estimate=cost(1, 1),
        name="reorder_columns",
    )(order, values)


def widest(width, most):
    return max(t for t in range(128, most + 1, 128) if width % t == 0)


def scatter_part_kernel(left_ref, right_ref, *refs):
    got_refs, out_ref, turned_left = refs[:-2], refs[-2], refs[-1]

    @pl.when(pl.program_id(0) == 0)
    def _():
        turned_left[...] = left_ref[...].T

    total = dot_nn(turned_left[...], right_ref[...])
    for got_ref in got_refs:
        total = total + got_ref[...].astype(jnp.float32)
    out_ref[...] = total.astype(out_ref.dtype)


def scatter_part(left, right, gots, first, size, dtype):
    rows, width = right.shape
    if size % 128 or first % size:
        total = contract("tm,tn->mn", left[:, first : first + size], right)
        for got, start in gots:
            total = total + got[start : start + size].astype(jnp.float32)
        return total.astype(dtype)
    tile = widest(width, 2304 if size <= 256 else 1152)
    return pl.pallas_call(
        scatter_part_kernel,
        grid=(width // tile,),
        in_specs=[
            pl.BlockSpec((rows, size), lambda i: (0, first // size)),
            pl.BlockSpec((rows, tile), lambda i: (0, i)),
        ]
        + [
            pl.BlockSpec((size, tile), lambda i, at=start // size: (at, i)) for unused, start in gots
        ],
        out_specs=pl.BlockSpec((size, tile), lambda i: (0, i)),
        out_shape=jax.ShapeDtypeStruct((size, width), dtype),
        scratch_shapes=[pltpu.VMEM((size, rows), jnp.bfloat16)],
        compiler_params=pltpu.CompilerParams(vmem_limit_bytes=24 * 2**20),
        cost_estimate=cost(1, 1),
        name="scatter_part",
    )(left, right, *[got for got, unused in gots])


def product_back_kernel(left_ref, right_ref, out_ref):
    out_ref[...] = dot_nt(left_ref[...], right_ref[...]).astype(out_ref.dtype)


def product_back(left, right, first, tile=512):
    rows, width = left.shape
    model = right.shape[0]
    return pl.pallas_call(
        product_back_kernel,
        grid=(model // tile,),
        in_specs=[
            pl.BlockSpec((rows, width), lambda i: (0, 0)),
            pl.BlockSpec((tile, width), lambda i: (i, first // width)),
        ],
        out_specs=pl.BlockSpec((rows, tile), lambda i: (0, i)),
        out_shape=jax.ShapeDtypeStruct((rows, model), jnp.bfloat16),
        compiler_params=pltpu.CompilerParams(vmem_limit_bytes=44 * 2**20),
        cost_estimate=cost(1, 1),
        name="product_back",
    )(left, right)


def join_kernel(start, ready_ref, got_ref, out_ref):
    size = ready_ref.shape[0]
    got = got_ref[start : start + size, :].astype(jnp.float32)
    out_ref[...] = (ready_ref[...] + got).astype(out_ref.dtype)


def join_parts(ready, got, start, dtype):
    size, width = ready.shape
    if size % 128 or start % size:
        return (ready + got[start : start + size].astype(jnp.float32)).astype(dtype)
    if size > 256:
        tile = widest(width, 1152)
        return pl.pallas_call(
            functools.partial(join_kernel, 0),
            grid=(width // tile,),
            in_specs=[
                pl.BlockSpec((size, tile), lambda i: (0, i)),
                pl.BlockSpec((size, tile), lambda i: (start // size, i)),
            ],
            out_specs=pl.BlockSpec((size, tile), lambda i: (0, i)),
            out_shape=jax.ShapeDtypeStruct((size, width), dtype),
            compiler_params=pltpu.CompilerParams(vmem_limit_bytes=24 * 2**20),
            cost_estimate=cost(1, 1),
            name="join_parts",
        )(ready, got)
    vmem = pl.BlockSpec(memory_space=pltpu.VMEM)
    return pl.pallas_call(
        functools.partial(join_kernel, start),
        in_specs=[vmem, vmem],
        out_specs=vmem,
        out_shape=jax.ShapeDtypeStruct((size, width), dtype),
        compiler_params=pltpu.CompilerParams(vmem_limit_bytes=16 * 2**20),
        cost_estimate=cost(1, 1),
        name="join_parts",
    )(ready, got)


def rms_back_kernel(value_ref, gain_ref, own_ref, other_ref, base_ref, live_ref, *out_refs):
    values = value_ref[...].astype(jnp.float32)
    gain = gain_ref[0:1]
    grad = own_ref[...].astype(jnp.float32) + other_ref[...].astype(jnp.float32)
    scale = lax.rsqrt(jnp.mean(values * values, axis=1, keepdims=True) + EPS)
    unit = values * scale
    scaled = grad * gain
    pull = jnp.mean(scaled * unit, axis=1, keepdims=True)
    total = base_ref[...].astype(jnp.float32) + (scaled - unit * pull) * scale
    out_refs[0][...] = total
    if len(out_refs) == 3:
        out_refs[2][...] = (total * live_ref[:, 0:1]).astype(jnp.bfloat16)
    gain_grad = jnp.broadcast_to(jnp.sum(grad * unit, axis=0, keepdims=True), out_refs[1].shape)

    @pl.when(pl.program_id(0) == 0)
    def _():
        out_refs[1][...] = gain_grad

    @pl.when(pl.program_id(0) > 0)
    def _():
        out_refs[1][...] += gain_grad


def rms_back(values, gain, own, other, base, live, with_rounded, tile=256):
    rows, model = values.shape
    each = pl.BlockSpec((tile, model), lambda i: (i, 0))
    whole = pl.BlockSpec((8, model), lambda i: (0, 0))
    shapes = [
        jax.ShapeDtypeStruct((rows, model), jnp.float32),
        jax.ShapeDtypeStruct((8, model), jnp.float32),
    ]
    if with_rounded:
        shapes.append(jax.ShapeDtypeStruct((rows, model), jnp.bfloat16))
    return pl.pallas_call(
        rms_back_kernel,
        grid=(rows // tile,),
        in_specs=[each, whole, each, each, each, pl.BlockSpec((tile, 128), lambda i: (i, 0))],
        out_specs=[each, whole, each][: len(shapes)],
        out_shape=shapes,
        compiler_params=pltpu.CompilerParams(vmem_limit_bytes=40 * 2**20),
        cost_estimate=cost(1, 1),
        name="rms_back",
    )(values, gain, own, other, base, live)


def beside_kernel(widths, *refs):
    out_ref, place, refs = refs[-1], 0, list(refs[:-1])
    for width, terms in widths:
        total = refs.pop(0)[...]
        if terms == 2:
            total = total.astype(jnp.float32) + refs.pop(0)[...].astype(jnp.float32)
        out_ref[:, place : place + width] = total.astype(out_ref.dtype)
        place += width
    if place < out_ref.shape[1]:
        out_ref[:, place:] = jnp.zeros((out_ref.shape[0], out_ref.shape[1] - place), out_ref.dtype)


def beside(width, *columns, tile=256):
    groups = [c if isinstance(c, tuple) else (c,) for c in columns]
    widths = tuple((g[0].shape[1], len(g)) for g in groups)
    arrays = [a for g in groups for a in g]
    rows = min(a.shape[0] for a in arrays)
    return pl.pallas_call(
        functools.partial(beside_kernel, widths),
        grid=(rows // tile,),
        in_specs=[pl.BlockSpec((tile, a.shape[1]), lambda i: (i, 0)) for a in arrays],
        out_specs=pl.BlockSpec((tile, width), lambda i: (i, 0)),
        out_shape=jax.ShapeDtypeStruct((rows, width), jnp.bfloat16),
        compiler_params=pltpu.CompilerParams(vmem_limit_bytes=16 * 2**20),
        cost_estimate=cost(1, 1),
        name="beside",
    )(*arrays)


def hidden_back_kernel(left_ref, keep_ref, weight_ref, out_ref, total):
    step = pl.program_id(0)
    last = pl.num_programs(0) - 1

    @pl.when(step == 0)
    def _():
        total[...] = jnp.zeros_like(total)

    left = jnp.where(step == last, left_ref[...] * keep_ref[0:1], left_ref[...])
    total[...] += dot_nt(left, weight_ref[...])

    @pl.when(step == last)
    def _():
        out_ref[...] = total[...].astype(out_ref.dtype)


def hidden_back(left, keep, weights):
    rows, width = left.shape
    model, tile = weights.shape[0], keep.shape[1]
    return pl.pallas_call(
        hidden_back_kernel,
        grid=(width // tile,),
        in_specs=[
            pl.BlockSpec((rows, tile), lambda i: (0, i)),
            pl.BlockSpec((8, tile), lambda i: (0, 0)),
            pl.BlockSpec((model, tile), lambda i: (0, i)),
        ],
        out_specs=pl.BlockSpec((rows, model), lambda i: (0, 0)),
        out_shape=jax.ShapeDtypeStruct((rows, model), jnp.bfloat16),
        scratch_shapes=[pltpu.VMEM((rows, model), jnp.float32)],
        compiler_params=pltpu.CompilerParams(vmem_limit_bytes=40 * 2**20),
        cost_estimate=cost(1, 1),
        name="hidden_back",
    )(left, keep, weights)


def rms_forward_kernel(base_ref, own_ref, other_ref, live_ref, gain_ref, middle_ref, out_ref):
    added = own_ref[...].astype(jnp.float32) + other_ref[...].astype(jnp.float32)
    values = base_ref[...].astype(jnp.float32) + added * live_ref[:, 0:1]
    middle_ref[...] = values
    scale = lax.rsqrt(jnp.mean(values * values, axis=1, keepdims=True) + EPS)
    out_ref[...] = (values * scale * gain_ref[0:1]).astype(out_ref.dtype)


def rms_forward(base, own, other, live, gain, tile=256):
    rows, model = base.shape
    each = pl.BlockSpec((tile, model), lambda i: (i, 0))
    return pl.pallas_call(
        rms_forward_kernel,
        grid=(rows // tile,),
        in_specs=[
            each,
            each,
            each,
            pl.BlockSpec((tile, 128), lambda i: (i, 0)),
            pl.BlockSpec((8, model), lambda i: (0, 0)),
        ],
        out_specs=[each, each],
        out_shape=[
            jax.ShapeDtypeStruct((rows, model), jnp.float32),
            jax.ShapeDtypeStruct((rows, model), jnp.bfloat16),
        ],
        compiler_params=pltpu.CompilerParams(vmem_limit_bytes=28 * 2**20),
        cost_estimate=cost(1, 1),
        name="rms_forward",
    )(base, own, other, live, gain)


def output_kernel(base_ref, own_ref, other_ref, live_ref, out_ref):
    added = own_ref[...].astype(jnp.float32) + other_ref[...].astype(jnp.float32)
    out_ref[...] = (base_ref[...] + added * live_ref[:, 0:1]).astype(out_ref.dtype)


def output_rows(base, own, other, live, tile=256):
    rows, model = base.shape
    each = pl.BlockSpec((tile, model), lambda i: (i, 0))
    return pl.pallas_call(
        output_kernel,
        grid=(rows // tile,),
        in_specs=[each, each, each, pl.BlockSpec((tile, 128), lambda i: (i, 0))],
        out_specs=each,
        out_shape=jax.ShapeDtypeStruct((rows, model), jnp.bfloat16),
        compiler_params=pltpu.CompilerParams(vmem_limit_bytes=24 * 2**20),
        cost_estimate=cost(1, 1),
        name="output_rows",
    )(base, own, other, live)


def stack_kernel(layout, *refs):
    out_ref, place, refs = refs[-1], 0, list(refs[:-1])
    out_ref[...] = jnp.zeros_like(out_ref)
    for start, count, terms in layout:
        total = refs.pop(0)[start : start + count, :].astype(jnp.float32)
        if terms == 2:
            total = total + refs.pop(0)[start : start + count, :].astype(jnp.float32)
        out_ref[place : place + count, : total.shape[1]] = total
        place += count


def stack_rows(width, *parts):
    layout = tuple((start, count, len(arrays)) for arrays, start, count in parts)
    total = -(-sum(count for unused, count, terms in layout) // 8) * 8
    vmem = pl.BlockSpec(memory_space=pltpu.VMEM)
    arrays = [array for arrays, start, count in parts for array in arrays]
    return pl.pallas_call(
        functools.partial(stack_kernel, layout),
        in_specs=[vmem] * len(arrays),
        out_specs=vmem,
        out_shape=jax.ShapeDtypeStruct((total, width), jnp.float32),
        compiler_params=pltpu.CompilerParams(vmem_limit_bytes=8 * 2**20),
        cost_estimate=cost(1, 1),
        name="stack_rows",
    )(*arrays)


def add_kernel(left_ref, right_ref, out_ref):
    out_ref[...] = left_ref[...] + right_ref[...]


def add_rows(left, right):
    vmem = pl.BlockSpec(memory_space=pltpu.VMEM)
    return pl.pallas_call(
        add_kernel,
        in_specs=[vmem, vmem],
        out_specs=vmem,
        out_shape=jax.ShapeDtypeStruct(left.shape, left.dtype),
        compiler_params=pltpu.CompilerParams(vmem_limit_bytes=8 * 2**20),
        cost_estimate=cost(1, 1),
        name="add_rows",
    )(left, right)


def turn_kernel(in_ref, out_ref):
    out_ref[...] = in_ref[...].T


def turned_copy(values, tile=512):
    rows, width = values.shape
    return pl.pallas_call(
        turn_kernel,
        grid=(width // tile,),
        in_specs=[pl.BlockSpec((rows, tile), lambda i: (0, i))],
        out_specs=pl.BlockSpec((tile, rows), lambda i: (i, 0)),
        out_shape=jax.ShapeDtypeStruct((width, rows), values.dtype),
        compiler_params=pltpu.CompilerParams(vmem_limit_bytes=8 * 2**20),
        cost_estimate=cost(1, 1),
        name="turned_copy",
    )(values)


def tie(*values):
    return lax.optimization_barrier(values)


def pair_swap(values):
    return lax.ppermute(values, "tensor", [(0, 1), (1, 0)])


def pair_sum(values):
    own = lax.reduce_precision(values.astype(jnp.float32), 8, 7)
    return own + pair_swap(own.astype(jnp.bfloat16)).astype(jnp.float32)


def pair_join(values):
    other = pair_swap(values)
    first = lax.axis_index("tensor") == 0
    return jnp.concatenate(
        [jnp.where(first, values, other), jnp.where(first, other, values)], axis=0
    )


def after(values, *earlier):
    return lax.optimization_barrier((values, *earlier))[0]


def bits_of(count):
    return tuple(1 << place for place in range(count.bit_length() - 1))


def owner_order(bits):
    offsets = [0]
    for bit in reversed(bits):
        offsets = [offset | bit for offset in offsets] + offsets
    return lax.axis_index("dp") ^ jnp.array(offsets, jnp.int32)


def across(values, bit):
    count = lax.axis_size("dp")
    return lax.ppermute(values, "dp", [(i, i ^ bit) for i in range(count)])


class Scatter:
    def __init__(self, left, right, bits):
        self.left, self.right, self.bits = left, right, bits
        self.rows = left.shape[1] // 2 ** len(bits)
        self.got = []
        self.total = None

    def place(self, step):
        count = 2 ** len(self.bits)
        return count - (count >> step), max(count >> (step + 1), 1)

    def meets(self, past, step):
        return (self.place(step)[0] - self.place(past + 1)[0]) * self.rows

    def begin(self, *earlier):
        first, size = self.place(0)
        left = after(self.left, *earlier)
        self.held = scatter_part(left, self.right, [], 0, size * self.rows, jnp.bfloat16)
        return self.held

    def send(self, *earlier):
        self.got.append(across(after(self.held, *earlier), self.bits[len(self.got)]))
        return self.got[-1]

    def prepare(self, *earlier):
        step = len(self.got)
        first, size = self.place(step)
        gots = [(got, self.meets(past, step)) for past, got in enumerate(self.got[:-1])]
        left = after(self.left, *earlier)
        self.ready = scatter_part(
            left, self.right, gots, first * self.rows, size * self.rows, jnp.float32
        )
        return self.ready

    def make(self, *earlier):
        step = len(self.got)
        first, size = self.place(step)
        gots = [(got, self.meets(past, step)) for past, got in enumerate(self.got)]
        done = step == len(self.bits)
        self.held = scatter_part(
            after(self.left, *earlier),
            self.right,
            gots,
            first * self.rows,
            size * self.rows,
            jnp.float32 if done else jnp.bfloat16,
        )
        if done:
            self.total = self.held
        return self.held

    def join(self, *earlier):
        step = len(self.got)
        done = step == len(self.bits)
        self.held = join_parts(
            after(self.ready, *earlier),
            self.got[-1],
            self.meets(step - 1, step),
            jnp.float32 if done else jnp.bfloat16,
        )
        if done:
            self.total = self.held
        return self.held

    def finish(self):
        while self.total is None:
            self.send()
            self.make()
        return self.total


def side_by_side(first, second):
    return with_layout_constraint(
        jnp.stack([first, second], axis=1), Layout(major_to_minor=(0, 1, 2))
    )


def local(
    tokens,
    cotangent,
    segment_ids,
    counts,
    mixer_gain,
    query_proj,
    key_value_matrix,
    attend_proj,
    inner_proj,
    state_proj,
    step_proj,
    conv_inner,
    conv_state,
    step_bias,
    decay_log,
    skip_gain,
    gated_gain,
    mamba_proj,
    dense_gain,
    gateup_proj,
    down_proj,
):
    row_count, model_width = tokens.shape
    shard_rows = query_proj.shape[0]
    dp_count = lax.axis_size("dp")
    bf16, f32 = jnp.bfloat16, jnp.float32
    heads_m = step_proj.shape[1]
    heads_q = query_proj.shape[1] // HEAD_DIMENSION
    q_cols = query_proj.shape[1]
    kv_cols = 2 * key_value_matrix.shape[2]
    x_cols = inner_proj.shape[2]
    state_cols = state_proj.shape[1]
    o_cols = attend_proj.shape[0]
    hidden_cols = gateup_proj.shape[2]
    tap_count = conv_state.shape[0]
    pair_width = conv_state.shape[1]

    small = jnp.concatenate(
        [
            jnp.concatenate([mixer_gain, dense_gain])[None],
            jnp.pad(conv_state, ((0, 0), (0, 2 * mixer_gain.shape[0] - pair_width))),
        ],
        axis=0,
    )
    state_rows_full = pair_join(state_proj)
    small_pair = pair_join(small[None])
    gain_half = mixer_gain.shape[0]
    small_rows = jnp.concatenate(
        [
            small_pair[:, 0, :gain_half].reshape(1, -1),
            small_pair[:, 0, gain_half:].reshape(1, -1),
            jnp.pad(
                jnp.concatenate([small_pair[0, 1:, :pair_width], small_pair[1, 1:, :pair_width]], axis=1),
                ((0, 0), (0, shard_rows - 2 * pair_width)),
            ),
        ],
        axis=0,
    )
    small_block = jnp.pad(
        small_rows, ((0, shard_rows - small_rows.shape[0]), (0, 128 - shard_rows))
    )
    step_pad = jnp.zeros((shard_rows, 128 - heads_m), bf16)
    group_mix = jnp.concatenate(
        [
            inner_proj[:, 0],
            query_proj,
            key_value_matrix.reshape(shard_rows, -1),
            inner_proj[:, 1],
            state_rows_full,
            step_proj,
            step_pad,
            small_block,
            attend_proj.T,
            mamba_proj.T,
        ],
        axis=1,
    )
    offsets, place = {}, 0
    for name, width in (
        ("z", x_cols),
        ("q", q_cols),
        ("kv", kv_cols),
        ("u", x_cols),
        ("state", state_cols),
        ("step", 128),
        ("end", 0),
    ):
        offsets[name] = place
        place += width
    out_first = offsets["end"] + 128
    group_ffn = jnp.concatenate([gateup_proj.reshape(shard_rows, -1), down_proj.T], axis=1)
    mix_full = lax.all_gather(group_mix, "dp", axis=0, tiled=True)
    ffn_full = lax.all_gather(after(group_ffn, mix_full), "dp", axis=0, tiled=True)
    out_t = mix_full[:, out_first:]
    down_t = ffn_full[:, 2 * hidden_cols :]

    small_full = mix_full[:, offsets["end"] : out_first]
    w_proj = mix_full[:, : offsets["end"]]
    small_full = small_full.reshape(dp_count, shard_rows, 128)
    gain_mix = small_full[:, 0, :shard_rows].reshape(-1).astype(f32)
    gain_dense = small_full[:, 1, :shard_rows].reshape(-1).astype(f32)
    conv_full = small_full[:, 2 : 2 + tap_count, : 2 * pair_width].astype(f32)
    conv_full = jnp.swapaxes(conv_full, 0, 1).reshape(tap_count, -1)
    conv_full = jnp.concatenate([conv_full, jnp.zeros((8 - tap_count, state_cols), f32)], axis=0)
    gain_gated = gated_gain.astype(f32)
    wide = jnp.concatenate(
        [
            conv_inner.astype(f32),
            jnp.repeat(skip_gain.astype(f32), HP)[None],
            gain_gated[None],
            jnp.zeros((1, x_cols), f32),
        ],
        axis=0,
    )
    extra = jnp.zeros((8, 128), f32)
    extra = extra.at[0, :heads_m].set(step_bias.astype(f32))
    extra = extra.at[1, :heads_m].set(jnp.exp(decay_log.astype(f32)))

    row_index = jnp.arange(row_count, dtype=jnp.int32)
    valid_rows = (row_index < counts[0]).astype(f32)[:, None]
    live = jnp.broadcast_to(valid_rows, (row_count, 128))
    position = positions_of(segment_ids)
    causal = (row_index[None, :] <= row_index[:, None]) & (
        segment_ids[None, :] == segment_ids[:, None]
    )
    mask = causal.astype(f32)
    mask_t = (
        (row_index[None, :] >= row_index[:, None]) & (segment_ids[None, :] == segment_ids[:, None])
    ).astype(f32)
    mask_qk = (causal & (row_index[None, :] < counts[0])).astype(f32)
    same = jnp.stack(
        [
            jnp.broadcast_to(((row_index >= lag) & (position >= lag)).astype(f32)[:, None], live.shape)
            for lag in range(1, tap_count - 1)
        ]
    )
    half = HEAD_DIMENSION // 2
    frequency = jnp.exp(
        jnp.arange(half, dtype=f32) * (-2.0 * math.log(THETA) / HEAD_DIMENSION)
    )
    angles = position.astype(f32)[:, None] * frequency[None, :]
    cos = jnp.cos(angles)
    sin = jnp.sin(angles)
    cos = jnp.concatenate([cos, cos], axis=1)
    sin = jnp.concatenate([-sin, sin], axis=1)
    bits = bits_of(dp_count)
    order = owner_order(bits)
    stream = tokens.astype(f32)
    upstream = cotangent.astype(f32)
    dense_grad_b = rounded(upstream * valid_rows)
    dense_split = reorder_columns(dense_grad_b, order)

    gain_dense_rows = jnp.broadcast_to(gain_dense[None], (8, model_width))
    gain_mix_rows = jnp.broadcast_to(gain_mix[None], (8, model_width))

    hidden_b = rounded(rms_scale(stream, gain_mix))
    projected = contract("td,dc->tc", hidden_b, w_proj)
    hidden_split = reorder_columns(hidden_b, order)
    mixed, gated, squares = ssm_forward(
        projected, wide, conv_full, extra, live, same, mask, offsets
    )
    own_squares = jnp.sum(squares, axis=-1)
    other_squares = pair_swap(own_squares)
    attended_b, query_b, key_b, value_b, logs = attention_forward(
        projected, cos, sin, mask_qk, offsets, heads_q
    )
    inverse = lax.rsqrt((own_squares + other_squares) / DSSM + EPS)
    normed_b = rounded(gated * inverse[:, None] * gain_gated)
    branch_in = jnp.concatenate([attended_b, normed_b], axis=1)
    branch_own = rounded(contract("tc,dc->td", branch_in, out_t))
    branch_other = pair_swap(branch_own)
    middle, ffn_in_b = rms_forward(tokens, branch_own, branch_other, live, gain_dense_rows)
    inverse_b = jnp.broadcast_to(inverse[:, None], live.shape)
    gated_rows = jnp.broadcast_to(gain_gated[None], (8, x_cols))
    first = (lax.axis_index("tensor") == 0).astype(bf16)
    last_cols = offsets["end"] + 128 - offsets["state"]
    keep = jnp.where(jnp.arange(last_cols) < state_cols, first, jnp.ones((), bf16))
    keep = jnp.broadcast_to(keep[None], (8, last_cols))
    ffn_split = reorder_columns(ffn_in_b, order)

    activated_b, grad_gate_b, grad_up_b, grad_ffn_part = feed_forward(
        ffn_in_b, after(dense_grad_b, ffn_split, dense_split), ffn_full, hidden_cols
    )
    down = Scatter(dense_split, activated_b, bits)
    gate_sum = Scatter(ffn_split, grad_gate_b, bits)
    up_sum = Scatter(ffn_split, grad_up_b, bits)
    held = down.begin()
    down.send()
    held = gate_sum.begin(held)
    ready = down.prepare(held)

    held = down.join(ready)
    down.send()
    grad_ffn_other = pair_swap(after(grad_ffn_part, ready))
    gate_sum.send(ready)
    held = up_sum.begin(held)
    ready = down.prepare(held)
    dense_own = product_back(after(activated_b, ready), ffn_full, 2 * hidden_cols)
    ready = gate_sum.prepare(dense_own)

    round_end = (ready, down.got[-1], gate_sum.got[-1], grad_ffn_other)
    held = gate_sum.join(*round_end)
    gate_sum.send()
    up_sum.send(*round_end)
    held = down.make(held)
    down.send()
    grad_middle, grad_dense_gain, mixer_grad_b = rms_back(
        middle, gain_dense_rows, after(grad_ffn_part, held), grad_ffn_other, cotangent, live, True
    )
    grad_attended_b, grad_normed, own_rows, column_part = norm_back(
        mixer_grad_b, mix_full, out_first, o_cols, gated, inverse_b, gated_rows
    )
    other_rows = pair_swap(own_rows)
    branch = Scatter(reorder_columns(mixer_grad_b, order), branch_in, bits)
    held = branch.begin(own_rows)
    ready = up_sum.prepare(held)
    grad_query_b, grad_key_b, grad_value_b = attention_backward(
        after(grad_attended_b, ready), query_b, key_b, value_b, logs, cos, sin, mask_qk
    )
    ready = grad_query_b

    round_end = (ready, gate_sum.got[-1], up_sum.got[-1], down.got[-1], other_rows)
    held = up_sum.join(*round_end)
    up_sum.send()
    branch.send(*round_end)
    held = gate_sum.make(held)
    gate_sum.send()
    held = down.make(held)
    down.send()
    dense_other = pair_swap(after(dense_own, *round_end))
    grad_z_b, grad_u_b, grad_state_part, grad_step_b, wide_grad, extra_grad = (
        ssm_backward(
            after(grad_normed, held),
            mixed,
            projected,
            inverse_b,
            own_rows,
            other_rows,
            wide,
            conv_full,
            extra,
            live,
            same,
            mask_t,
            offsets,
        )
    )
    head_b = beside(x_cols + q_cols, grad_z_b, grad_query_b)
    z_sum = Scatter(hidden_split, head_b, bits)
    inner_b = beside(kv_cols + x_cols, grad_key_b, grad_value_b, after(grad_u_b, head_b))
    u_sum = Scatter(hidden_split, inner_b, bits)
    held = z_sum.begin(grad_state_part)
    ready = branch.prepare(held)

    round_end = (ready, up_sum.got[-1], gate_sum.got[-1], branch.got[-1], down.got[-1], dense_other)
    held = branch.join(*round_end)
    branch.send()
    z_sum.send(*round_end)
    grad_state_other = pair_swap(after(grad_state_part, *round_end))
    held = up_sum.make(held)
    up_sum.send()
    held = gate_sum.make(held)
    gate_sum.send()
    held = u_sum.begin(held)
    other_b = beside(last_cols, (grad_state_part, after(grad_state_other, held)), grad_step_b)
    other_sum = Scatter(hidden_split, other_b, bits)
    columns_b = beside(offsets["end"] + 128, head_b, inner_b, other_b)
    grad_hidden_own = hidden_back(columns_b, keep, mix_full)
    held = other_sum.begin(grad_hidden_own)
    ready = z_sum.prepare(held)

    round_end = (ready, branch.got[-1], up_sum.got[-1], gate_sum.got[-1], z_sum.got[-1])
    held = z_sum.join(*round_end)
    z_sum.send()
    u_sum.send(*round_end)
    grad_hidden_other = pair_swap(after(grad_hidden_own, *round_end))
    held = branch.make(held)
    branch.send()
    held = up_sum.make(held)
    up_sum.send()
    held = gate_sum.make(held)
    held = down.make(held)
    red_down = turned_copy(after(down.finish(), held))
    output = output_rows(middle, after(dense_own, red_down), dense_other, live)
    ready = u_sum.prepare(output)
    ready = z_sum.prepare(ready)
    ready = branch.prepare(ready)
    ready = up_sum.prepare(ready)

    round_end = (ready, z_sum.got[-1], u_sum.got[-1], branch.got[-1], up_sum.got[-1], grad_hidden_other)
    held = u_sum.join(*round_end)
    u_sum.send()
    other_sum.send(*round_end)
    held = z_sum.join(held)
    z_sum.send()
    held = branch.join(held)
    branch.send()
    held = up_sum.join(held)
    red_gateup = side_by_side(after(gate_sum.finish(), held), up_sum.finish())
    grad_tokens, grad_mixer_gain = rms_back(
        tokens, gain_mix_rows, after(grad_hidden_own, red_gateup), grad_hidden_other, grad_middle, live, False
    )
    own_sums = stack_rows(
        model_width,
        ((grad_mixer_gain,), 0, 1),
        ((grad_dense_gain,), 0, 1),
        ((wide_grad,), 0, tap_count + 1),
        ((column_part,), 0, 1),
        ((grad_state_part, grad_state_other), row_count, tap_count),
        ((extra_grad,), 0, 2),
    )
    sums = add_rows(own_sums, across(own_sums, bits[0]))
    ready = other_sum.prepare(sums)
    ready = u_sum.prepare(ready)
    ready = z_sum.prepare(ready)
    ready = branch.prepare(ready)

    round_end = (ready, u_sum.got[-1], other_sum.got[-1], z_sum.got[-1], branch.got[-1])
    held = other_sum.join(*round_end)
    other_sum.send()
    held = u_sum.join(held)
    u_sum.send()
    others = across(after(sums, *round_end), bits[1])
    held = z_sum.join(held)
    z_sum.send()
    held = branch.join(held)
    red_branch = branch.finish()
    red_attend = turned_copy(after(red_branch[:, :o_cols], held))
    red_mamba = turned_copy(after(red_branch[:, o_cols:], red_attend))
    ready = other_sum.prepare(red_mamba)
    ready = u_sum.prepare(ready)
    ready = z_sum.prepare(ready)

    round_end = (ready, other_sum.got[-1], u_sum.got[-1], z_sum.got[-1], others)
    held = other_sum.join(*round_end)
    other_sum.send()
    sums = add_rows(after(sums, held), others)
    others = across(sums, bits[2])
    held = u_sum.join(sums)
    u_sum.send()
    held = z_sum.join(held)
    ready = other_sum.prepare(held)
    ready = u_sum.prepare(ready)

    held = other_sum.join(ready, other_sum.got[-1], u_sum.got[-1], others)
    other_sum.send()
    sums = add_rows(after(sums, held), others)
    others = across(sums, bits[3])
    held = u_sum.join(sums)
    ready = other_sum.prepare(held)
    held = other_sum.join(ready)
    red_head = after(z_sum.finish(), held)
    red_next = u_sum.finish()
    red_inner = side_by_side(red_head[:, :x_cols], red_next[:, kv_cols:])
    sums = add_rows(after(sums, held), others)
    for bit in bits[4:]:
        sums = add_rows(sums, across(sums, bit))
    at = 2 + tap_count + 2
    conv_sum = sums[at : at + tap_count, :state_cols]
    at += tap_count
    skip_sum = jnp.sum(sums[2 + tap_count, :x_cols].reshape(heads_m, HP), axis=1)
    owner = lax.axis_index("dp") * 2 + lax.axis_index("tensor")

    def own_part(values, axis_dim):
        width = values.shape[axis_dim] // (2 * dp_count)
        return lax.dynamic_slice_in_dim(values, owner * width, width, axis_dim)

    red_other = other_sum.finish()
    state_rows = shard_rows // 2
    red_state = lax.dynamic_slice_in_dim(
        red_other[:, :state_cols], lax.axis_index("tensor") * state_rows, state_rows, 0
    )
    return (
        output,
        grad_tokens,
        own_part(sums[0], 0),
        red_head[:, x_cols:],
        red_next[:, :kv_cols].reshape(shard_rows, 2, -1),
        red_attend,
        red_inner,
        red_state,
        red_other[:, state_cols : state_cols + heads_m],
        sums[2 : 2 + tap_count, :x_cols],
        own_part(conv_sum, 1),
        sums[at, :heads_m],
        sums[at + 1, :heads_m],
        skip_sum,
        sums[3 + tap_count, :x_cols],
        red_mamba,
        own_part(sums[1], 0),
        red_gateup,
        red_down,
    )


def solution(mesh):
    placed = (
        P("dp", None),
        P("dp", None),
        P("dp"),
        P("dp"),
        P(("dp", "tensor")),
        P("dp", "tensor"),
        P("dp", None, "tensor"),
        P("tensor", "dp"),
        P("dp", None, "tensor"),
        P(("dp", "tensor"), None),
        P("dp", "tensor"),
        P(None, "tensor"),
        P(None, ("dp", "tensor")),
        P("tensor"),
        P("tensor"),
        P("tensor"),
        P("tensor"),
        P("tensor", "dp"),
        P(("dp", "tensor")),
        P("dp", None, "tensor"),
        P("tensor", "dp"),
    )
    return jax.shard_map(
        local,
        mesh=mesh,
        in_specs=placed,
        out_specs=(
            P("dp", None),
            P("dp", None),
            P(("dp", "tensor")),
            P("dp", "tensor"),
            P("dp", None, "tensor"),
            P("tensor", "dp"),
            P("dp", None, "tensor"),
            P(("dp", "tensor"), None),
            P("dp", "tensor"),
            P(None, "tensor"),
            P(None, ("dp", "tensor")),
            P("tensor"),
            P("tensor"),
            P("tensor"),
            P("tensor"),
            P("tensor", "dp"),
            P(("dp", "tensor")),
            P("dp", None, "tensor"),
            P("tensor", "dp"),
        ),
        check_vma=False,
    )
```

```python
import functools
import math

import jax
import jax.numpy as jnp
from jax import lax
from jax.experimental import pallas as pl
from jax.experimental.pallas import tpu as pltpu
from jax.experimental.layout import Layout, with_layout_constraint
from jax.sharding import PartitionSpec as P

HP = 64
HEAD_DIMENSION = 128
DSSM = 3072
TILE = 256

EPS = 1e-05
THETA = 100000000000.0


def rounded(values):
    return values.astype(jnp.bfloat16)


def contract(form, left, right):
    return jnp.einsum(form, left, right, preferred_element_type=jnp.float32)


def rms_scale(values, gain):
    return values * lax.rsqrt(jnp.mean(values * values, axis=-1, keepdims=True) + EPS) * gain


def cost(flops, traffic, transcendentals=0):
    return pl.CostEstimate(
        flops=flops, bytes_accessed=traffic, transcendentals=transcendentals
    )


def positions_of(segment):
    row_index = jnp.arange(segment.shape[0], dtype=jnp.int32)
    starts = jnp.concatenate([jnp.ones((1,), jnp.bool_), segment[1:] != segment[:-1]])
    first_row = lax.cummax(jnp.where(starts, row_index, 0), axis=0)
    return row_index - first_row


def silu_parts(values):
    gate = jax.nn.sigmoid(values)
    return values * gate, gate * (1.0 + values * (1.0 - gate))


def dot_nn(left, right):
    return lax.dot_general(left, right, (((1,), (0,)), ((), ())), preferred_element_type=jnp.float32)


def dot_nt(left, right):
    return lax.dot_general(left, right, (((1,), (1,)), ((), ())), preferred_element_type=jnp.float32)


def dot_tn(left, right):
    return lax.dot_general(left, right, (((0,), (0,)), ((), ())), preferred_element_type=jnp.float32)


def shifted_rows(values, lag, same_ref):
    columns = values.shape[1]
    mask = same_ref[lag - 1]
    if columns > mask.shape[1]:
        mask = jnp.concatenate([mask] * (columns // mask.shape[1]), axis=1)
    return mask * pltpu.roll(values, lag, 0)


def conv_rows(values, taps, same_ref):
    total = taps[4:5] + taps[3:4] * values
    for lag in range(1, 4):
        total = total + taps[3 - lag : 4 - lag] * shifted_rows(values, lag, same_ref)
    return total


def conv_rows_back(grad, values, taps, same_ref):
    rows = grad.shape[0]
    total = taps[3:4] * grad
    tap_grads = [None] * 5
    tap_grads[4] = jnp.sum(grad, axis=0, keepdims=True)
    tap_grads[3] = jnp.sum(grad * values, axis=0, keepdims=True)
    for lag in range(1, 4):
        mask = same_ref[lag - 1]
        if grad.shape[1] > mask.shape[1]:
            mask = jnp.concatenate([mask] * (grad.shape[1] // mask.shape[1]), axis=1)
        masked = grad * mask
        total = total + taps[3 - lag : 4 - lag] * pltpu.roll(masked, rows - lag, 0)
        tap_grads[3 - lag] = jnp.sum(
            masked * pltpu.roll(values, lag, 0), axis=0, keepdims=True
        )
    return total, tap_grads


def running_sum(values, backward=False):
    rows = values.shape[0]
    index = lax.broadcasted_iota(jnp.int32, values.shape, 0)
    step = 1
    while step < rows:
        if backward:
            moved = pltpu.roll(values, rows - step, 0)
            values = values + jnp.where(index < rows - step, moved, 0.0)
        else:
            moved = pltpu.roll(values, step, 0)
            values = values + jnp.where(index >= step, moved, 0.0)
        step *= 2
    return values


def step_sizes(raw, extra_ref, live):
    shifted = raw + extra_ref[0:1]
    size = (jnp.maximum(shifted, 0.0) + jnp.log1p(jnp.exp(-jnp.abs(shifted)))) * live
    return shifted, size, -size * extra_ref[1:2]


def lane_column(values, lane):
    lanes = lax.broadcasted_iota(jnp.int32, values.shape, 1)
    return jnp.sum(jnp.where(lanes == lane, values, 0.0), axis=1, keepdims=True)


def head_sums(values, pair):
    lanes = lax.broadcasted_iota(jnp.int32, (128, 128), 0)
    heads = lax.broadcasted_iota(jnp.int32, (128, 128), 1)
    chosen = (heads == 2 * pair + lanes // HP).astype(jnp.bfloat16)
    high = values.astype(jnp.bfloat16)
    low = (values - high.astype(jnp.float32)).astype(jnp.bfloat16)
    return dot_nn(jnp.concatenate([high, low], axis=1), jnp.concatenate([chosen, chosen], axis=0))


def ssm_forward_kernel(
    u_ref, z_ref, state_b_ref, state_c_ref, step_ref, wide_ref, conv_ref, extra_ref, live_ref, same_ref, mask_ref,
    y_ref, gated_ref, square_ref, gram, sizes, running, running_t,
):
    step = pl.program_id(0)
    live = live_ref[...]
    rows = live.shape[0]

    @pl.when(step == 0)
    def _():
        unused, size, decay = step_sizes(step_ref[...], extra_ref, live)
        total = running_sum(decay)
        sizes[...] = size
        running[...] = total
        running_t[...] = total.T
        width = conv_ref.shape[1]
        wide_live = jnp.concatenate([live] * (width // 128), axis=1)
        state = jnp.concatenate([state_b_ref[...], state_c_ref[...]], axis=1) * wide_live
        inner = conv_rows(state, conv_ref[...], same_ref)
        both = (inner * jax.nn.sigmoid(inner)).astype(jnp.bfloat16)
        gram[...] = dot_nt(both[:, width // 2 :], both[:, : width // 2]) * mask_ref[...]
        square_ref[...] = jnp.zeros_like(square_ref)

    for part in range(2):
        pair = 2 * step + part
        at = slice(part * 128, (part + 1) * 128)
        taps = wide_ref[:, at]
        inner = conv_rows(u_ref[:, at] * live, taps, same_ref)
        x_in = inner * jax.nn.sigmoid(inner)
        left_lanes = lax.broadcasted_iota(jnp.int32, (rows, 128), 1) < HP
        size = sizes[...]
        size_pair = jnp.where(left_lanes, lane_column(size, 2 * pair), lane_column(size, 2 * pair + 1))
        inflow = (size_pair * x_in).astype(jnp.bfloat16)
        total = running[...]
        columns = [lane_column(total, 2 * pair + k) for k in range(2)]
        row_vectors = [running_t[pl.ds(2 * pair + k, 1), :] for k in range(2)]
        skipped = taps[5:6] * x_in
        gate = z_ref[:, at]
        gate = gate * jax.nn.sigmoid(gate)
        for block in range(rows // TILE):
            top, end = block * TILE, (block + 1) * TILE
            parts = []
            for k in range(2):
                gaps = columns[k][top:end] - row_vectors[k][:, :end]
                mixing = (gram[top:end, :end] * jnp.exp(jnp.minimum(gaps, 0.0))).astype(jnp.bfloat16)
                parts.append(dot_nn(mixing, inflow[:end]))
            mixed = jnp.where(left_lanes[top:end], parts[0], parts[1]) + skipped[top:end]
            y_ref[top:end, at] = mixed
            gated = mixed * gate[top:end]
            gated_ref[top:end, at] = gated
            square_ref[top:end, :] += gated * gated


def ssm_forward(projected, wide, conv_state, extra, live, same, mask, offsets):
    rows = projected.shape[0]
    pairs = wide.shape[1] // 128
    width = conv_state.shape[1]
    const2 = lambda i: (0, 0)
    at = lambda name, size: offsets[name] // size
    block = lambda name: pl.BlockSpec((rows, 128 * 2), lambda i, o=at(name, 128 * 2): (0, o + i))
    return pl.pallas_call(
        ssm_forward_kernel,
        grid=(pairs // 2,),
        in_specs=[
            block("u"),
            block("z"),
            pl.BlockSpec((rows, width // 2), lambda i: (0, at("state", width // 2))),
            pl.BlockSpec((rows, width // 2), lambda i: (0, at("state", width // 2) + 1)),
            pl.BlockSpec((rows, 128), lambda i: (0, at("step", 128))),
            pl.BlockSpec((8, 128 * 2), lambda i: (0, i)),
            pl.BlockSpec((8, width), const2),
            pl.BlockSpec((8, 128), const2),
            pl.BlockSpec((rows, 128), const2),
            pl.BlockSpec((3, rows, 128), lambda i: (0, 0, 0)),
            pl.BlockSpec((rows, rows), const2),
        ],
        out_specs=[
            pl.BlockSpec((rows, 128 * 2), lambda i: (0, i)),
            pl.BlockSpec((rows, 128 * 2), lambda i: (0, i)),
            pl.BlockSpec((rows, 128), const2),
        ],
        out_shape=[
            jax.ShapeDtypeStruct((rows, pairs * 128), jnp.float32),
            jax.ShapeDtypeStruct((rows, pairs * 128), jnp.float32),
            jax.ShapeDtypeStruct((rows, 128), jnp.float32),
        ],
        scratch_shapes=[
            pltpu.VMEM((rows, rows), jnp.float32),
            pltpu.VMEM((rows, 128), jnp.float32),
            pltpu.VMEM((rows, 128), jnp.float32),
            pltpu.VMEM((128, rows), jnp.float32),
        ],
        compiler_params=pltpu.CompilerParams(vmem_limit_bytes=28 * 2**20),
        name="ssm_forward",
    )(projected, projected, projected, projected, projected, wide, conv_state, extra, live, same, mask)


def ssm_backward_kernel(
    dn_ref, y_ref, u_ref, z_ref, state_b_ref, state_c_ref, step_ref, inverse_ref, own_ref, other_ref,
    wide_ref, conv_ref, extra_ref, live_ref, same_ref, mask_t_ref,
    dz_ref, du_ref, ds_ref, dr_ref, wide_grad_ref, extra_grad_ref,
    gram_t, gram_grad, sizes, decays, running, running_t, size_grad, total_grad, states, state_slopes,
):
    step = pl.program_id(0)
    live = live_ref[...]
    rows = live.shape[0]
    width = conv_ref.shape[1]
    wide_live = jnp.concatenate([live] * (width // 128), axis=1)

    @pl.when(step == 0)
    def _():
        unused, size, decay = step_sizes(step_ref[...], extra_ref, live)
        total = running_sum(decay)
        sizes[...] = size
        decays[...] = decay
        running[...] = total
        running_t[...] = total.T
        state = jnp.concatenate([state_b_ref[...], state_c_ref[...]], axis=1) * wide_live
        inner = conv_rows(state, conv_ref[...], same_ref)
        value, slope = silu_parts(inner)
        both = value.astype(jnp.bfloat16)
        states[...] = both
        state_slopes[...] = slope
        gram_t[...] = dot_nt(both[:, : width // 2], both[:, width // 2 :]) * mask_t_ref[...]
        gram_grad[...] = jnp.zeros_like(gram_grad)
        size_grad[...] = jnp.zeros_like(size_grad)
        total_grad[...] = jnp.zeros_like(total_grad)

    for part in range(2):
        pair = 2 * step + part
        at = slice(part * 128, (part + 1) * 128)
        taps = wide_ref[:, at]
        u_live = u_ref[:, at] * live
        inner = conv_rows(u_live, taps, same_ref)
        x_in, x_slope = silu_parts(inner)
        gate, gate_slope = silu_parts(z_ref[:, at])
        mixed = y_ref[:, at]
        gated = mixed * gate
        inverse = inverse_ref[:, 0:1]
        pull = (own_ref[:, 0:1] + other_ref[:, 0:1]) * inverse * inverse * inverse / DSSM
        grad_gated = taps[6:7] * dn_ref[:, at] * inverse - gated * pull
        grad_mixed = grad_gated * gate
        dz_ref[:, at] = (grad_gated * mixed * gate_slope).astype(dz_ref.dtype)
        grad_mixed_b = grad_mixed.astype(jnp.bfloat16)
        lanes = lax.broadcasted_iota(jnp.int32, (rows, 128), 1)
        left_lanes = lanes < HP
        size = sizes[...]
        size_pair = jnp.where(left_lanes, lane_column(size, 2 * pair), lane_column(size, 2 * pair + 1))
        inflow = (size_pair * x_in).astype(jnp.bfloat16)
        zero = jnp.zeros_like(inflow)
        inflow_heads = [jnp.where(left_lanes, inflow, zero), jnp.where(left_lanes, zero, inflow)]
        total = running[...]
        columns = [lane_column(total, 2 * pair + k) for k in range(2)]
        row_vectors = [running_t[pl.ds(2 * pair + k, 1), :] for k in range(2)]
        blocks = []
        for block in range(rows // TILE):
            top, end = block * TILE, (block + 1) * TILE
            parts = []
            gram_part = None
            for k in range(2):
                gaps = row_vectors[k][:, top:] - columns[k][top:end]
                decay = jnp.exp(jnp.minimum(gaps, 0.0))
                mixing_t = (gram_t[top:end, top:] * decay).astype(jnp.bfloat16)
                parts.append(dot_nn(mixing_t, grad_mixed_b[top:]))
                term = dot_nt(inflow_heads[k][top:end], grad_mixed_b[top:]) * decay
                gram_part = term if gram_part is None else gram_part + term
            gram_grad[top:end, top:] += gram_part
            blocks.append(jnp.where(left_lanes[top:end], parts[0], parts[1]))
        grad_inflow = jnp.concatenate(blocks, axis=0)
        grad_x = grad_mixed * taps[5:6] + grad_inflow * size_pair
        by_size = grad_inflow * x_in
        mixed_only = mixed - taps[5:6] * x_in
        by_total = grad_mixed_b.astype(jnp.float32) * mixed_only - grad_inflow * inflow.astype(jnp.float32)
        size_grad[...] += head_sums(by_size, pair)
        total_grad[...] += head_sums(by_total, pair)
        grad_u, tap_grads = conv_rows_back(grad_x * x_slope, u_live, taps, same_ref)
        du_ref[:, at] = (grad_u * live).astype(du_ref.dtype)
        skip_grad = jnp.sum(grad_mixed * x_in, axis=0, keepdims=True)
        wide_grad_ref[:, at] = jnp.concatenate(
            tap_grads + [skip_grad, jnp.zeros((2, 128), jnp.float32)], axis=0
        )

    @pl.when(step == pl.num_programs(0) - 1)
    def _():
        half = width // 2
        gram_grad_b = (gram_grad[...] * mask_t_ref[...]).astype(jnp.bfloat16)
        grad_b = dot_nn(gram_grad_b, states[:, half:])
        grad_c = dot_tn(gram_grad_b, states[:, :half])
        grad_bc = jnp.concatenate([grad_b, grad_c], axis=1) * state_slopes[...]
        state = jnp.concatenate([state_b_ref[...], state_c_ref[...]], axis=1) * wide_live
        grad_in, state_taps = conv_rows_back(grad_bc, state, conv_ref[...], same_ref)
        ds_ref[:rows, :] = (grad_in * wide_live).astype(ds_ref.dtype)
        ds_ref[rows:, :] = jnp.concatenate(
            state_taps + [jnp.zeros((11, width), jnp.float32)], axis=0
        ).astype(ds_ref.dtype)
        decay_grad = running_sum(total_grad[...], backward=True)
        shifted = step_ref[...] + extra_ref[0:1]
        grad_size = size_grad[...] - decay_grad * extra_ref[1:2]
        grad_raw = grad_size * live * jax.nn.sigmoid(shifted)
        dr_ref[...] = grad_raw.astype(dr_ref.dtype)
        extra_grad_ref[...] = jnp.concatenate(
            [
                jnp.sum(grad_raw, axis=0, keepdims=True),
                jnp.sum(decay_grad * decays[...], axis=0, keepdims=True),
                jnp.zeros((6, 128), jnp.float32),
            ],
            axis=0,
        )


def ssm_backward(
    grad_normed, mixed, projected, inverse, own, other, wide, conv_state, extra, live, same, mask_t, offsets
):
    rows = projected.shape[0]
    pairs = wide.shape[1] // 128
    width = conv_state.shape[1]
    const2 = lambda i: (0, 0)
    at = lambda name, size: offsets[name] // size
    block = lambda name: pl.BlockSpec((rows, 128 * 2), lambda i, o=at(name, 128 * 2): (0, o + i))
    plain = pl.BlockSpec((rows, 128 * 2), lambda i: (0, i))
    f32, b16 = jnp.float32, jnp.bfloat16
    return pl.pallas_call(
        ssm_backward_kernel,
        grid=(pairs // 2,),
        in_specs=[
            plain,
            plain,
            block("u"),
            block("z"),
            pl.BlockSpec((rows, width // 2), lambda i: (0, at("state", width // 2))),
            pl.BlockSpec((rows, width // 2), lambda i: (0, at("state", width // 2) + 1)),
            pl.BlockSpec((rows, 128), lambda i: (0, at("step", 128))),
            pl.BlockSpec((rows, 128), const2),
            pl.BlockSpec((rows, 128), const2),
            pl.BlockSpec((rows, 128), const2),
            pl.BlockSpec((8, 128 * 2), lambda i: (0, i)),
            pl.BlockSpec((8, width), const2),
            pl.BlockSpec((8, 128), const2),
            pl.BlockSpec((rows, 128), const2),
            pl.BlockSpec((3, rows, 128), lambda i: (0, 0, 0)),
            pl.BlockSpec((rows, rows), const2),
        ],
        out_specs=[
            plain,
            plain,
            pl.BlockSpec((rows + 16, width), const2),
            pl.BlockSpec((rows, 128), const2),
            pl.BlockSpec((8, 128 * 2), lambda i: (0, i)),
            pl.BlockSpec((8, 128), const2),
        ],
        out_shape=[
            jax.ShapeDtypeStruct((rows, pairs * 128), b16),
            jax.ShapeDtypeStruct((rows, pairs * 128), b16),
            jax.ShapeDtypeStruct((rows + 16, width), b16),
            jax.ShapeDtypeStruct((rows, 128), b16),
            jax.ShapeDtypeStruct((8, pairs * 128), f32),
            jax.ShapeDtypeStruct((8, 128), f32),
        ],
        scratch_shapes=[
            pltpu.VMEM((rows, rows), f32),
            pltpu.VMEM((rows, rows), f32),
            pltpu.VMEM((rows, 128), f32),
            pltpu.VMEM((rows, 128), f32),
            pltpu.VMEM((rows, 128), f32),
            pltpu.VMEM((128, rows), f32),
            pltpu.VMEM((rows, 128), f32),
            pltpu.VMEM((rows, 128), f32),
            pltpu.VMEM((rows, width), b16),
            pltpu.VMEM((rows, width), f32),
        ],
        compiler_params=pltpu.CompilerParams(vmem_limit_bytes=32 * 2**20),
        cost_estimate=cost(1, 1),
        name="ssm_backward",
    )(
        grad_normed, mixed, projected, projected, projected, projected, projected, inverse, own, other,
        wide, conv_state, extra, live, same, mask_t,
    )


def turned(values, cos_ref, sin_ref):
    return values * cos_ref[...] + pltpu.roll(values, HEAD_DIMENSION // 2, 1) * sin_ref[...]


def attention_forward_kernel(
    q_ref, k_ref, v_ref, cos_ref, sin_ref, mask_ref, out_ref, query_ref, key_ref, value_ref, log_ref
):
    head = pl.program_id(0)
    rows = q_ref.shape[0]
    scale = HEAD_DIMENSION**-0.5

    @pl.when(head == 0)
    def _():
        key_ref[...] = turned(k_ref[...], cos_ref, sin_ref).astype(jnp.bfloat16)
        value_ref[...] = v_ref[...].astype(jnp.bfloat16)

    query = turned(q_ref[...], cos_ref, sin_ref).astype(jnp.bfloat16)
    query_ref[...] = query
    for block in range(rows // TILE):
        top, end = block * TILE, (block + 1) * TILE
        scores = dot_nt(query[top:end], key_ref[:end, :]) * scale
        scores = jnp.where(mask_ref[top:end, :end] > 0.0, scores, -1e30)
        largest = jnp.max(scores, axis=1, keepdims=True)
        weights = jnp.exp(scores - largest)
        total = jnp.sum(weights, axis=1, keepdims=True)
        probs = (weights / total).astype(jnp.bfloat16)
        out_ref[top:end, :] = dot_nn(probs, value_ref[:end, :]).astype(out_ref.dtype)
        log_ref[top:end, :] = jnp.broadcast_to(largest + jnp.log(total), (TILE, 128))


def attention_forward(projected, cos, sin, mask, offsets, heads):
    rows = projected.shape[0]
    at = lambda name: offsets[name] // 128
    const2 = lambda i: (0, 0)
    one = pl.BlockSpec((rows, 128), const2)
    each = pl.BlockSpec((rows, 128), lambda i: (0, i))
    b16 = jnp.bfloat16
    return pl.pallas_call(
        attention_forward_kernel,
        grid=(heads,),
        in_specs=[
            pl.BlockSpec((rows, 128), lambda i: (0, at("q") + i)),
            pl.BlockSpec((rows, 128), lambda i: (0, at("kv"))),
            pl.BlockSpec((rows, 128), lambda i: (0, at("kv") + 1)),
            one,
            one,
            pl.BlockSpec((rows, rows), const2),
        ],
        out_specs=[each, each, one, one, each],
        out_shape=[
            jax.ShapeDtypeStruct((rows, heads * 128), b16),
            jax.ShapeDtypeStruct((rows, heads * 128), b16),
            jax.ShapeDtypeStruct((rows, 128), b16),
            jax.ShapeDtypeStruct((rows, 128), b16),
            jax.ShapeDtypeStruct((rows, heads * 128), jnp.float32),
        ],
        compiler_params=pltpu.CompilerParams(vmem_limit_bytes=24 * 2**20),
        name="attention_forward",
    )(projected, projected, projected, cos, sin, mask)


def attention_backward_kernel(
    grad_ref, query_ref, key_ref, value_ref, log_ref, cos_ref, sin_ref, mask_ref,
    dq_ref, dk_ref, dv_ref, key_sum, value_sum,
):
    head = pl.program_id(0)
    rows = query_ref.shape[0]
    scale = HEAD_DIMENSION**-0.5

    @pl.when(head == 0)
    def _():
        key_sum[...] = jnp.zeros_like(key_sum)
        value_sum[...] = jnp.zeros_like(value_sum)

    for block in range(rows // TILE):
        top, end = block * TILE, (block + 1) * TILE
        query = query_ref[top:end, :]
        grad = grad_ref[top:end, :]
        scores = dot_nt(query, key_ref[:end, :]) * scale
        scores = jnp.where(mask_ref[top:end, :end] > 0.0, scores, -1e30)
        probs = jnp.exp(scores - log_ref[top:end, 0:1])
        grad_probs = dot_nt(grad, value_ref[:end, :])
        inner = jnp.sum(grad_probs * probs, axis=1, keepdims=True)
        grad_scores = (probs * (grad_probs - inner)).astype(jnp.bfloat16)
        dq = dot_nn(grad_scores, key_ref[:end, :]) * scale
        dq_ref[top:end, :] = (
            dq * cos_ref[top:end, :]
            - pltpu.roll(dq, HEAD_DIMENSION // 2, 1) * sin_ref[top:end, :]
        ).astype(dq_ref.dtype)
        key_sum[:end, :] += dot_tn(grad_scores, query)
        value_sum[:end, :] += dot_tn(probs.astype(jnp.bfloat16), grad)

    @pl.when(head == pl.num_programs(0) - 1)
    def _():
        dk = key_sum[...] * scale
        dk_ref[...] = (
            dk * cos_ref[...] - pltpu.roll(dk, HEAD_DIMENSION // 2, 1) * sin_ref[...]
        ).astype(dk_ref.dtype)
        dv_ref[...] = value_sum[...].astype(dv_ref.dtype)


def attention_backward(grad, query, key, value, logs, cos, sin, mask):
    rows = query.shape[0]
    heads = query.shape[1] // 128
    const2 = lambda i: (0, 0)
    one = pl.BlockSpec((rows, 128), const2)
    each = pl.BlockSpec((rows, 128), lambda i: (0, i))
    b16 = jnp.bfloat16
    return pl.pallas_call(
        attention_backward_kernel,
        grid=(heads,),
        in_specs=[each, each, one, one, each, one, one, pl.BlockSpec((rows, rows), const2)],
        out_specs=[each, one, one],
        out_shape=[
            jax.ShapeDtypeStruct((rows, heads * 128), b16),
            jax.ShapeDtypeStruct((rows, 128), b16),
            jax.ShapeDtypeStruct((rows, 128), b16),
        ],
        scratch_shapes=[pltpu.VMEM((rows, 128), jnp.float32), pltpu.VMEM((rows, 128), jnp.float32)],
        compiler_params=pltpu.CompilerParams(vmem_limit_bytes=24 * 2**20),
        cost_estimate=cost(1, 1),
        name="attention_backward",
    )(grad, query, key, value, logs, cos, sin, mask)


def feed_forward_kernel(
    in_ref, grad_ref, gate_w_ref, up_w_ref, down_ref, act_ref, dgate_ref, dup_ref, din_ref, total
):
    step = pl.program_id(0)

    @pl.when(step == 0)
    def _():
        total[...] = jnp.zeros_like(total)

    gate = dot_nn(in_ref[...], gate_w_ref[...])
    up = dot_nn(in_ref[...], up_w_ref[...])
    grad_act = dot_nn(grad_ref[...], down_ref[...])
    value, slope = silu_parts(gate)
    act_ref[...] = (value * up).astype(act_ref.dtype)
    dgate = (grad_act * up * slope).astype(jnp.bfloat16)
    dup = (grad_act * value).astype(jnp.bfloat16)
    dgate_ref[...] = dgate
    dup_ref[...] = dup
    total[...] += dot_nt(dgate, gate_w_ref[...]) + dot_nt(dup, up_w_ref[...])

    @pl.when(step == pl.num_programs(0) - 1)
    def _():
        din_ref[...] = total[...].astype(din_ref.dtype)


def feed_forward(ffn_in, grad, weights, hidden, tile=512):
    rows, model = grad.shape
    steps = hidden // tile
    each = pl.BlockSpec((rows, tile), lambda i: (0, i))
    whole = pl.BlockSpec((rows, model), lambda i: (0, 0))
    b16 = jnp.bfloat16
    return pl.pallas_call(
        feed_forward_kernel,
        grid=(steps,),
        in_specs=[
            whole,
            whole,
            pl.BlockSpec((model, tile), lambda i: (0, i)),
            pl.BlockSpec((model, tile), lambda i: (0, steps + i)),
            pl.BlockSpec((model, tile), lambda i: (0, 2 * steps + i)),
        ],
        out_specs=[each, each, each, whole],
        out_shape=[
            jax.ShapeDtypeStruct((rows, hidden), b16),
            jax.ShapeDtypeStruct((rows, hidden), b16),
            jax.ShapeDtypeStruct((rows, hidden), b16),
            jax.ShapeDtypeStruct((rows, model), b16),
        ],
        scratch_shapes=[pltpu.VMEM((rows, model), jnp.float32)],
        compiler_params=pltpu.CompilerParams(vmem_limit_bytes=44 * 2**20),
        cost_estimate=cost(1, 1),
        name="feed_forward",
    )(ffn_in, grad, weights, weights, weights)


def norm_back_kernel(
    grad_ref, weight_ref, gated_ref, inverse_ref, gain_ref, dout_ref, dn_ref, row_ref, column_ref, *, split
):
    step = pl.program_id(0)

    @pl.when(step == 0)
    def _():
        row_ref[...] = jnp.zeros_like(row_ref)

    grad = dot_nn(grad_ref[...], weight_ref[...])

    @pl.when(step < split)
    def _():
        dout_ref[...] = grad.astype(dout_ref.dtype)

    @pl.when(step >= split)
    def _():
        dn_ref[...] = grad
        product = grad * gated_ref[...]
        scaled = product * gain_ref[0:1]
        part = scaled[:, :128]
        for k in range(1, scaled.shape[1] // 128):
            part = part + scaled[:, k * 128 : (k + 1) * 128]
        row_ref[...] += part
        total = jnp.sum(product * inverse_ref[:, 0:1], axis=0, keepdims=True)
        column_ref[...] = jnp.broadcast_to(total, column_ref.shape)

    @pl.when(step == pl.num_programs(0) - 1)
    def _():
        row_ref[...] = jnp.broadcast_to(
            jnp.sum(row_ref[...], axis=1, keepdims=True), row_ref.shape
        )


def norm_back(grad, weights, first, attended, gated, inverse, gains, tile=512):
    rows, model = grad.shape
    width = gated.shape[1]
    split = attended // tile
    later = lambda i: (0, jnp.maximum(i - split, 0))
    f32 = jnp.float32
    return pl.pallas_call(
        functools.partial(norm_back_kernel, split=split),
        grid=((attended + width) // tile,),
        in_specs=[
            pl.BlockSpec((rows, model), lambda i: (0, 0)),
            pl.BlockSpec((model, tile), lambda i: (0, first // tile + i)),
            pl.BlockSpec((rows, tile), later),
            pl.BlockSpec((rows, 128), lambda i: (0, 0)),
            pl.BlockSpec((8, tile), later),
        ],
        out_specs=[
            pl.BlockSpec((rows, tile), lambda i: (0, jnp.minimum(i, split - 1))),
            pl.BlockSpec((rows, tile), later),
            pl.BlockSpec((rows, 128), lambda i: (0, 0)),
            pl.BlockSpec((8, tile), later),
        ],
        out_shape=[
            jax.ShapeDtypeStruct((rows, attended), jnp.bfloat16),
            jax.ShapeDtypeStruct((rows, width), f32),
            jax.ShapeDtypeStruct((rows, 128), f32),
            jax.ShapeDtypeStruct((8, width), f32),
        ],
        compiler_params=pltpu.CompilerParams(vmem_limit_bytes=40 * 2**20),
        cost_estimate=cost(1, 1),
        name="norm_back",
    )(grad, weights, gated, inverse, gains)


def reorder_kernel(order_ref, in_ref, out_ref):
    width = in_ref.shape[1] // order_ref.shape[0]
    for place in range(order_ref.shape[0]):
        column = pl.multiple_of(order_ref[place] * width, width)
        out_ref[:, place * width : (place + 1) * width] = in_ref[:, pl.ds(column, width)]


def reorder_columns(values, order):
    rows, model = values.shape
    count = order.shape[0]
    width = model // count
    if width % 128:
        return jnp.take(values.reshape(rows, count, width), order, axis=1).reshape(rows, model)
    return pl.pallas_call(
        reorder_kernel,
        in_specs=[
            pl.BlockSpec(memory_space=pltpu.SMEM),
            pl.BlockSpec(memory_space=pltpu.VMEM),
        ],
        out_specs=pl.BlockSpec(memory_space=pltpu.VMEM),
        out_shape=jax.ShapeDtypeStruct(values.shape, values.dtype),
        compiler_params=pltpu.CompilerParams(vmem_limit_bytes=8 * 2**20),
        cost_estimate=cost(1, 1),
        name="reorder_columns",
    )(order, values)


def widest(width, most):
    return max(t for t in range(128, most + 1, 128) if width % t == 0)


def scatter_part_kernel(left_ref, right_ref, *refs):
    got_refs, out_ref, turned_left = refs[:-2], refs[-2], refs[-1]

    @pl.when(pl.program_id(0) == 0)
    def _():
        turned_left[...] = left_ref[...].T

    total = dot_nn(turned_left[...], right_ref[...])
    for got_ref in got_refs:
        total = total + got_ref[...].astype(jnp.float32)
    out_ref[...] = total.astype(out_ref.dtype)


def scatter_part(left, right, gots, first, size, dtype):
    rows, width = right.shape
    if size % 128 or first % size:
        total = contract("tm,tn->mn", left[:, first : first + size], right)
        for got, start in gots:
            total = total + got[start : start + size].astype(jnp.float32)
        return total.astype(dtype)
    tile = widest(width, 2304 if size <= 256 else 1152)
    return pl.pallas_call(
        scatter_part_kernel,
        grid=(width // tile,),
        in_specs=[
            pl.BlockSpec((rows, size), lambda i: (0, first // size)),
            pl.BlockSpec((rows, tile), lambda i: (0, i)),
        ]
        + [
            pl.BlockSpec((size, tile), lambda i, at=start // size: (at, i)) for unused, start in gots
        ],
        out_specs=pl.BlockSpec((size, tile), lambda i: (0, i)),
        out_shape=jax.ShapeDtypeStruct((size, width), dtype),
        scratch_shapes=[pltpu.VMEM((size, rows), jnp.bfloat16)],
        compiler_params=pltpu.CompilerParams(vmem_limit_bytes=24 * 2**20),
        cost_estimate=cost(1, 1),
        name="scatter_part",
    )(left, right, *[got for got, unused in gots])


def product_back_kernel(left_ref, right_ref, out_ref):
    out_ref[...] = dot_nt(left_ref[...], right_ref[...]).astype(out_ref.dtype)


def product_back(left, right, first, tile=512):
    rows, width = left.shape
    model = right.shape[0]
    return pl.pallas_call(
        product_back_kernel,
        grid=(model // tile,),
        in_specs=[
            pl.BlockSpec((rows, width), lambda i: (0, 0)),
            pl.BlockSpec((tile, width), lambda i: (i, first // width)),
        ],
        out_specs=pl.BlockSpec((rows, tile), lambda i: (0, i)),
        out_shape=jax.ShapeDtypeStruct((rows, model), jnp.bfloat16),
        compiler_params=pltpu.CompilerParams(vmem_limit_bytes=44 * 2**20),
        cost_estimate=cost(1, 1),
        name="product_back",
    )(left, right)


def join_kernel(start, ready_ref, got_ref, out_ref):
    size = ready_ref.shape[0]
    got = got_ref[start : start + size, :].astype(jnp.float32)
    out_ref[...] = (ready_ref[...].astype(jnp.float32) + got).astype(out_ref.dtype)


def join_parts(ready, got, start, dtype):
    size, width = ready.shape
    if size % 128 or start % size:
        got = got[start : start + size].astype(jnp.float32)
        return (ready.astype(jnp.float32) + got).astype(dtype)
    if size > 256:
        tile = widest(width, 1152)
        return pl.pallas_call(
            functools.partial(join_kernel, 0),
            grid=(width // tile,),
            in_specs=[
                pl.BlockSpec((size, tile), lambda i: (0, i)),
                pl.BlockSpec((size, tile), lambda i: (start // size, i)),
            ],
            out_specs=pl.BlockSpec((size, tile), lambda i: (0, i)),
            out_shape=jax.ShapeDtypeStruct((size, width), dtype),
            compiler_params=pltpu.CompilerParams(vmem_limit_bytes=24 * 2**20),
            cost_estimate=cost(1, 1),
            name="join_parts",
        )(ready, got)
    vmem = pl.BlockSpec(memory_space=pltpu.VMEM)
    return pl.pallas_call(
        functools.partial(join_kernel, start),
        in_specs=[vmem, vmem],
        out_specs=vmem,
        out_shape=jax.ShapeDtypeStruct((size, width), dtype),
        compiler_params=pltpu.CompilerParams(vmem_limit_bytes=16 * 2**20),
        cost_estimate=cost(1, 1),
        name="join_parts",
    )(ready, got)


def rms_back_kernel(value_ref, gain_ref, own_ref, other_ref, base_ref, live_ref, *out_refs):
    values = value_ref[...].astype(jnp.float32)
    gain = gain_ref[0:1]
    grad = own_ref[...].astype(jnp.float32) + other_ref[...].astype(jnp.float32)
    scale = lax.rsqrt(jnp.mean(values * values, axis=1, keepdims=True) + EPS)
    unit = values * scale
    scaled = grad * gain
    pull = jnp.mean(scaled * unit, axis=1, keepdims=True)
    total = base_ref[...].astype(jnp.float32) + (scaled - unit * pull) * scale
    out_refs[0][...] = total
    if len(out_refs) == 3:
        out_refs[2][...] = (total * live_ref[:, 0:1]).astype(jnp.bfloat16)
    gain_grad = jnp.broadcast_to(jnp.sum(grad * unit, axis=0, keepdims=True), out_refs[1].shape)

    @pl.when(pl.program_id(0) == 0)
    def _():
        out_refs[1][...] = gain_grad

    @pl.when(pl.program_id(0) > 0)
    def _():
        out_refs[1][...] += gain_grad


def rms_back(values, gain, own, other, base, live, with_rounded, tile=256):
    rows, model = values.shape
    each = pl.BlockSpec((tile, model), lambda i: (i, 0))
    whole = pl.BlockSpec((8, model), lambda i: (0, 0))
    shapes = [
        jax.ShapeDtypeStruct((rows, model), jnp.float32),
        jax.ShapeDtypeStruct((8, model), jnp.float32),
    ]
    if with_rounded:
        shapes.append(jax.ShapeDtypeStruct((rows, model), jnp.bfloat16))
    return pl.pallas_call(
        rms_back_kernel,
        grid=(rows // tile,),
        in_specs=[each, whole, each, each, each, pl.BlockSpec((tile, 128), lambda i: (i, 0))],
        out_specs=[each, whole, each][: len(shapes)],
        out_shape=shapes,
        compiler_params=pltpu.CompilerParams(vmem_limit_bytes=40 * 2**20),
        cost_estimate=cost(1, 1),
        name="rms_back",
    )(values, gain, own, other, base, live)


def beside_kernel(widths, *refs):
    out_ref, place, refs = refs[-1], 0, list(refs[:-1])
    for width, terms in widths:
        total = refs.pop(0)[...]
        if terms == 2:
            total = total.astype(jnp.float32) + refs.pop(0)[...].astype(jnp.float32)
        out_ref[:, place : place + width] = total.astype(out_ref.dtype)
        place += width
    if place < out_ref.shape[1]:
        out_ref[:, place:] = jnp.zeros((out_ref.shape[0], out_ref.shape[1] - place), out_ref.dtype)


def beside(width, *columns, tile=256):
    groups = [c if isinstance(c, tuple) else (c,) for c in columns]
    widths = tuple((g[0].shape[1], len(g)) for g in groups)
    arrays = [a for g in groups for a in g]
    rows = min(a.shape[0] for a in arrays)
    return pl.pallas_call(
        functools.partial(beside_kernel, widths),
        grid=(rows // tile,),
        in_specs=[pl.BlockSpec((tile, a.shape[1]), lambda i: (i, 0)) for a in arrays],
        out_specs=pl.BlockSpec((tile, width), lambda i: (i, 0)),
        out_shape=jax.ShapeDtypeStruct((rows, width), jnp.bfloat16),
        compiler_params=pltpu.CompilerParams(vmem_limit_bytes=16 * 2**20),
        cost_estimate=cost(1, 1),
        name="beside",
    )(*arrays)


def hidden_back_kernel(left_ref, keep_ref, weight_ref, out_ref, total):
    step = pl.program_id(0)
    last = pl.num_programs(0) - 1

    @pl.when(step == 0)
    def _():
        total[...] = jnp.zeros_like(total)

    left = jnp.where(step == last, left_ref[...] * keep_ref[0:1], left_ref[...])
    total[...] += dot_nt(left, weight_ref[...])

    @pl.when(step == last)
    def _():
        out_ref[...] = total[...].astype(out_ref.dtype)


def hidden_back(left, keep, weights):
    rows, width = left.shape
    model, tile = weights.shape[0], keep.shape[1]
    return pl.pallas_call(
        hidden_back_kernel,
        grid=(width // tile,),
        in_specs=[
            pl.BlockSpec((rows, tile), lambda i: (0, i)),
            pl.BlockSpec((8, tile), lambda i: (0, 0)),
            pl.BlockSpec((model, tile), lambda i: (0, i)),
        ],
        out_specs=pl.BlockSpec((rows, model), lambda i: (0, 0)),
        out_shape=jax.ShapeDtypeStruct((rows, model), jnp.bfloat16),
        scratch_shapes=[pltpu.VMEM((rows, model), jnp.float32)],
        compiler_params=pltpu.CompilerParams(vmem_limit_bytes=40 * 2**20),
        cost_estimate=cost(1, 1),
        name="hidden_back",
    )(left, keep, weights)


def rms_forward_kernel(base_ref, own_ref, other_ref, live_ref, gain_ref, middle_ref, out_ref):
    added = own_ref[...].astype(jnp.float32) + other_ref[...].astype(jnp.float32)
    values = base_ref[...].astype(jnp.float32) + added * live_ref[:, 0:1]
    middle_ref[...] = values
    scale = lax.rsqrt(jnp.mean(values * values, axis=1, keepdims=True) + EPS)
    out_ref[...] = (values * scale * gain_ref[0:1]).astype(out_ref.dtype)


def rms_forward(base, own, other, live, gain, tile=256):
    rows, model = base.shape
    each = pl.BlockSpec((tile, model), lambda i: (i, 0))
    return pl.pallas_call(
        rms_forward_kernel,
        grid=(rows // tile,),
        in_specs=[
            each,
            each,
            each,
            pl.BlockSpec((tile, 128), lambda i: (i, 0)),
            pl.BlockSpec((8, model), lambda i: (0, 0)),
        ],
        out_specs=[each, each],
        out_shape=[
            jax.ShapeDtypeStruct((rows, model), jnp.float32),
            jax.ShapeDtypeStruct((rows, model), jnp.bfloat16),
        ],
        compiler_params=pltpu.CompilerParams(vmem_limit_bytes=28 * 2**20),
        cost_estimate=cost(1, 1),
        name="rms_forward",
    )(base, own, other, live, gain)


def output_kernel(base_ref, own_ref, other_ref, live_ref, out_ref):
    added = own_ref[...].astype(jnp.float32) + other_ref[...].astype(jnp.float32)
    out_ref[...] = (base_ref[...] + added * live_ref[:, 0:1]).astype(out_ref.dtype)


def output_rows(base, own, other, live, tile=256):
    rows, model = base.shape
    each = pl.BlockSpec((tile, model), lambda i: (i, 0))
    return pl.pallas_call(
        output_kernel,
        grid=(rows // tile,),
        in_specs=[each, each, each, pl.BlockSpec((tile, 128), lambda i: (i, 0))],
        out_specs=each,
        out_shape=jax.ShapeDtypeStruct((rows, model), jnp.bfloat16),
        compiler_params=pltpu.CompilerParams(vmem_limit_bytes=24 * 2**20),
        cost_estimate=cost(1, 1),
        name="output_rows",
    )(base, own, other, live)


def stack_kernel(layout, *refs):
    out_ref, place, refs = refs[-1], 0, list(refs[:-1])
    out_ref[...] = jnp.zeros_like(out_ref)
    for start, count, terms in layout:
        total = refs.pop(0)[start : start + count, :].astype(jnp.float32)
        if terms == 2:
            total = total + refs.pop(0)[start : start + count, :].astype(jnp.float32)
        out_ref[place : place + count, : total.shape[1]] = total.astype(out_ref.dtype)
        place += count


def stack_rows(width, *parts):
    layout = tuple((start, count, len(arrays)) for arrays, start, count in parts)
    total = -(-sum(count for unused, count, terms in layout) // 16) * 16
    vmem = pl.BlockSpec(memory_space=pltpu.VMEM)
    arrays = [array for arrays, start, count in parts for array in arrays]
    return pl.pallas_call(
        functools.partial(stack_kernel, layout),
        in_specs=[vmem] * len(arrays),
        out_specs=vmem,
        out_shape=jax.ShapeDtypeStruct((total, width), jnp.bfloat16),
        compiler_params=pltpu.CompilerParams(vmem_limit_bytes=8 * 2**20),
        cost_estimate=cost(1, 1),
        name="stack_rows",
    )(*arrays)


def add_kernel(left_ref, right_ref, out_ref):
    total = left_ref[...].astype(jnp.float32) + right_ref[...].astype(jnp.float32)
    out_ref[...] = total.astype(out_ref.dtype)


def add_rows(left, right):
    vmem = pl.BlockSpec(memory_space=pltpu.VMEM)
    return pl.pallas_call(
        add_kernel,
        in_specs=[vmem, vmem],
        out_specs=vmem,
        out_shape=jax.ShapeDtypeStruct(left.shape, left.dtype),
        compiler_params=pltpu.CompilerParams(vmem_limit_bytes=8 * 2**20),
        cost_estimate=cost(1, 1),
        name="add_rows",
    )(left, right)


def turn_kernel(in_ref, out_ref):
    out_ref[...] = in_ref[...].T


def turned_copy(values, tile=512):
    rows, width = values.shape
    return pl.pallas_call(
        turn_kernel,
        grid=(width // tile,),
        in_specs=[pl.BlockSpec((rows, tile), lambda i: (0, i))],
        out_specs=pl.BlockSpec((tile, rows), lambda i: (i, 0)),
        out_shape=jax.ShapeDtypeStruct((width, rows), values.dtype),
        compiler_params=pltpu.CompilerParams(vmem_limit_bytes=8 * 2**20),
        cost_estimate=cost(1, 1),
        name="turned_copy",
    )(values)


def tie(*values):
    return lax.optimization_barrier(values)


def pair_swap(values):
    return lax.ppermute(values, "tensor", [(0, 1), (1, 0)])


def pair_sum(values):
    own = lax.reduce_precision(values.astype(jnp.float32), 8, 7)
    return own + pair_swap(own.astype(jnp.bfloat16)).astype(jnp.float32)


def pair_join(values):
    other = pair_swap(values)
    first = lax.axis_index("tensor") == 0
    return jnp.concatenate(
        [jnp.where(first, values, other), jnp.where(first, other, values)], axis=0
    )


def after(values, *earlier):
    return lax.optimization_barrier((values, *earlier))[0]


def bits_of(count):
    return tuple(1 << place for place in range(count.bit_length() - 1))


def owner_order(bits):
    offsets = [0]
    for bit in reversed(bits):
        offsets = [offset | bit for offset in offsets] + offsets
    return lax.axis_index("dp") ^ jnp.array(offsets, jnp.int32)


def across(values, bit):
    count = lax.axis_size("dp")
    return lax.ppermute(values, "dp", [(i, i ^ bit) for i in range(count)])


class Scatter:
    def __init__(self, left, right, bits):
        self.left, self.right, self.bits = left, right, bits
        self.rows = left.shape[1] // 2 ** len(bits)
        self.got = []
        self.total = None

    def place(self, step):
        count = 2 ** len(self.bits)
        return count - (count >> step), max(count >> (step + 1), 1)

    def meets(self, past, step):
        return (self.place(step)[0] - self.place(past + 1)[0]) * self.rows

    def begin(self, *earlier):
        first, size = self.place(0)
        left = after(self.left, *earlier)
        self.held = scatter_part(left, self.right, [], 0, size * self.rows, jnp.bfloat16)
        return self.held

    def send(self, *earlier):
        self.got.append(across(after(self.held, *earlier), self.bits[len(self.got)]))
        return self.got[-1]

    def prepare(self, *earlier):
        step = len(self.got)
        first, size = self.place(step)
        gots = [(got, self.meets(past, step)) for past, got in enumerate(self.got[:-1])]
        left = after(self.left, *earlier)
        dtype = jnp.bfloat16 if step == 1 else jnp.float32
        self.ready = scatter_part(
            left, self.right, gots, first * self.rows, size * self.rows, dtype
        )
        return self.ready

    def make(self, *earlier):
        step = len(self.got)
        first, size = self.place(step)
        gots = [(got, self.meets(past, step)) for past, got in enumerate(self.got)]
        done = step == len(self.bits)
        self.held = scatter_part(
            after(self.left, *earlier),
            self.right,
            gots,
            first * self.rows,
            size * self.rows,
            jnp.float32 if done else jnp.bfloat16,
        )
        if done:
            self.total = self.held
        return self.held

    def join(self, *earlier):
        step = len(self.got)
        done = step == len(self.bits)
        self.held = join_parts(
            after(self.ready, *earlier),
            self.got[-1],
            self.meets(step - 1, step),
            jnp.float32 if done else jnp.bfloat16,
        )
        if done:
            self.total = self.held
        return self.held

    def finish(self):
        while self.total is None:
            self.send()
            self.make()
        return self.total


def side_by_side(first, second):
    return with_layout_constraint(
        jnp.stack([first, second], axis=1), Layout(major_to_minor=(0, 1, 2))
    )


def local(
    tokens,
    cotangent,
    segment_ids,
    counts,
    mixer_gain,
    query_proj,
    key_value_matrix,
    attend_proj,
    inner_proj,
    state_proj,
    step_proj,
    conv_inner,
    conv_state,
    step_bias,
    decay_log,
    skip_gain,
    gated_gain,
    mamba_proj,
    dense_gain,
    gateup_proj,
    down_proj,
):
    row_count, model_width = tokens.shape
    shard_rows = query_proj.shape[0]
    dp_count = lax.axis_size("dp")
    bf16, f32 = jnp.bfloat16, jnp.float32
    heads_m = step_proj.shape[1]
    heads_q = query_proj.shape[1] // HEAD_DIMENSION
    q_cols = query_proj.shape[1]
    kv_cols = 2 * key_value_matrix.shape[2]
    x_cols = inner_proj.shape[2]
    state_cols = state_proj.shape[1]
    o_cols = attend_proj.shape[0]
    hidden_cols = gateup_proj.shape[2]
    tap_count = conv_state.shape[0]
    pair_width = conv_state.shape[1]

    small = jnp.concatenate(
        [
            jnp.concatenate([mixer_gain, dense_gain])[None],
            jnp.pad(conv_state, ((0, 0), (0, 2 * mixer_gain.shape[0] - pair_width))),
        ],
        axis=0,
    )
    state_rows_full = pair_join(state_proj)
    small_pair = pair_join(small[None])
    gain_half = mixer_gain.shape[0]
    small_rows = jnp.concatenate(
        [
            small_pair[:, 0, :gain_half].reshape(1, -1),
            small_pair[:, 0, gain_half:].reshape(1, -1),
            jnp.pad(
                jnp.concatenate([small_pair[0, 1:, :pair_width], small_pair[1, 1:, :pair_width]], axis=1),
                ((0, 0), (0, shard_rows - 2 * pair_width)),
            ),
        ],
        axis=0,
    )
    small_block = jnp.pad(
        small_rows, ((0, shard_rows - small_rows.shape[0]), (0, 128 - shard_rows))
    )
    step_pad = jnp.zeros((shard_rows, 128 - heads_m), bf16)
    group_mix = jnp.concatenate(
        [
            inner_proj[:, 0],
            query_proj,
            key_value_matrix.reshape(shard_rows, -1),
            inner_proj[:, 1],
            state_rows_full,
            step_proj,
            step_pad,
            small_block,
            attend_proj.T,
            mamba_proj.T,
        ],
        axis=1,
    )
    offsets, place = {}, 0
    for name, width in (
        ("z", x_cols),
        ("q", q_cols),
        ("kv", kv_cols),
        ("u", x_cols),
        ("state", state_cols),
        ("step", 128),
        ("end", 0),
    ):
        offsets[name] = place
        place += width
    out_first = offsets["end"] + 128
    group_ffn = jnp.concatenate([gateup_proj.reshape(shard_rows, -1), down_proj.T], axis=1)
    mix_full = lax.all_gather(group_mix, "dp", axis=0, tiled=True)
    ffn_full = lax.all_gather(after(group_ffn, mix_full), "dp", axis=0, tiled=True)
    out_t = mix_full[:, out_first:]
    down_t = ffn_full[:, 2 * hidden_cols :]

    small_full = mix_full[:, offsets["end"] : out_first]
    w_proj = mix_full[:, : offsets["end"]]
    small_full = small_full.reshape(dp_count, shard_rows, 128)
    gain_mix = small_full[:, 0, :shard_rows].reshape(-1).astype(f32)
    gain_dense = small_full[:, 1, :shard_rows].reshape(-1).astype(f32)
    conv_full = small_full[:, 2 : 2 + tap_count, : 2 * pair_width].astype(f32)
    conv_full = jnp.swapaxes(conv_full, 0, 1).reshape(tap_count, -1)
    conv_full = jnp.concatenate([conv_full, jnp.zeros((8 - tap_count, state_cols), f32)], axis=0)
    gain_gated = gated_gain.astype(f32)
    wide = jnp.concatenate(
        [
            conv_inner.astype(f32),
            jnp.repeat(skip_gain.astype(f32), HP)[None],
            gain_gated[None],
            jnp.zeros((1, x_cols), f32),
        ],
        axis=0,
    )
    extra = jnp.zeros((8, 128), f32)
    extra = extra.at[0, :heads_m].set(step_bias.astype(f32))
    extra = extra.at[1, :heads_m].set(jnp.exp(decay_log.astype(f32)))

    row_index = jnp.arange(row_count, dtype=jnp.int32)
    valid_rows = (row_index < counts[0]).astype(f32)[:, None]
    live = jnp.broadcast_to(valid_rows, (row_count, 128))
    position = positions_of(segment_ids)
    causal = (row_index[None, :] <= row_index[:, None]) & (
        segment_ids[None, :] == segment_ids[:, None]
    )
    mask = causal.astype(f32)
    mask_t = (
        (row_index[None, :] >= row_index[:, None]) & (segment_ids[None, :] == segment_ids[:, None])
    ).astype(f32)
    mask_qk = (causal & (row_index[None, :] < counts[0])).astype(f32)
    same = jnp.stack(
        [
            jnp.broadcast_to(((row_index >= lag) & (position >= lag)).astype(f32)[:, None], live.shape)
            for lag in range(1, tap_count - 1)
        ]
    )
    half = HEAD_DIMENSION // 2
    frequency = jnp.exp(
        jnp.arange(half, dtype=f32) * (-2.0 * math.log(THETA) / HEAD_DIMENSION)
    )
    angles = position.astype(f32)[:, None] * frequency[None, :]
    cos = jnp.cos(angles)
    sin = jnp.sin(angles)
    cos = jnp.concatenate([cos, cos], axis=1)
    sin = jnp.concatenate([-sin, sin], axis=1)
    bits = bits_of(dp_count)
    order = owner_order(bits)
    stream = tokens.astype(f32)
    upstream = cotangent.astype(f32)
    dense_grad_b = rounded(upstream * valid_rows)
    dense_split = reorder_columns(dense_grad_b, order)

    gain_dense_rows = jnp.broadcast_to(gain_dense[None], (8, model_width))
    gain_mix_rows = jnp.broadcast_to(gain_mix[None], (8, model_width))

    hidden_b = rounded(rms_scale(stream, gain_mix))
    projected = contract("td,dc->tc", hidden_b, w_proj)
    hidden_split = reorder_columns(hidden_b, order)
    mixed, gated, squares = ssm_forward(
        projected, wide, conv_full, extra, live, same, mask, offsets
    )
    own_squares = jnp.sum(squares, axis=-1)
    other_squares = pair_swap(own_squares)
    attended_b, query_b, key_b, value_b, logs = attention_forward(
        projected, cos, sin, mask_qk, offsets, heads_q
    )
    inverse = lax.rsqrt((own_squares + other_squares) / DSSM + EPS)
    normed_b = rounded(gated * inverse[:, None] * gain_gated)
    branch_in = jnp.concatenate([attended_b, normed_b], axis=1)
    branch_own = rounded(contract("tc,dc->td", branch_in, out_t))
    branch_other = pair_swap(branch_own)
    middle, ffn_in_b = rms_forward(tokens, branch_own, branch_other, live, gain_dense_rows)
    inverse_b = jnp.broadcast_to(inverse[:, None], live.shape)
    gated_rows = jnp.broadcast_to(gain_gated[None], (8, x_cols))
    first = (lax.axis_index("tensor") == 0).astype(bf16)
    last_cols = offsets["end"] + 128 - offsets["state"]
    keep = jnp.where(jnp.arange(last_cols) < state_cols, first, jnp.ones((), bf16))
    keep = jnp.broadcast_to(keep[None], (8, last_cols))
    ffn_split = reorder_columns(ffn_in_b, order)

    activated_b, grad_gate_b, grad_up_b, grad_ffn_part = feed_forward(
        ffn_in_b, after(dense_grad_b, ffn_split, dense_split), ffn_full, hidden_cols
    )
    down = Scatter(dense_split, activated_b, bits)
    gate_sum = Scatter(ffn_split, grad_gate_b, bits)
    up_sum = Scatter(ffn_split, grad_up_b, bits)
    held = down.begin()
    down.send()
    held = gate_sum.begin(held)
    ready = down.prepare(held)

    held = down.join(ready)
    down.send()
    grad_ffn_other = pair_swap(after(grad_ffn_part, ready))
    gate_sum.send(ready)
    held = up_sum.begin(held)
    ready = down.prepare(held)
    dense_own = product_back(after(activated_b, ready), ffn_full, 2 * hidden_cols)
    ready = gate_sum.prepare(dense_own)

    round_end = (ready, down.got[-1], gate_sum.got[-1], grad_ffn_other)
    held = gate_sum.join(*round_end)
    gate_sum.send()
    up_sum.send(*round_end)
    held = down.make(held)
    down.send()
    grad_middle, grad_dense_gain, mixer_grad_b = rms_back(
        middle, gain_dense_rows, after(grad_ffn_part, held), grad_ffn_other, cotangent, live, True
    )
    grad_attended_b, grad_normed, own_rows, column_part = norm_back(
        mixer_grad_b, mix_full, out_first, o_cols, gated, inverse_b, gated_rows
    )
    other_rows = pair_swap(own_rows)
    branch = Scatter(reorder_columns(mixer_grad_b, order), branch_in, bits)
    held = branch.begin(own_rows)
    ready = up_sum.prepare(held)
    grad_query_b, grad_key_b, grad_value_b = attention_backward(
        after(grad_attended_b, ready), query_b, key_b, value_b, logs, cos, sin, mask_qk
    )
    ready = grad_query_b

    round_end = (ready, gate_sum.got[-1], up_sum.got[-1], down.got[-1], other_rows)
    held = up_sum.join(*round_end)
    up_sum.send()
    branch.send(*round_end)
    held = gate_sum.make(held)
    gate_sum.send()
    held = down.make(held)
    down.send()
    dense_other = pair_swap(after(dense_own, *round_end))
    grad_z_b, grad_u_b, grad_state_part, grad_step_b, wide_grad, extra_grad = (
        ssm_backward(
            after(grad_normed, held),
            mixed,
            projected,
            inverse_b,
            own_rows,
            other_rows,
            wide,
            conv_full,
            extra,
            live,
            same,
            mask_t,
            offsets,
        )
    )
    head_b = beside(x_cols + q_cols, grad_z_b, grad_query_b)
    z_sum = Scatter(hidden_split, head_b, bits)
    inner_b = beside(kv_cols + x_cols, grad_key_b, grad_value_b, after(grad_u_b, head_b))
    u_sum = Scatter(hidden_split, inner_b, bits)
    held = z_sum.begin(grad_state_part)
    ready = branch.prepare(held)

    round_end = (ready, up_sum.got[-1], gate_sum.got[-1], branch.got[-1], down.got[-1], dense_other)
    held = branch.join(*round_end)
    branch.send()
    z_sum.send(*round_end)
    grad_state_other = pair_swap(after(grad_state_part, *round_end))
    held = up_sum.make(held)
    up_sum.send()
    held = gate_sum.make(held)
    gate_sum.send()
    held = u_sum.begin(held)
    other_b = beside(last_cols, (grad_state_part, after(grad_state_other, held)), grad_step_b)
    other_sum = Scatter(hidden_split, other_b, bits)
    columns_b = beside(offsets["end"] + 128, head_b, inner_b, other_b)
    grad_hidden_own = hidden_back(columns_b, keep, mix_full)
    held = other_sum.begin(grad_hidden_own)
    ready = z_sum.prepare(held)

    round_end = (ready, branch.got[-1], up_sum.got[-1], gate_sum.got[-1], z_sum.got[-1])
    held = z_sum.join(*round_end)
    z_sum.send()
    u_sum.send(*round_end)
    grad_hidden_other = pair_swap(after(grad_hidden_own, *round_end))
    held = branch.make(held)
    branch.send()
    held = up_sum.make(held)
    up_sum.send()
    held = gate_sum.make(held)
    held = down.make(held)
    red_down = turned_copy(after(down.finish(), held))
    output = output_rows(middle, after(dense_own, red_down), dense_other, live)
    ready = u_sum.prepare(output)
    ready = z_sum.prepare(ready)
    ready = branch.prepare(ready)
    ready = up_sum.prepare(ready)

    round_end = (ready, z_sum.got[-1], u_sum.got[-1], branch.got[-1], up_sum.got[-1], grad_hidden_other)
    held = u_sum.join(*round_end)
    u_sum.send()
    other_sum.send(*round_end)
    held = z_sum.join(held)
    z_sum.send()
    held = branch.join(held)
    branch.send()
    held = up_sum.join(held)
    red_gateup = side_by_side(after(gate_sum.finish(), held), up_sum.finish())
    grad_tokens, grad_mixer_gain = rms_back(
        tokens, gain_mix_rows, after(grad_hidden_own, red_gateup), grad_hidden_other, grad_middle, live, False
    )
    own_sums = stack_rows(
        model_width,
        ((grad_mixer_gain,), 0, 1),
        ((grad_dense_gain,), 0, 1),
        ((wide_grad,), 0, tap_count + 1),
        ((column_part,), 0, 1),
        ((grad_state_part, grad_state_other), row_count, tap_count),
        ((extra_grad,), 0, 2),
    )
    sums = add_rows(own_sums, across(own_sums, bits[0]))
    ready = other_sum.prepare(sums)
    ready = u_sum.prepare(ready)
    ready = z_sum.prepare(ready)
    ready = branch.prepare(ready)

    round_end = (ready, u_sum.got[-1], other_sum.got[-1], z_sum.got[-1], branch.got[-1])
    held = other_sum.join(*round_end)
    other_sum.send()
    held = u_sum.join(held)
    u_sum.send()
    others = across(after(sums, *round_end), bits[1])
    held = z_sum.join(held)
    z_sum.send()
    held = branch.join(held)
    red_branch = branch.finish()
    red_attend = turned_copy(after(red_branch[:, :o_cols], held))
    red_mamba = turned_copy(after(red_branch[:, o_cols:], red_attend))
    ready = other_sum.prepare(red_mamba)
    ready = u_sum.prepare(ready)
    ready = z_sum.prepare(ready)

    round_end = (ready, other_sum.got[-1], u_sum.got[-1], z_sum.got[-1], others)
    held = other_sum.join(*round_end)
    other_sum.send()
    sums = add_rows(after(sums, held), others)
    others = across(sums, bits[2])
    held = u_sum.join(sums)
    u_sum.send()
    held = z_sum.join(held)
    ready = other_sum.prepare(held)
    ready = u_sum.prepare(ready)

    held = other_sum.join(ready, other_sum.got[-1], u_sum.got[-1], others)
    other_sum.send()
    sums = add_rows(after(sums, held), others)
    others = across(sums, bits[3])
    held = u_sum.join(sums)
    ready = other_sum.prepare(held)
    held = other_sum.join(ready)
    red_head = after(z_sum.finish(), held)
    red_next = u_sum.finish()
    red_inner = side_by_side(red_head[:, :x_cols], red_next[:, kv_cols:])
    sums = add_rows(after(sums, held), others)
    for bit in bits[4:]:
        sums = add_rows(sums, across(sums, bit))
    sums = sums.astype(f32)
    at = 2 + tap_count + 2
    conv_sum = sums[at : at + tap_count, :state_cols]
    at += tap_count
    skip_sum = jnp.sum(sums[2 + tap_count, :x_cols].reshape(heads_m, HP), axis=1)
    owner = lax.axis_index("dp") * 2 + lax.axis_index("tensor")

    def own_part(values, axis_dim):
        width = values.shape[axis_dim] // (2 * dp_count)
        return lax.dynamic_slice_in_dim(values, owner * width, width, axis_dim)

    red_other = other_sum.finish()
    state_rows = shard_rows // 2
    red_state = lax.dynamic_slice_in_dim(
        red_other[:, :state_cols], lax.axis_index("tensor") * state_rows, state_rows, 0
    )
    return (
        output,
        grad_tokens,
        own_part(sums[0], 0),
        red_head[:, x_cols:],
        red_next[:, :kv_cols].reshape(shard_rows, 2, -1),
        red_attend,
        red_inner,
        red_state,
        red_other[:, state_cols : state_cols + heads_m],
        sums[2 : 2 + tap_count, :x_cols],
        own_part(conv_sum, 1),
        sums[at, :heads_m],
        sums[at + 1, :heads_m],
        skip_sum,
        sums[3 + tap_count, :x_cols],
        red_mamba,
        own_part(sums[1], 0),
        red_gateup,
        red_down,
    )


def solution(mesh):
    placed = (
        P("dp", None),
        P("dp", None),
        P("dp"),
        P("dp"),
        P(("dp", "tensor")),
        P("dp", "tensor"),
        P("dp", None, "tensor"),
        P("tensor", "dp"),
        P("dp", None, "tensor"),
        P(("dp", "tensor"), None),
        P("dp", "tensor"),
        P(None, "tensor"),
        P(None, ("dp", "tensor")),
        P("tensor"),
        P("tensor"),
        P("tensor"),
        P("tensor"),
        P("tensor", "dp"),
        P(("dp", "tensor")),
        P("dp", None, "tensor"),
        P("tensor", "dp"),
    )
    return jax.shard_map(
        local,
        mesh=mesh,
        in_specs=placed,
        out_specs=(
            P("dp", None),
            P("dp", None),
            P(("dp", "tensor")),
            P("dp", "tensor"),
            P("dp", None, "tensor"),
            P("tensor", "dp"),
            P("dp", None, "tensor"),
            P(("dp", "tensor"), None),
            P("dp", "tensor"),
            P(None, "tensor"),
            P(None, ("dp", "tensor")),
            P("tensor"),
            P("tensor"),
            P("tensor"),
            P("tensor"),
            P("tensor", "dp"),
            P(("dp", "tensor")),
            P("dp", None, "tensor"),
            P("tensor", "dp"),
        ),
        check_vma=False,
    )
```
